32 devices in a mesh: fsdp: 16 (over z, x, core), seq: 2 (over y).
Axes of the slice: x: 2, y: 2, z: 4, core: 2. Of those that a mesh axis runs over, the one named last changes fastest.
Arguments:
- inputs: bfloat16 [32, 1024, 896], P('fsdp', 'seq'), may hold values from -6 to 6
- positions: int32 [32, 1024], P('fsdp', 'seq'), may hold values from 0 to 8188, as said below
- qkv_weight: bfloat16 [896, 1152], P('fsdp'), may hold values from -0.1875 to 0.1875
- qkv_bias: bfloat16 [1152], P('fsdp'), may hold values from -3 to 3
- output_weight: bfloat16 [896, 896], P('fsdp'), may hold values from -1 to 1
- first_gain: bfloat16 [896], P('fsdp'), may hold values from 0.25 to 1.75
- gate_weight: bfloat16 [896, 4864], P('fsdp'), may hold values from -0.1875 to 0.1875
- up_weight: bfloat16 [896, 4864], P('fsdp'), may hold values from -0.1875 to 0.1875
- down_weight: bfloat16 [4864, 896], P('fsdp'), may hold values from -0.15625 to 0.15625
- second_gain: bfloat16 [896], P('fsdp'), may hold values from 0.25 to 1.75
- cotangent: bfloat16 [32, 1024, 896], P('fsdp', 'seq'), may hold values from -6 to 6
Outputs:
- result: bfloat16 [32, 1024, 896], P('fsdp', 'seq')
- input_grad: float32 [32, 1024, 896], P('fsdp', 'seq')
- qkv_grad: float32 [896, 1152], P(('fsdp', 'seq'))
- bias_grad: float32 [1152], P(('fsdp', 'seq'))
- output_grad: float32 [896, 896], P(('fsdp', 'seq'))
- first_grad: float32 [896], P(('fsdp', 'seq'))
- gate_grad: float32 [896, 4864], P(('fsdp', 'seq'))
- up_grad: float32 [896, 4864], P(('fsdp', 'seq'))
- down_grad: float32 [4864, 896], P(('fsdp', 'seq'))
- second_grad: float32 [896], P(('fsdp', 'seq'))
The draws below stay inside these ranges and needn't reach their ends.
Inputs may be any that keep to these rules, and one draw needn't show every extreme that they name: Along each sequence the positions rise strictly, by 1 to 4 from one token to the next, from a first position between 0 and 4096; some sequence begins at 0, and some sequence begins at 4096 and rises by 4 at every token.
All inputs are finite; a program needn't handle non-finite values.
Results may differ from the reference program's by a relative error of at most 0.015.
Values may be sent and summed in bfloat16 or wider, within the bound.
A program may use at most 320 MiB of HBM per device.

```python
import jax
import jax.numpy as jnp
from jax import lax

D = 896
HEADS = 14
KV_HEADS = 2
HEAD_DIM = 64
FF = 4864
SEQ_LEN = 1024
QBLOCK = 512
OFFSET_MAX = 4096
QW = 896
QKV = 1152
BATCH = 32


def draw_positions(key, part):
    key = jax.random.fold_in(key, 11)
    first, second, third, fourth = jax.random.split(key, 4)
    offsets = jax.random.randint(first, (BATCH,), 0, OFFSET_MAX + 1)
    highest = jax.random.randint(second, (), 0, BATCH)
    lowest = (highest + 1 + jax.random.randint(third, (), 0, BATCH - 1)) % BATCH
    offsets = offsets.at[highest].set(OFFSET_MAX).at[lowest].set(0)
    steps = jax.random.randint(fourth, (BATCH, SEQ_LEN), 1, 5)
    steps = steps.at[highest].set(4)
    steps = steps.at[:, 0].set(0)
    rises = jnp.cumsum(steps, axis=1)
    return (offsets[:, None] + rises).astype(jnp.int32)


def levels(key, dims, shards, smallest, high):
    level, own = 1.0, jax.random.fold_in(key, 6)
    for axis_at, blocks in shards:
        draws = jnp.exp(jax.random.uniform(jax.random.fold_in(own, axis_at), (blocks,), jnp.float32, smallest / len(shards), high / len(shards)))
        level = level * jnp.repeat(draws, dims[axis_at] // blocks).reshape([-1 if axis == axis_at else 1 for axis in range(len(dims))])
    return level


def gaussian(key, shape, scale, limit, cuts=(), kind=jnp.bfloat16):
    entries = scale * jax.random.normal(key, shape, jnp.float32)
    if cuts:
        entries = entries * levels(key, shape, cuts, -0.22, 0.18)
    return jnp.clip(entries, -limit, limit).astype(kind)


def setup_inputs(seed: int = 0) -> dict:
    key_list = jax.random.split(jax.random.key(seed), 12)
    inputs = gaussian(key_list[0], (BATCH, SEQ_LEN, D), 1.0, 6.0, ((0, 16), (1, 2)))
    positions = draw_positions(jax.random.fold_in(key_list[11], 71), 0)
    qkv_weight = gaussian(key_list[2], (D, QKV), D ** -0.5, 0.1875, ((0, 16),))
    qkv_bias = gaussian(key_list[3], (QKV,), 0.5, 3.0, ((0, 16),))
    output_weight = gaussian(key_list[4], (QW, D), (QW // 32) ** -0.5, 1.0, ((0, 16),))
    first_gain = jnp.clip(1.0 + 0.15 * jax.random.normal(key_list[5], (D,), jnp.float32), 0.25, 1.75).astype(jnp.bfloat16)
    gate_weight = gaussian(key_list[6], (D, FF), D ** -0.5, 0.1875, ((0, 16),))
    up_weight = gaussian(key_list[7], (D, FF), D ** -0.5, 0.1875, ((0, 16),))
    down_weight = gaussian(key_list[8], (FF, D), (FF // 4) ** -0.5, 0.15625, ((0, 16),))
    second_gain = jnp.clip(1.0 + 0.15 * jax.random.normal(key_list[9], (D,), jnp.float32), 0.25, 1.75).astype(jnp.bfloat16)
    cotangent = gaussian(key_list[10], (BATCH, SEQ_LEN, D), 1.0, 6.0, ((0, 16), (1, 2)))
    return dict(inputs=inputs, positions=positions, qkv_weight=qkv_weight, qkv_bias=qkv_bias, output_weight=output_weight, first_gain=first_gain, gate_weight=gate_weight, up_weight=up_weight, down_weight=down_weight, second_gain=second_gain, cotangent=cotangent)


EPS = 1e-06
THETA = 1000000.0
HIGH = lax.Precision.HIGHEST

@jax.custom_vjp
def low(v):
    return lax.optimization_barrier(v.astype(jnp.bfloat16)).astype(jnp.float32)

@jax.custom_vjp
def low_back(v):
    return v

def low_keep(v):
    return (low(v), None)

def low_pass(kept, grad):
    return (grad,)

def back_keep(v):
    return (v, None)

def back_low(kept, grad):
    return (low(grad),)
low.defvjp(low_keep, low_pass)
low_back.defvjp(back_keep, back_low)

def matmul(left, right):
    return jnp.dot(left, right, precision=HIGH, preferred_element_type=jnp.float32)

def rms_norm(values, gain):
    return values * lax.rsqrt(lax.optimization_barrier(jnp.mean(values * values, axis=-1, keepdims=True)) + EPS) * gain

def rope_tables(positions):
    freqs = THETA ** (-jnp.arange(0, HEAD_DIM, 2).astype(jnp.float32) / HEAD_DIM)
    angles = positions.astype(jnp.float32)[..., None] * freqs
    angles = jnp.concatenate([angles, angles], axis=-1)
    return (jnp.cos(angles), jnp.sin(angles))

def rotate(values, cosine, sine):
    half = HEAD_DIM // 2
    turned = jnp.concatenate([-values[..., half:], values[..., :half]], axis=-1)
    return values * cosine + turned * sine

def attention(query, keys, values, positions):
    group = HEADS // KV_HEADS
    keys_all = jnp.repeat(keys, group, axis=1)
    values_all = jnp.repeat(values, group, axis=1)
    scale = HEAD_DIM ** (-0.5)

    def block(start):
        rows = lax.dynamic_slice_in_dim(query, start, QBLOCK, 0)
        row_pos = lax.dynamic_slice_in_dim(positions, start, QBLOCK, 0)
        scores = jnp.einsum('ihd,jhd->hij', rows, keys_all, precision=HIGH) * scale
        scores = low_back(scores)
        allowed = row_pos[:, None] >= positions[None, :]
        scores = jnp.where(allowed[None], scores, -1e+30)
        probs = low(jax.nn.softmax(scores, axis=-1))
        return jnp.einsum('hij,jhd->ihd', probs, values_all, precision=HIGH)
    starts = jnp.arange(SEQ_LEN // QBLOCK, dtype=jnp.int32) * QBLOCK
    outs = lax.map(jax.checkpoint(block), starts)
    return outs.reshape(SEQ_LEN, HEADS, HEAD_DIM)

def forward(tokens, positions, qkv_weight, qkv_bias, output_weight, first_gain, gate_weight, up_weight, down_weight, second_gain):
    qwidth = HEADS * HEAD_DIM
    kvwidth = KV_HEADS * HEAD_DIM
    normed1 = low(rms_norm(tokens, first_gain))
    pre = low_back(matmul(normed1, qkv_weight) + qkv_bias)
    cosine, sine = rope_tables(positions)
    cosine = cosine[:, None, :]
    sine = sine[:, None, :]
    query = pre[:, :qwidth].reshape(SEQ_LEN, HEADS, HEAD_DIM)
    keys = pre[:, qwidth:qwidth + kvwidth].reshape(SEQ_LEN, KV_HEADS, HEAD_DIM)
    values = pre[:, qwidth + kvwidth:].reshape(SEQ_LEN, KV_HEADS, HEAD_DIM)
    query = low_back(low(rotate(query, cosine, sine)))
    keys = low_back(low(rotate(keys, cosine, sine)))
    values = low(values)
    mixed = attention(query, keys, values, positions)
    mixed = low_back(low(mixed)).reshape(SEQ_LEN, qwidth)
    hidden = tokens + low_back(matmul(mixed, output_weight))
    normed2 = low(rms_norm(hidden, second_gain))
    gate = low_back(matmul(normed2, gate_weight))
    up = low_back(matmul(normed2, up_weight))
    act = low(jax.nn.silu(gate) * up)
    return hidden + matmul(act, down_weight)

def reference(inputs, positions, qkv_weight, qkv_bias, output_weight, first_gain, gate_weight, up_weight, down_weight, second_gain, cotangent):
    weights = tuple((w.astype(jnp.float32) for w in (qkv_weight, qkv_bias, output_weight, first_gain, gate_weight, up_weight, down_weight, second_gain)))
    tokens = inputs.astype(jnp.float32)
    grads_in = cotangent.astype(jnp.float32)

    def one_sequence(carry, item):
        seq_in, seq_pos, seq_cot = item

        def apply_layer(seq_x, *params):
            return forward(seq_x, seq_pos, *params)
        output, pull = jax.vjp(apply_layer, seq_in, *weights)
        grads = pull(seq_cot)
        carry = tuple((c + g for c, g in zip(carry, grads[1:])))
        return (carry, (output.astype(jnp.bfloat16), grads[0]))
    start_sums = tuple((jnp.zeros_like(w) for w in weights))
    sums, (result, input_grad) = lax.scan(one_sequence, start_sums, (tokens, positions, grads_in))
    return (result, input_grad, sums[0], sums[1], sums[2], sums[3], sums[4], sums[5], sums[6], sums[7])
```

```python
import functools

import jax
import jax.numpy as jnp
from jax import lax
from jax.experimental import pallas as pl
from jax.experimental.pallas import tpu as pltpu
from jax.sharding import PartitionSpec as P

HEADS = 14
KV_HEADS = 2
HEAD_DIM = 64
GROUP = HEADS // KV_HEADS
PAIRS = HEADS // 2
LANES = 128
BLOCK = 256
CHUNK = 256
EPS = 1e-06
THETA = 1000000.0
BF16 = jnp.bfloat16
F32 = jnp.float32
VMEM_LIMIT = 60 * 1024 * 1024

NN = (((1,), (0,)), ((), ()))
NT = (((1,), (1,)), ((), ()))
TN = (((0,), (0,)), ((), ()))


def mm(left, right, dims=NN):
    return lax.dot_general(left, right, dims, preferred_element_type=F32)


def params():
    return pltpu.CompilerParams(vmem_limit_bytes=VMEM_LIMIT)


def swap_halves(values):
    lane = lax.broadcasted_iota(jnp.int32, values.shape, 1)
    half = HEAD_DIM // 2
    ahead = pltpu.roll(values, LANES - half, 1)
    behind = pltpu.roll(values, half, 1)
    return jnp.where(lane % HEAD_DIM < half, ahead, behind)


def qkv_kernel(x_ref, gain_ref, weight_ref, bias_ref, cos_ref, sin_ref, normed_ref, query_ref, pair_ref):
    x = x_ref[...].astype(F32)
    scale = lax.rsqrt(jnp.mean(x * x, axis=-1, keepdims=True) + EPS)
    normed = (x * scale * gain_ref[...].astype(F32)).astype(BF16)
    normed_ref[...] = normed
    pre = mm(normed, weight_ref[...]) + bias_ref[...].astype(F32)
    cosine, sine = cos_ref[...], sin_ref[...]
    qwidth = HEADS * HEAD_DIM
    for tile in range(PAIRS):
        part = pre[:, tile * LANES : (tile + 1) * LANES]
        turned = part * cosine + swap_halves(part) * sine
        query_ref[:, tile * LANES : (tile + 1) * LANES] = turned.astype(BF16)
    part = pre[:, qwidth : qwidth + LANES]
    pair_ref[:, :LANES] = (part * cosine + swap_halves(part) * sine).astype(BF16)
    pair_ref[:, LANES:] = pre[:, qwidth + LANES :].astype(BF16)


def split_heads(block):
    wide = block.astype(F32)
    lane = lax.broadcasted_iota(jnp.int32, wide.shape, 1)
    first = jnp.where(lane < HEAD_DIM, wide, 0.0)
    second = jnp.where(lane < HEAD_DIM, pltpu.roll(wide, HEAD_DIM, 1), 0.0)
    return first, second


def join_heads(first, second):
    lane = lax.broadcasted_iota(jnp.int32, first.shape, 1)
    return jnp.where(lane < HEAD_DIM, first, pltpu.roll(second, HEAD_DIM, 1))


def attend_kernel(length, query_ref, key_ref, value_ref, mixed_ref, log_ref):
    pair = pl.program_id(1)
    scale = HEAD_DIM**-0.5
    heads = [part.astype(BF16) for part in split_heads(query_ref[0])]
    lane = lax.broadcasted_iota(jnp.int32, (BLOCK, LANES), 1)
    row = lax.broadcasted_iota(jnp.int32, (BLOCK, BLOCK), 0)
    col = lax.broadcasted_iota(jnp.int32, (BLOCK, BLOCK), 1)
    for index in range(length // BLOCK):
        rows = slice(index * BLOCK, (index + 1) * BLOCK)
        seen = index * BLOCK
        outs = []
        for which in range(2):
            head = 2 * pair + which
            kv = head // GROUP
            query = heads[which][rows]
            keys = key_ref[0, kv]
            diagonal = mm(query, keys[rows], NT) * scale
            diagonal = jnp.where(row >= col, diagonal, -1e30)
            top = jnp.max(diagonal, axis=-1, keepdims=True)
            if seen:
                before = mm(query, keys[:seen], NT) * scale
                top = jnp.maximum(top, jnp.max(before, axis=-1, keepdims=True))
            probs = jnp.exp(diagonal - top).astype(BF16)
            mixed = mm(probs, value_ref[0, kv, rows, :])
            if seen:
                probs = jnp.exp(before - top).astype(BF16)
                mixed = mixed + mm(probs, value_ref[0, kv, :seen, :])
            total = mixed[:, HEAD_DIM : HEAD_DIM + 1]
            outs.append(mixed / total)
            kept = jnp.where(lane == head, top + jnp.log(total), log_ref[0, rows, :])
            log_ref[0, rows, :] = kept
        mixed_ref[0, rows, :] = join_heads(outs[0], outs[1]).astype(BF16)


def widen(values, column):
    lane = lax.broadcasted_iota(jnp.int32, values.shape, 1)
    high = column.astype(BF16).astype(F32)
    middle = (column - high).astype(BF16).astype(F32)
    low = column - high - middle
    values = jnp.where(lane == HEAD_DIM, high, values)
    values = jnp.where(lane == HEAD_DIM + 1, middle, values)
    return jnp.where(lane == HEAD_DIM + 2, low, values).astype(BF16)


def back_kernel(length, query_ref, grad_ref, mixed_ref, log_ref, key_ref, value_ref, d_query_ref, d_key_ref, d_value_ref):
    pair = pl.program_id(1)
    scale = HEAD_DIM**-0.5

    @pl.when(pair == 0)
    def start():
        d_key_ref[...] = jnp.zeros_like(d_key_ref)
        d_value_ref[...] = jnp.zeros_like(d_value_ref)

    queries = split_heads(query_ref[0])
    grads = split_heads(grad_ref[0])
    mixes = split_heads(mixed_ref[0])
    lane = lax.broadcasted_iota(jnp.int32, (length, LANES), 1)
    row = lax.broadcasted_iota(jnp.int32, (BLOCK, BLOCK), 0)
    col = lax.broadcasted_iota(jnp.int32, (BLOCK, BLOCK), 1)
    outs = []
    for which in range(2):
        head = 2 * pair + which
        kv = head // GROUP
        log_total = jnp.sum(jnp.where(lane == head, log_ref[0], 0.0), axis=-1, keepdims=True)
        inner = jnp.sum(grads[which] * mixes[which], axis=-1, keepdims=True)
        query = widen(queries[which] * scale, -log_total)
        query_low = queries[which].astype(BF16)
        grad = widen(grads[which], -inner)
        grad_low = grads[which].astype(BF16)
        parts = [None] * (length // BLOCK)
        for index in range(length // BLOCK):
            own = slice(index * BLOCK, (index + 1) * BLOCK)
            keys, values = key_ref[0, kv, own, :], value_ref[0, kv, own, :]
            key_sum = value_sum = None
            for other in range(index, length // BLOCK):
                rows = slice(other * BLOCK, (other + 1) * BLOCK)
                scores = mm(keys, query[rows], NT)
                if other == index:
                    scores = jnp.where(row <= col, scores, -1e30)
                probs = jnp.exp(scores)
                d_scores = (probs * mm(values, grad[rows], NT)).astype(BF16)
                value_part = mm(probs.astype(BF16), grad_low[rows])
                key_part = mm(d_scores, query_low[rows])
                key_sum = key_part if key_sum is None else key_sum + key_part
                value_sum = value_part if value_sum is None else value_sum + value_part
                part = mm(d_scores, keys, TN)
                parts[other] = part if parts[other] is None else parts[other] + part
            d_key_ref[0, kv, own, :] += key_sum * scale
            d_value_ref[0, kv, own, :] += value_sum
        outs.append(parts)
    for index in range(length // BLOCK):
        rows = slice(index * BLOCK, (index + 1) * BLOCK)
        joined = join_heads(outs[0][index], outs[1][index]) * scale
        d_query_ref[0, rows, :] = joined.astype(BF16)


def plain_feed_kernel(
    normed_ref, turned_ref, cot_ref, gate_ref, up_ref, down_ref,
    result_ref, d_normed_ref, gate_grad_ref, up_grad_ref, down_grad_ref,
):
    @pl.when(pl.program_id(0) == 0)
    def start():
        result_ref[...] = jnp.zeros_like(result_ref)
        d_normed_ref[...] = jnp.zeros_like(d_normed_ref)

    normed, cot = normed_ref[...], cot_ref[...]
    gate_weight, up_weight, down_weight = gate_ref[...], up_ref[...], down_ref[...]
    gate = mm(normed, gate_weight)
    up = mm(normed, up_weight)
    d_act = mm(cot, down_weight, NT)
    sigma = jax.nn.sigmoid(gate)
    silu = gate * sigma
    act = (silu * up).astype(BF16)
    d_gate = (d_act * up * sigma * (1.0 + gate * (1.0 - sigma))).astype(BF16)
    d_up = (d_act * silu).astype(BF16)
    result_ref[...] += mm(act, down_weight)
    d_normed_ref[...] += mm(d_gate, gate_weight, NT) + mm(d_up, up_weight, NT)
    turned = turned_ref[...]
    gate_grad_ref[...] = mm(turned, d_gate).astype(gate_grad_ref.dtype)
    up_grad_ref[...] = mm(turned, d_up).astype(up_grad_ref.dtype)
    down_grad_ref[...] = mm(act, cot, TN).astype(down_grad_ref.dtype)


MESH = pl.DeviceIdType.MESH
ANY = pl.BlockSpec(memory_space=pl.ANY)


class Ring:
    def __init__(self, chips):
        self.n = chips
        self.core = lax.rem(lax.axis_index("fsdp"), 2)
        self.chip = lax.div(lax.axis_index("fsdp"), 2)
        self.mine = lax.axis_index("seq")
        side, line = lax.rem(self.chip, 2), lax.div(self.chip, 2)
        self.rank = line * (1 - side) + (chips - 1 - line) * side
        self.right = {"fsdp": 2 * self.chip_at(1) + self.core}
        self.left = {"fsdp": 2 * self.chip_at(-1) + self.core}
        self.partner = {"fsdp": 2 * self.chip + 1 - self.core}
        self.peer = {"seq": 1 - self.mine}

    def chip_at(self, offset):
        rank = lax.rem(self.rank + 2 * self.n + offset, self.n)
        side = lax.div(rank, self.n // 2)
        line = rank * (1 - side) + (self.n - 1 - rank) * side
        return 2 * line + side

    def greet(self, others):
        barrier = pltpu.get_barrier_semaphore()
        for other in others:
            pl.semaphore_signal(barrier, inc=1, device_id=other, device_id_type=MESH)
        pl.semaphore_wait(barrier, len(others))


def remote(src, dst, send, recv, device):
    return pltpu.make_async_remote_copy(
        src_ref=src, dst_ref=dst, send_sem=send, recv_sem=recv, device_id=device, device_id_type=MESH
    )


class Gather:
    def __init__(self, ring, pieces, sems):
        self.ring, self.pieces, self.sems = ring, pieces, sems

    def refs(self, piece, hop):
        direction, own, block = self.pieces[piece][:3]
        dst = block(self.ring.chip_at(-direction * hop))
        return (own if hop == 0 else dst), dst

    def along(self, piece, hop):
        src, dst = self.refs(piece, hop)
        target = self.ring.right if self.pieces[piece][0] > 0 else self.ring.left
        return remote(src, dst, self.sems[0].at[piece, hop], self.sems[1].at[piece, hop], target)

    def mirror(self, piece, hop):
        src, dst = self.refs(piece, hop)
        return remote(src, dst, self.sems[2].at[piece, hop], self.sems[3].at[piece, hop], self.pieces[piece][3])

    def mirrored(self, piece, hop):
        return self.pieces[piece][3] is not None and self.pieces[piece][4] <= hop <= self.pieces[piece][5]

    def advance(self, hop, pieces):
        for piece in pieces:
            reach = self.pieces[piece][5]
            if 0 < hop <= reach:
                self.along(piece, hop - 1).wait_recv()
            if hop < reach:
                self.along(piece, hop).start()
            if self.mirrored(piece, hop):
                self.mirror(piece, hop).start()

    def finish(self):
        for piece in range(len(self.pieces)):
            for hop in range(self.ring.n):
                if hop < self.pieces[piece][5]:
                    self.along(piece, hop).wait_send()
                if self.mirrored(piece, hop):
                    self.mirror(piece, hop).wait()


def gather_sems(pieces):
    return [pltpu.SemaphoreType.DMA((pieces, CHIPS)) for _ in range(4)]


class Reduce:
    def __init__(self, ring, pieces, buffers, sems):
        self.ring, self.pieces, self.buffers, self.sems = ring, pieces, buffers, sems

    def chip(self, piece, hop):
        return self.ring.chip_at(self.pieces[piece][0] * (self.pieces[piece][5] - hop))

    def give(self, piece, hop):
        src = self.pieces[piece][2](self.chip(piece, hop))
        dst = self.buffers[piece][2].at[hop]
        return remote(src, dst, self.sems[2].at[piece, hop], self.sems[3].at[piece, hop], self.pieces[piece][3])

    def along(self, piece, hop):
        send, recv = self.buffers[piece][:2]
        src = self.pieces[piece][1](self.chip(piece, 0)) if hop == 0 and self.alone(piece) else send.at[hop % 2]
        target = self.ring.right if self.pieces[piece][0] > 0 else self.ring.left
        return remote(src, recv.at[hop], self.sems[0].at[piece, hop], self.sems[1].at[piece, hop], target)

    def alone(self, piece):
        return self.pieces[piece][2] is None

    def begin(self):
        self.offer(0, range(len(self.pieces)))

    def given(self, piece, hop):
        reach, kept = self.pieces[piece][5:]
        return not self.alone(piece) and (hop < reach or hop == reach and kept)

    def offer(self, hop, pieces):
        for piece in pieces:
            if self.given(piece, hop):
                self.give(piece, hop).start()

    def advance(self, hop, pieces):
        for piece in pieces:
            reach, kept = self.pieces[piece][5:]
            send, recv, land = self.buffers[piece]
            if not kept and hop == reach + 1:
                self.along(piece, reach - 1).wait_recv()
                self.pieces[piece][4][...] += recv[reach - 1].astype(F32)
            if hop > reach or hop == reach and not kept:
                continue
            self.offer(hop + 1, [piece])
            if hop == 0 and self.alone(piece):
                self.along(piece, 0).start()
                continue
            if 2 <= hop < reach:
                self.along(piece, hop - 2).wait_send()
            addends = [self.pieces[piece][1](self.chip(piece, hop))[...].astype(F32)]
            if self.given(piece, hop):
                self.give(piece, hop).wait_recv()
                addends.append(land[hop].astype(F32))
            if hop > 0:
                self.along(piece, hop - 1).wait_recv()
                addends.append(recv[hop - 1].astype(F32))
            total = functools.reduce(lax.add, addends)
            if hop < reach:
                send[hop % 2] = total.astype(send.dtype)
                self.along(piece, hop).start()
            else:
                self.pieces[piece][4][...] = total

    def finish(self):
        for piece in range(len(self.pieces)):
            reach = self.pieces[piece][5]
            for hop in (reach - 2, reach - 1):
                self.along(piece, hop).wait_send()
            for hop in range(self.ring.n):
                if self.given(piece, hop):
                    self.give(piece, hop).wait_send()


def reduce_scratch(shapes):
    buffers = []
    for rows, columns, shared in shapes:
        buffers += [pltpu.VMEM((2, rows, columns), BF16), pltpu.VMEM((CHIPS - 1, rows, columns), BF16)]
        if shared:
            buffers.append(pltpu.VMEM((CHIPS, rows, columns), BF16))
    return buffers + [pltpu.SemaphoreType.DMA((len(shapes), CHIPS)) for _ in range(4)]


def make_reduce(ring, pieces, scratch):
    scratch = list(scratch)
    buffers = []
    for piece in pieces:
        send, recv = scratch.pop(0), scratch.pop(0)
        buffers.append((send, recv, None if piece[2] is None else scratch.pop(0)))
    return Reduce(ring, pieces, buffers, scratch)


class Share:
    def __init__(self, ring, part, out, scratch):
        self.ring, self.part, self.out = ring, part, out
        self.peer_send, self.peer_recv, self.core_send, self.core_recv, self.sems = scratch
        self.split = len(out.shape) == 4
        self.rows = out.shape[-2]

    def over_seq(self):
        return remote(self.peer_send, self.peer_recv, self.sems.at[0], self.sems.at[1], self.ring.peer)

    def over_core(self):
        return remote(self.core_send, self.core_recv, self.sems.at[2], self.sems.at[3], self.ring.partner)

    def owned(self, core, seq):
        start = (2 * core + seq) * self.rows
        return self.part[start : start + self.rows, :]

    def first(self):
        for mine in range(2):

            @pl.when(self.ring.mine == mine)
            def pick(mine=mine):
                for core in range(2):
                    self.peer_send[core] = self.owned(core, 1 - mine).astype(BF16)

        self.over_seq().start()

    def second(self):
        self.over_seq().wait()
        for mine in range(2):
            for core in range(2):

                @pl.when((self.ring.mine == mine) & (self.ring.core == core))
                def pick(mine=mine, core=core):
                    if self.split:
                        self.out[mine, core] = self.owned(core, mine)
                        self.out[1 - mine, core] = self.peer_recv[core].astype(F32)
                        self.core_send[mine] = self.owned(1 - core, mine).astype(BF16)
                        self.core_send[1 - mine] = self.peer_recv[1 - core]
                    else:
                        self.out[core] = self.owned(core, mine) + self.peer_recv[core].astype(F32)
                        give = self.owned(1 - core, mine) + self.peer_recv[1 - core].astype(F32)
                        self.core_send[0] = give.astype(BF16)

        self.over_core().start()

    def third(self):
        self.over_core().wait()
        if self.split:
            for seq in range(2):
                self.out[seq, 1 - self.ring.core] = self.core_recv[seq].astype(F32)
        else:
            self.out[1 - self.ring.core] = self.core_recv[0].astype(F32)


def share_scratch(rows, columns, split):
    both, last = (2, rows, columns), (2 if split else 1, rows, columns)
    return [
        pltpu.VMEM(both, BF16), pltpu.VMEM(both, BF16), pltpu.VMEM(last, BF16), pltpu.VMEM(last, BF16),
        pltpu.SemaphoreType.DMA((4,)),
    ]


class ShareRows:
    def __init__(self, ring, part, out, scratch):
        self.ring, self.part, self.out = ring, part, out
        self.send, self.recv, self.sems = scratch
        self.rows = out.shape[0]

    def over_seq(self):
        return remote(self.send, self.recv, self.sems.at[0], self.sems.at[1], self.ring.peer)

    def first(self):
        for mine in range(2):

            @pl.when(self.ring.mine == mine)
            def pick(mine=mine):
                start = (1 - mine) * self.rows
                self.send[...] = self.part[start : start + self.rows, :].astype(BF16)

        self.over_seq().start()

    def second(self):
        self.over_seq().wait()
        for mine in range(2):

            @pl.when(self.ring.mine == mine)
            def pick(mine=mine):
                start = mine * self.rows
                self.out[...] = self.part[start : start + self.rows, :] + self.recv[...].astype(F32)


def share_rows_scratch(rows, columns):
    one = (rows, columns)
    return [pltpu.VMEM(one, BF16), pltpu.VMEM(one, BF16), pltpu.SemaphoreType.DMA((2,))]


def spread(points, halves, now):
    plan = [[] for _ in range(points + 1)]
    steps = [(hop, half) for hop in range(CHIPS) for half in halves]
    plan[0] = steps[:now]
    rest = steps[now:]
    for index, step in enumerate(rest):
        plan[-(-(index + 1) * points // len(rest))].append(step)
    return plan


def at_point(step, first, plan, points, which, transfer):
    for place, moves in enumerate(plan[:-1]):
        if moves and place % points == which:

            @pl.when(step == first + place // points)
            def move(moves=moves):
                for hop, pieces in moves:
                    transfer.advance(hop, pieces)


def at_end(plan, transfer):
    for hop, pieces in plan[-1]:
        transfer.advance(hop, pieces)
    transfer.finish()


def rope_tables(positions):
    half = HEAD_DIM // 2
    freqs = THETA ** (-jnp.arange(0, HEAD_DIM, 2).astype(F32) / HEAD_DIM)
    angles = positions.astype(F32)[..., None] * freqs
    cosine, sine = jnp.cos(angles), jnp.sin(angles)
    return jnp.tile(cosine, (1, LANES // half)), jnp.tile(
        jnp.concatenate([-sine, sine], axis=-1), (1, LANES // HEAD_DIM)
    )


def rms_back(values, scale, gain, upstream):
    weighted = upstream * gain
    inner = jnp.mean(weighted * values, axis=-1, keepdims=True)
    grad_in = scale * weighted - values * (scale * scale * scale) * inner
    grad_gain = jnp.sum(upstream * values * scale, axis=0)
    return (grad_in, grad_gain)


def rotate_back(grads, cosine, sine):
    tokens, width = grads.shape
    tiles = grads.reshape(tokens, width // LANES, LANES)
    half = HEAD_DIM // 2
    lane = lax.iota(jnp.int32, LANES)
    ahead = jnp.concatenate([tiles[..., half:], tiles[..., :half]], axis=-1)
    behind = jnp.concatenate([tiles[..., -half:], tiles[..., :-half]], axis=-1)
    other = jnp.where(lane % HEAD_DIM < half, ahead, behind)
    return (tiles * cosine[:, None, :] - other * sine[:, None, :]).reshape(tokens, width)


def full(shape):
    return pl.BlockSpec(shape, lambda *_: (0,) * len(shape))


def plain_shards(
    inputs, positions, qkv_weight, qkv_bias, output_weight, first_gain,
    gate_weight, up_weight, down_weight, second_gain, cotangent,
):
    seqs, half_len, width = inputs.shape
    nseq = lax.axis_size("seq")
    length = half_len * nseq
    whole = seqs // nseq
    tokens = whole * length
    qwidth = HEADS * HEAD_DIM
    kvwidth = KV_HEADS * HEAD_DIM

    def gather(part):
        return lax.all_gather(part, "fsdp", axis=0, tiled=True)

    def to_sequences(part):
        return lax.all_to_all(part, "seq", split_axis=0, concat_axis=1, tiled=True)

    def to_tokens(part):
        return lax.all_to_all(part, "seq", split_axis=1, concat_axis=0, tiled=True)

    def scatter(grad):
        part = lax.psum_scatter(grad.astype(BF16), "fsdp", scatter_dimension=0, tiled=True)
        return lax.psum_scatter(part.astype(F32), "seq", scatter_dimension=0, tiled=True)

    x_low = to_sequences(inputs).reshape(tokens, width)
    places = to_sequences(positions).reshape(tokens)
    cot = to_sequences(cotangent).reshape(tokens, width)
    full_qkv, full_bias, full_output = gather(qkv_weight), gather(qkv_bias), gather(output_weight)
    gain1, gain2 = gather(first_gain), gather(second_gain)
    full_gate, full_up, full_down = gather(gate_weight), gather(up_weight), gather(down_weight)

    cosine, sine = rope_tables(places)
    normed1, query, pair = pl.pallas_call(
        qkv_kernel,
        grid=(tokens // BLOCK,),
        in_specs=[
            pl.BlockSpec((BLOCK, width), lambda i: (i, 0)),
            full((1, width)),
            full((width, qwidth + 2 * kvwidth)),
            full((1, qwidth + 2 * kvwidth)),
            pl.BlockSpec((BLOCK, LANES), lambda i: (i, 0)),
            pl.BlockSpec((BLOCK, LANES), lambda i: (i, 0)),
        ],
        out_specs=[
            pl.BlockSpec((BLOCK, width), lambda i: (i, 0)),
            pl.BlockSpec((BLOCK, qwidth), lambda i: (i, 0)),
            pl.BlockSpec((BLOCK, 2 * kvwidth), lambda i: (i, 0)),
        ],
        out_shape=[
            jax.ShapeDtypeStruct((tokens, width), BF16),
            jax.ShapeDtypeStruct((tokens, qwidth), BF16),
            jax.ShapeDtypeStruct((tokens, 2 * kvwidth), BF16),
        ],
        compiler_params=params(),
    )(x_low, gain1[None], full_qkv, full_bias[None], cosine, sine)

    query = query.reshape(whole, length, qwidth)
    pair = pair.reshape(whole, length, 2, KV_HEADS, HEAD_DIM).transpose(2, 0, 3, 1, 4)
    ones = jnp.ones((2, whole, KV_HEADS, length, 3), BF16)
    pair = jnp.pad(jnp.concatenate([pair, ones], axis=-1), ((0, 0),) * 4 + ((0, HEAD_DIM - 3),))
    keys, values = pair[0], pair[1]
    lanes_spec = pl.BlockSpec((1, length, LANES), lambda b, p: (b, 0, p))
    kv_spec = pl.BlockSpec((1, KV_HEADS, length, LANES), lambda b, p: (b, 0, 0, 0))
    log_spec = pl.BlockSpec((1, length, LANES), lambda b, p: (b, 0, 0))
    mixed, logs = pl.pallas_call(
        functools.partial(attend_kernel, length),
        grid=(whole, PAIRS),
        in_specs=[lanes_spec, kv_spec, kv_spec],
        out_specs=[lanes_spec, log_spec],
        out_shape=[
            jax.ShapeDtypeStruct((whole, length, qwidth), BF16),
            jax.ShapeDtypeStruct((whole, length, LANES), F32),
        ],
        compiler_params=params(),
    )(query, keys, values)

    mixed_tokens = mixed.reshape(tokens, qwidth)
    x = x_low.astype(F32)
    hidden = x + mm(mixed_tokens, full_output)
    gain2 = gain2.astype(F32)
    scale2 = lax.rsqrt(jnp.mean(hidden * hidden, axis=-1, keepdims=True) + EPS)
    normed2 = (hidden * scale2 * gain2).astype(BF16)

    ff = gate_weight.shape[1]
    column = pl.BlockSpec((width, CHUNK), lambda j: (0, j))
    line = pl.BlockSpec((CHUNK, width), lambda j: (j, 0))
    total, d_normed2, gate_grad, up_grad, down_grad = pl.pallas_call(
        plain_feed_kernel,
        grid=(ff // CHUNK,),
        in_specs=[full((tokens, width)), full((width, tokens)), full((tokens, width)), column, column, line],
        out_specs=[full((tokens, width)), full((tokens, width)), column, column, line],
        out_shape=[
            jax.ShapeDtypeStruct((tokens, width), F32),
            jax.ShapeDtypeStruct((tokens, width), F32),
            jax.ShapeDtypeStruct((width, ff), BF16),
            jax.ShapeDtypeStruct((width, ff), BF16),
            jax.ShapeDtypeStruct((ff, width), BF16),
        ],
        compiler_params=params(),
    )(normed2, normed2.T, cot, full_gate, full_up, full_down)

    result = to_tokens((hidden + total).astype(BF16).reshape(whole, length, width))
    back2, second_grad = rms_back(hidden, scale2, gain2, d_normed2)
    d_hidden = cot.astype(F32) + back2
    d_branch = d_hidden.astype(BF16)
    output_grad = mm(mixed_tokens, d_branch, TN)
    d_mixed = mm(d_branch, full_output, NT).astype(BF16).reshape(whole, length, qwidth)

    d_query, d_keys, d_values = pl.pallas_call(
        functools.partial(back_kernel, length),
        grid=(whole, PAIRS),
        in_specs=[lanes_spec, lanes_spec, lanes_spec, log_spec, kv_spec, kv_spec],
        out_specs=[lanes_spec, kv_spec, kv_spec],
        out_shape=[
            jax.ShapeDtypeStruct((whole, length, qwidth), BF16),
            jax.ShapeDtypeStruct((whole, KV_HEADS, length, LANES), F32),
            jax.ShapeDtypeStruct((whole, KV_HEADS, length, LANES), F32),
        ],
        compiler_params=params(),
    )(query, d_mixed, mixed, logs, keys, values)

    def merge(part):
        part = part[..., :HEAD_DIM].astype(BF16)
        return part.transpose(0, 2, 1, 3).reshape(tokens, kvwidth)

    turned = jnp.concatenate([d_query.reshape(tokens, qwidth), merge(d_keys)], axis=-1).astype(F32)
    turned = rotate_back(turned, cosine, sine).astype(BF16)
    d_pre = jnp.concatenate([turned, merge(d_values)], axis=-1)
    qkv_grad = mm(normed1, d_pre, TN)
    bias_grad = jnp.sum(d_pre.astype(F32), axis=0)
    d_normed1 = mm(d_pre, full_qkv, NT)
    scale1 = lax.rsqrt(jnp.mean(x * x, axis=-1, keepdims=True) + EPS)
    back1, first_grad = rms_back(x, scale1, gain1.astype(F32), d_normed1)
    input_grad = (d_hidden + back1).astype(BF16).reshape(whole, length, width)
    input_grad = to_tokens(input_grad).astype(F32)

    def scatter_small(grad):
        return lax.psum_scatter(grad, ("fsdp", "seq"), scatter_dimension=0, tiled=True)

    return (
        result,
        input_grad,
        scatter(qkv_grad),
        scatter_small(bias_grad),
        scatter(output_grad),
        scatter_small(first_grad),
        scatter(gate_grad),
        scatter(up_grad),
        scatter(down_grad),
        scatter_small(second_grad),
    )


CHIPS = 8
OWNERS = 4
SPLITS = (64, 88)
STARTS = (0, 64)
BITS = 16
QUARTER = 512
BOTH = 1024


def inside(shape):
    return pl.BlockSpec(shape, lambda *_: (0,) * len(shape), pipeline_mode=pl.Buffered(1))


def dma(*shape):
    return pltpu.SemaphoreType.DMA(shape)


def spans():
    return [2 * CHIPS * split for split in SPLITS]


def stack_rows(first, second):
    return jnp.concatenate([first.astype(F32), second.astype(F32)], axis=0)


def one_hot(rows, segments):
    row = lax.broadcasted_iota(jnp.int32, (rows, LANES), 0)
    col = lax.broadcasted_iota(jnp.int32, (rows, LANES), 1)
    found = None
    for a, b, shift in segments:
        here = (row - col == shift) & (col >= a) & (col < b)
        found = here if found is None else found | here
    return jnp.where(found, 1.0, 0.0).astype(BF16)


def owner_columns(core, group, section):
    own = sum(SPLITS)
    return (section // 2) * OWNERS * own + 2 * own * core + (section % 2) * own + STARTS[group]


def gather_columns(source, core, group, store):
    split = SPLITS[group]
    for tile in range(2 * CHIPS * split // LANES):
        segments, low, high = [], None, None
        for section in range(tile * LANES // split, ((tile + 1) * LANES - 1) // split + 1):
            a = max(section * split - tile * LANES, 0)
            b = min((section + 1) * split - tile * LANES, LANES)
            shift = owner_columns(core, group, section) + tile * LANES - section * split
            segments.append((a, b, shift))
            low = a + shift if low is None else low
            high = b + shift
        start = low // LANES * LANES
        count = -(-(high - start) // LANES) * LANES
        pick = one_hot(count, [(a, b, shift - start) for a, b, shift in segments])
        store(tile, mm(source[:, start : start + count], pick))


def spread_columns(sources, store, width):
    own = sum(SPLITS)
    for tile in range(width // LANES):
        total = None
        column = tile * LANES
        while column < (tile + 1) * LANES:
            chip, rest = divmod(column, OWNERS * own)
            core, rest = divmod(rest, 2 * own)
            seq, rest = divmod(rest, own)
            group = 0 if rest < SPLITS[0] else 1
            left = SPLITS[0] - rest if group == 0 else own - rest
            stop = min(column + left, (tile + 1) * LANES)
            index = (2 * chip + seq) * SPLITS[group] + rest - STARTS[group]
            start = index // LANES * LANES
            a, b = column - tile * LANES, stop - tile * LANES
            high = index + b - a
            count = -(-(high - start) // LANES) * LANES
            pick = one_hot(count, [(a, b, index - a - start)])
            part = mm(sources[group][core][:, start : start + count], pick)
            total = part if total is None else total + part
            column = stop
        store(tile, total)


def project(length, x_ref, table_ref, vectors_ref, weight_ref, turned_ref, query_ref, key_ref, value_ref):
    width = x_ref.shape[2]
    qwidth = HEADS * HEAD_DIM
    lane = lax.broadcasted_iota(jnp.int32, (BLOCK, LANES), 1)
    extra = (lane >= HEAD_DIM) & (lane < HEAD_DIM + 3)
    bias, gain = vectors_ref[0:1, :], vectors_ref[1:2, :width]
    early = weight_ref[0].reshape(width, BOTH)
    late = weight_ref[1, :, :, : qwidth + 2 * LANES - BOTH].reshape(width, qwidth + 2 * LANES - BOTH)
    for index in range(length // BLOCK):
        rows = slice(index * BLOCK, (index + 1) * BLOCK)
        half, start = index * BLOCK // (length // 2), index * BLOCK % (length // 2)
        x = x_ref[half, start : start + BLOCK, :].astype(F32)
        scale = lax.rsqrt(jnp.mean(x * x, axis=-1, keepdims=True) + EPS)
        normed = (x * scale * gain).astype(BF16)
        turned_ref[:, rows] = normed.T
        pre = mm(normed, early) + bias[:, :BOTH]
        values = mm(normed, late) + bias[:, BOTH:]
        cosine, sine = tables(table_ref[half, start : start + BLOCK, :])
        for tile in range(PAIRS):
            columns = slice(tile * LANES, (tile + 1) * LANES)
            part = pre[:, columns]
            query_ref[rows, columns] = (part * cosine + swap_halves(part) * sine).astype(BF16)
        part = pre[:, qwidth : qwidth + LANES]
        part = part * cosine + swap_halves(part) * sine
        for ref, both in ((key_ref, part), (value_ref, values)):
            for kv, head in enumerate(split_heads(both)):
                ref[kv, rows, :] = jnp.where(extra, 1.0, head).astype(BF16)


def tables(packed):
    lane = lax.broadcasted_iota(jnp.int32, packed.shape, 1)
    turned = pltpu.roll(packed, HEAD_DIM, 1)
    low = lane < HEAD_DIM
    return jnp.where(low, packed, turned), jnp.where(low, turned, packed)


def attend_pair(pair, length, query_ref, key_ref, value_ref, mixed_ref, log_ref):
    scale = HEAD_DIM**-0.5
    columns = pl.ds(pl.multiple_of(pair * LANES, LANES), LANES)
    heads = [part.astype(BF16) for part in split_heads(query_ref[:, columns])]
    lane = lax.broadcasted_iota(jnp.int32, (BLOCK, LANES), 1)
    row = lax.broadcasted_iota(jnp.int32, (BLOCK, BLOCK), 0)
    col = lax.broadcasted_iota(jnp.int32, (BLOCK, BLOCK), 1)
    for index in range(length // BLOCK):
        rows = slice(index * BLOCK, (index + 1) * BLOCK)
        seen = index * BLOCK
        outs = []
        for which in range(2):
            head = 2 * pair + which
            kv = head // GROUP
            query = heads[which][rows]
            diagonal = mm(query, key_ref[kv, rows, :], NT) * scale
            diagonal = jnp.where(row >= col, diagonal, -1e30)
            top = jnp.max(diagonal, axis=-1, keepdims=True)
            if seen:
                before = mm(query, key_ref[kv, :seen, :], NT) * scale
                top = jnp.maximum(top, jnp.max(before, axis=-1, keepdims=True))
            probs = jnp.exp(diagonal - top).astype(BF16)
            mixed = mm(probs, value_ref[kv, rows, :])
            if seen:
                probs = jnp.exp(before - top).astype(BF16)
                mixed = mixed + mm(probs, value_ref[kv, :seen, :])
            total = mixed[:, HEAD_DIM : HEAD_DIM + 1]
            outs.append(mixed / total)
            log_ref[rows, :] = jnp.where(lane == head, top + jnp.log(total), log_ref[rows, :])
        mixed_ref[rows, columns] = join_heads(outs[0], outs[1]).astype(BF16)


def settle(length, x_ref, mixed_ref, weight_ref, vectors_ref, hidden_ref, normed_ref, turned_ref):
    width = x_ref.shape[2]
    gain = vectors_ref[2:3, :width]
    weight = weight_ref[1, :, :, BOTH - width :].reshape(width, width)
    for index in range(length // BLOCK):
        rows = slice(index * BLOCK, (index + 1) * BLOCK)
        half, start = index * BLOCK // (length // 2), index * BLOCK % (length // 2)
        hidden = x_ref[half, start : start + BLOCK, :].astype(F32) + mm(mixed_ref[rows, :], weight)
        hidden_ref[rows, :] = hidden
        scale = lax.rsqrt(jnp.mean(hidden * hidden, axis=-1, keepdims=True) + EPS)
        normed = (hidden * scale * gain).astype(BF16)
        normed_ref[rows, :] = normed
        turned_ref[:, rows] = normed.T


HALVES = ((0, 1), (2, 3))
WAYS = ((1, CHIPS // 2), (-1, CHIPS - 1 - CHIPS // 2))


def row_cuts(rows):
    early = rows // 2 // 16 * 16 if rows == 112 else 80
    return (0, early), (early, rows - early)


def feed_gather(ring, own_wide, own_down, wide, down, sems):
    rows, count = own_wide.shape[1], own_down.shape[0]
    pieces = []
    for (start, some), (down_start, down_some) in zip(row_cuts(rows), row_cuts(count)):

        def down_block(chip, start=down_start, some=down_some):
            return down.at[pl.ds(pl.multiple_of(chip * count + start, 16), some), :]

        def wide_block(chip, start=start, some=some):
            return wide.at[ring.mine, chip, pl.ds(start, some), :]

        pieces.append((1, own_down.at[pl.ds(down_start, down_some), :], down_block, None, 0, CHIPS - 1))
        pieces.append((-1, own_wide.at[ring.mine, pl.ds(start, some), :], wide_block, ring.peer, 1, CHIPS - 1))
    return Gather(ring, pieces, sems)


def feed_keep(ring, own_wide, own_down, wide, down, sems):
    count = own_down.shape[0]
    rows = pl.ds(pl.multiple_of(ring.chip * count, 16), count)
    return [
        pltpu.make_async_copy(own_wide, wide.at[:, ring.chip], sems.at[0]),
        pltpu.make_async_copy(own_down, down.at[rows, :], sems.at[1]),
    ]


def feed_reduce(ring, wide, down, wide_part, down_part, scratch):
    rows, count = wide_part.shape[0], down_part.shape[0]
    pieces = []
    for (start, some), (down_start, down_some) in zip(row_cuts(rows), row_cuts(count)):

        def down_block(chip, start=down_start, some=down_some):
            return down.at[pl.ds(pl.multiple_of(chip * count + start, 16), some), :]

        def own_block(chip, start=start, some=some):
            return wide.at[ring.mine, chip, pl.ds(start, some), :]

        def other_block(chip, start=start, some=some):
            return wide.at[1 - ring.mine, chip, pl.ds(start, some), :]

        down_out = down_part.at[pl.ds(down_start, down_some), :]
        pieces.append((1, down_block, None, None, down_out, CHIPS - 1, True))
        pieces.append((
            -1, own_block, other_block, ring.peer, wide_part.at[pl.ds(start, some), :], CHIPS - 1, True
        ))
    return make_reduce(ring, pieces, scratch)


def feed_reduce_scratch(rows, span, count, width):
    shapes = []
    for (_, some), (_, down_some) in zip(row_cuts(rows), row_cuts(count)):
        shapes += [(down_some, width, False), (some, span, True)]
    return reduce_scratch(shapes)


def first_kernel(
    length, plan,
    x_in, table_in, both_in, small_in, gate_in, up_in, down_in, cot_in,
    x_out, table_out, weight_out, turned1_out, query_out, key_out, value_out,
    vectors_ref, mixed_ref, log_ref, hidden_ref, own_wide2, own_down2,
    cot_out, wide_out, down_out, normed_out, turned_out,
    x_ref, table_ref, weight_ref, turned1_ref, query_ref, key_ref, value_ref,
    normed_ref, turned_ref, both_land, small_land, both_own, small_own, small_all, perm_ref, wide_land, own_wide1, own_down1,
    swap_sems, core_sems, keep_sems, cot_sems, store_sems, *sems,
):
    step = pl.program_id(0)
    ring = Ring(CHIPS)
    core, mine = ring.core, ring.mine
    gather = feed_gather(ring, own_wide1, own_down1, wide_out, down_out, sems[:4])
    keeps = feed_keep(ring, own_wide1, own_down1, wide_out, down_out, keep_sems)
    early = BOTH // 2
    pieces = []
    for start in (0, early):
        part = pl.ds(start, early)
        for direction, reach in WAYS:
            pieces.append((
                direction, both_own.at[:, part], lambda chip, part=part: weight_ref.at[core, chip, :, part],
                ring.partner, 0 if direction > 0 else 1, reach,
            ))
    for direction, reach in WAYS:
        pieces.append((direction, small_own, lambda chip: small_all.at[chip], None, 0, reach))
    attention = Gather(ring, pieces, sems[4:])
    every = range(len(pieces))
    swaps = [
        remote(src.at[1 - mine], dst.at[mine], swap_sems.at[2 * k], swap_sems.at[2 * k + 1], ring.peer)
        for k, (src, dst) in enumerate([(x_in, x_ref), (table_in, table_ref), (cot_in, cot_out.at[core])])
    ]
    trades = [
        remote(src, dst, core_sems.at[2 * k], core_sems.at[2 * k + 1], ring.partner)
        for k, (src, dst) in enumerate([
            (both_in.at[1 - core], both_land), (small_in, small_land), (perm_ref.at[1 - core], wide_land),
            (cot_out.at[core], cot_out.at[core]), (normed_ref, normed_out.at[core]),
            (turned_ref, turned_out.at[core]),
        ])
    ]
    cot_keep = pltpu.make_async_copy(cot_in.at[mine], cot_out.at[core, mine], cot_sems.at[0])
    stores = [
        pltpu.make_async_copy(src, dst, store_sems.at[k])
        for k, (src, dst) in enumerate([
            (x_ref, x_out), (table_ref, table_out), (weight_ref, weight_out), (turned1_ref, turned1_out),
            (query_ref, query_out), (key_ref, key_out), (value_ref, value_out),
            (normed_ref, normed_out.at[core]), (turned_ref, turned_out.at[core]),
        ])
    ]

    @pl.when(step == 0)
    def enter():
        ring.greet([ring.right, ring.left, ring.partner, ring.peer])
        trades[0].start()
        trades[1].start()
        for swap in swaps:
            swap.start()
        cot_keep.start()
        x_ref[mine] = x_in[mine]
        table_ref[mine] = table_in[mine]
        trades[0].wait()
        trades[1].wait()
        half = small_in.shape[0]
        rows = both_in.shape[1]
        for which in range(2):

            @pl.when(core == which)
            def own(which=which):
                pair = (both_in[which], both_land[...])
                both_own[...] = stack_rows(*pair[:: 1 - 2 * which]).astype(BF16)
                pair = (small_in[...], small_land[...])[:: 1 - 2 * which]
                lane = lax.broadcasted_iota(jnp.int32, (2 * half, LANES), 1)
                gains = stack_rows(pair[0][:rows], pair[1][:rows])
                gains = jnp.concatenate([gains, jnp.zeros((2 * (half - rows), LANES), F32)], axis=0)
                small_own[...] = jnp.where(lane == 0, stack_rows(*pair), gains).astype(BF16)

        attention.advance(0, every)
        weight_ref[core, ring.chip] = both_own[...]
        small_all[ring.chip] = small_own[...]
        wide = stack_rows(gate_in[...], up_in[...]).astype(BF16)
        for side in range(2):
            for group, span in enumerate(spans()):

                def store(tile, part, side=side, first=group * spans()[0]):
                    columns = slice(first + tile * LANES, first + (tile + 1) * LANES)
                    perm_ref[side, 0, :, columns] = part[:rows].astype(BF16)
                    perm_ref[side, 1, :, columns] = part[rows:].astype(BF16)

                gather_columns(wide, side, group, store)
        trades[2].start()
        own = sum(SPLITS)
        for group, ref in enumerate((own_down1, own_down2)):
            start, count = STARTS[group], SPLITS[group]
            ref[...] = stack_rows(
                down_in[start : start + count, :], down_in[own + start : own + start + count, :]
            ).astype(BF16)
        attention.advance(1, every)
        trades[2].wait()
        for which in range(2):

            @pl.when(core == which)
            def chip_rows(which=which):
                for tensor in range(2):
                    pair = (perm_ref[which, tensor], wide_land[tensor])
                    block = stack_rows(*pair[:: 1 - 2 * which]).astype(BF16)
                    own_wide1[tensor] = block[:, : spans()[0]]
                    own_wide2[tensor] = block[:, spans()[0] :]

        gather.advance(0, (0, 1, 2, 3))
        for keep in keeps:
            keep.start()
        for hop in range(2, WAYS[0][1] + 1):
            attention.advance(hop, every)
            if hop == 3:
                gather.advance(1, HALVES[0])
        gather.advance(1, HALVES[1])
        attention.finish()
        rows = small_all.shape[1]
        turned = small_all[...].astype(F32).reshape(CHIPS * rows, LANES).T
        vectors_ref[0:1, :] = turned[0:1, :]
        width = x_in.shape[2]
        chip_rows = width // CHIPS
        turned = small_all[:, :chip_rows, :].astype(F32).reshape(width, LANES).T
        vectors_ref[1:3, :width] = turned[1:3, :]
        swaps[0].wait()
        swaps[1].wait()
        project(length, x_ref, table_ref, vectors_ref, weight_ref, turned1_ref, query_ref, key_ref, value_ref)
        for store in stores[:-2]:
            store.start()
        log_ref[...] = jnp.zeros_like(log_ref)

    at_point(step, 1, plan, 1, 0, gather)

    @pl.when((step >= 1) & (step <= PAIRS))
    def pairs():
        attend_pair(step - 1, length, query_ref, key_ref, value_ref, mixed_ref, log_ref)

    @pl.when(step == 4)
    def cotangent():
        swaps[2].wait()
        cot_keep.wait()
        trades[3].start()

    @pl.when(step == PAIRS + 1)
    def last():
        settle(length, x_ref, mixed_ref, weight_ref, vectors_ref, hidden_ref, normed_ref, turned_ref)
        for copy in trades[4:] + stores[-2:]:
            copy.start()
        at_end(plan, gather)
        for copy in keeps + trades[3:] + stores:
            copy.wait()


def first_part(x, table, both, small, gate, up, down, cot):
    _, half, width = x.shape
    tokens = 2 * half
    rows, ff = gate.shape
    one, two = spans()
    down_rows = [2 * split for split in SPLITS]
    stored = [
        (x.shape, BF16), (table.shape, F32), ((2, CHIPS, 2 * rows, BOTH), BF16), ((width, tokens), BF16),
        ((tokens, width), BF16), ((KV_HEADS, tokens, LANES), BF16), ((KV_HEADS, tokens, LANES), BF16),
    ]
    kept = [
        ((8, 2 * CHIPS * small.shape[0]), F32), ((tokens, width), BF16), ((tokens, LANES), F32),
        ((tokens, width), F32),
        ((2, 2 * rows, two), BF16), ((down_rows[1], width), BF16),
    ]
    far = [
        ((2,) + cot.shape, BF16), ((2, CHIPS, 2 * rows, one), BF16), ((CHIPS * down_rows[0], width), BF16),
        ((2, tokens, width), BF16), ((2, width, tokens), BF16),
    ]
    ins = [x, table, both, small, gate, up, down]
    steps = [(hop, half) for hop in range(2, CHIPS) for half in HALVES]
    points = PAIRS + 1
    plan = [[] for _ in range(points + 1)]
    for index, move in enumerate(steps):
        plan[-(-(index + 1) * points // len(steps))].append(move)
    return pl.pallas_call(
        functools.partial(first_kernel, tokens, plan),
        grid=(PAIRS + 2,),
        in_specs=[inside(part.shape) for part in ins] + [ANY],
        out_specs=[ANY] * len(stored) + [inside(shape) for shape, _ in kept] + [ANY] * len(far),
        out_shape=[jax.ShapeDtypeStruct(shape, kind) for shape, kind in stored + kept + far],
        scratch_shapes=[pltpu.VMEM(shape, kind) for shape, kind in stored]
        + [
            pltpu.VMEM((tokens, width), BF16), pltpu.VMEM((width, tokens), BF16),
            pltpu.VMEM(both.shape[1:], BF16), pltpu.VMEM(small.shape, BF16),
            pltpu.VMEM((2 * rows, BOTH), BF16), pltpu.VMEM((2 * small.shape[0], LANES), BF16),
            pltpu.VMEM((CHIPS, 2 * small.shape[0], LANES), BF16),
            pltpu.VMEM((2, 2, rows, one + two), BF16), pltpu.VMEM((2, rows, one + two), BF16),
            pltpu.VMEM((2, 2 * rows, one), BF16), pltpu.VMEM((down_rows[0], width), BF16),
            dma(6), dma(12), dma(2), dma(1), dma(len(stored) + 2),
        ]
        + gather_sems(4)
        + gather_sems(6),
        compiler_params=pltpu.CompilerParams(
            collective_id=0, has_side_effects=True, vmem_limit_bytes=VMEM_LIMIT
        ),
    )(*ins, cot)


def feed_chunk(count, offset, normed_ref, turned_ref, cot_ref, wide, down, result_ref, d_normed_ref, work, pause):
    width = normed_ref.shape[2]
    columns = pl.ds(offset, count)
    gate_weight = wide[0, :, :, columns].reshape(width, count)
    up_weight = wide[1, :, :, columns].reshape(width, count)
    down_weight = down[columns, :]
    act_at, gate_at, up_at = (slice(k * CHUNK, k * CHUNK + count) for k in range(3))
    parts = normed_ref.shape[1] // QUARTER
    for part in range(2 * parts):
        core, rows = part // parts, slice(part % parts * QUARTER, (part % parts + 1) * QUARTER)
        normed, cot = normed_ref[core, rows, :], cot_ref[core, rows, :]
        gate = mm(normed, gate_weight)
        up = mm(normed, up_weight)
        d_act = mm(cot, down_weight, NT)
        sigma = jax.nn.sigmoid(gate)
        silu = gate * sigma
        act = (silu * up).astype(BF16)
        d_gate = (d_act * up * sigma * (1.0 + gate * (1.0 - sigma))).astype(BF16)
        d_up = (d_act * silu).astype(BF16)
        work[core, rows, act_at], work[core, rows, gate_at], work[core, rows, up_at] = act, d_gate, d_up
        result_ref[core, rows, :] += mm(act, down_weight)
        d_normed_ref[core, rows, :] += mm(d_gate, gate_weight, NT) + mm(d_up, up_weight, NT)
        if part + 1 == parts:
            pause(1)
    pause(2)
    for tensor, at in ((0, gate_at), (1, up_at)):
        grad = mm(turned_ref[0], work[0, :, at]) + mm(turned_ref[1], work[1, :, at])
        wide[tensor, :, :, columns] = grad.astype(BF16).reshape(wide.shape[1], wide.shape[2], count)
    grad = mm(work[0, :, act_at], cot_ref[0], TN) + mm(work[1, :, act_at], cot_ref[1], TN)
    down[columns, :] = grad.astype(BF16)


def feed_kernel(
    gather_plan, reduce_plan,
    normed_ref, turned_ref, cot_ref, hidden_in, wide_in, down_in, own_wide, own_down,
    result_out, d_normed_out, other_out, wide_out, down_out, wide_part, down_part,
    result_ref, d_normed_ref, work, wide1, down1, wide2, down2,
    load_sems, keep_sems, trade_sems, store_sems, *scratch,
):
    step = pl.program_id(0)
    ring = Ring(CHIPS)
    core = ring.core
    gather = feed_gather(ring, own_wide, own_down, wide2, down2, scratch[:4])
    keeps = feed_keep(ring, own_wide, own_down, wide2, down2, keep_sems)
    reduce = feed_reduce(ring, wide1, down1, wide_part, down_part, scratch[4:])
    loads = [
        pltpu.make_async_copy(src, dst, load_sems.at[k])
        for k, (src, dst) in enumerate([(wide_in, wide1), (down_in, down1), (hidden_in, result_ref.at[core])])
    ]
    trades = [
        remote(work.at[k], other_out.at[k], trade_sems.at[2 * k], trade_sems.at[2 * k + 1], ring.partner)
        for k in range(2)
    ]
    stores = [
        pltpu.make_async_copy(src, dst, store_sems.at[k])
        for k, (src, dst) in enumerate([
            (wide2, wide_out), (down2, down_out), (result_ref.at[core], result_out),
            (d_normed_ref.at[core], d_normed_out),
        ])
    ]
    one, two = wide1.shape[3], wide2.shape[3]
    turns, last = one // CHUNK, one // CHUNK + -(-two // CHUNK) - 1

    @pl.when(step == 0)
    def begin():
        for load in loads:
            load.start()
        ring.greet([ring.right, ring.left, ring.partner, ring.peer])

    at_point(step, 0, gather_plan, 3, 0, gather)

    @pl.when(step == 0)
    def start():
        for keep in keeps:
            keep.start()
        result_ref[1 - core] = jnp.zeros(result_ref.shape[1:], F32)
        d_normed_ref[...] = jnp.zeros_like(d_normed_ref)
        for load in loads:
            load.wait()

    def chunk(count, offset, wide, down, first, plan, transfer):
        feed_chunk(
            count, offset, normed_ref, turned_ref, cot_ref, wide, down, result_ref, d_normed_ref, work,
            lambda which: at_point(step, first, plan, 3, which, transfer),
        )

    @pl.when(step < turns)
    def first_group():
        chunk(CHUNK, pl.multiple_of(step * CHUNK, CHUNK), wide1, down1, 0, gather_plan, gather)

    @pl.when(step == turns - 1)
    def between():
        at_end(gather_plan, gather)
        for keep in keeps:
            keep.wait()
        reduce.begin()

    at_point(step, turns, reduce_plan, 3, 0, reduce)

    @pl.when((step >= turns) & (step < last))
    def second_group():
        chunk(CHUNK, pl.multiple_of((step - turns) * CHUNK, CHUNK), wide2, down2, turns, reduce_plan, reduce)

    @pl.when(step == last)
    def end():
        done = (last - turns) * CHUNK
        chunk(two - done, done, wide2, down2, turns, reduce_plan, reduce)
        for store in stores:
            store.start()
        work[0] = result_ref[1 - core].astype(BF16)
        trades[0].start()
        work[1] = d_normed_ref[1 - core].astype(BF16)
        trades[1].start()
        at_end(reduce_plan, reduce)
        for copy in trades + stores:
            copy.wait()


def feed(normed, turned, cot, hidden, wide, down, own_wide, own_down):
    _, tokens, width = normed.shape
    one, two = wide.shape[3], own_wide.shape[2]
    rows = own_wide.shape[1]
    counts = [2 * split for split in SPLITS]
    turns, more = one // CHUNK, -(-two // CHUNK)
    wide_two, down_two = (2, CHIPS, rows, two), (CHIPS * counts[1], width)
    whole, halves = (tokens, width), (2, tokens, width)
    far = [(whole, F32), (whole, F32), (halves, BF16), (wide_two, BF16), (down_two, BF16)]
    near = [((rows, one), F32), ((counts[0], width), F32)]
    return pl.pallas_call(
        functools.partial(
            feed_kernel, spread(3 * turns, HALVES, len(HALVES)), spread(3 * more, HALVES, 0)
        ),
        grid=(turns + more,),
        in_specs=[inside(part.shape) for part in (normed, turned, cot)] + [ANY] * 5,
        out_specs=[ANY] * len(far) + [inside(shape) for shape, _ in near],
        out_shape=[jax.ShapeDtypeStruct(shape, kind) for shape, kind in far + near],
        scratch_shapes=[
            pltpu.VMEM(halves, F32), pltpu.VMEM(halves, F32), pltpu.VMEM(halves, BF16),
            pltpu.VMEM(wide.shape, BF16), pltpu.VMEM(down.shape, BF16),
            pltpu.VMEM(wide_two, BF16), pltpu.VMEM(down_two, BF16),
            dma(3), dma(2), dma(4), dma(4),
        ]
        + gather_sems(4)
        + feed_reduce_scratch(rows, one, counts[0], width),
        compiler_params=pltpu.CompilerParams(
            collective_id=1, has_side_effects=True, vmem_limit_bytes=VMEM_LIMIT
        ),
    )(normed, turned, cot, hidden, wide, down, own_wide, own_down)


def unsettle(
    rows, first, hidden_ref, d_own_ref, other_ref, own_ref, cot_ref, vectors_ref, mixed_ref, weight_ref,
    d_hidden_ref, d_mixed_ref, output_grad_ref, second_ref, result_ref, place,
):
    width = hidden_ref.shape[1]
    gain = vectors_ref[2:3, :width]
    weight = weight_ref[0, :, BOTH - width :]
    hidden = hidden_ref[...]
    upstream = d_own_ref[...] + other_ref[1].astype(F32)
    scale = lax.rsqrt(jnp.mean(hidden * hidden, axis=-1, keepdims=True) + EPS)
    weighted = upstream * gain
    inner = jnp.mean(weighted * hidden, axis=-1, keepdims=True)
    d_hidden = cot_ref[rows, :].astype(F32) + scale * weighted - hidden * (scale * scale * scale * inner)
    d_hidden_ref[rows, :] = d_hidden
    result_ref[place] = (own_ref[...] + other_ref[0].astype(F32)).astype(BF16)
    branch = d_hidden.astype(BF16)
    d_mixed_ref[rows, :] = mm(branch, weight, NT).astype(BF16)
    grad = mm(mixed_ref[rows, :], branch, TN)
    part = jnp.sum(upstream * hidden * scale, axis=0, keepdims=True)

    @pl.when(first)
    def begin():
        second_ref[...] = part
        output_grad_ref[...] = grad

    @pl.when(jnp.logical_not(first))
    def more():
        second_ref[...] += part
        output_grad_ref[...] += grad


def back_head(pair, which, length, query_ref, grad_ref, mixed_ref, log_ref, key_ref, value_ref, d_key_ref, d_value_ref):
    scale = HEAD_DIM**-0.5
    columns = pl.ds(pl.multiple_of(pair * LANES, LANES), LANES)
    query, grad, mixed = (split_heads(ref[:, columns])[which] for ref in (query_ref, grad_ref, mixed_ref))
    lane = lax.broadcasted_iota(jnp.int32, (length, LANES), 1)
    row = lax.broadcasted_iota(jnp.int32, (BLOCK, BLOCK), 0)
    col = lax.broadcasted_iota(jnp.int32, (BLOCK, BLOCK), 1)
    head = 2 * pair + which
    kv = head // GROUP
    log_total = jnp.sum(jnp.where(lane == head, log_ref[...], 0.0), axis=-1, keepdims=True)
    inner = jnp.sum(grad * mixed, axis=-1, keepdims=True)
    query_low, grad_low = query.astype(BF16), grad.astype(BF16)
    query, grad = widen(query * scale, -log_total), widen(grad, -inner)
    parts = [None] * (length // BLOCK)
    for index in range(length // BLOCK):
        own = slice(index * BLOCK, (index + 1) * BLOCK)
        keys, values = key_ref[kv, own, :], value_ref[kv, own, :]
        key_sum = value_sum = None
        for other in range(index, length // BLOCK):
            rows = slice(other * BLOCK, (other + 1) * BLOCK)
            scores = mm(keys, query[rows], NT)
            if other == index:
                scores = jnp.where(row <= col, scores, -1e30)
            probs = jnp.exp(scores)
            d_scores = (probs * mm(values, grad[rows], NT)).astype(BF16)
            value_part = mm(probs.astype(BF16), grad_low[rows])
            key_part = mm(d_scores, query_low[rows])
            key_sum = key_part if key_sum is None else key_sum + key_part
            value_sum = value_part if value_sum is None else value_sum + value_part
            part = mm(d_scores, keys, TN)
            parts[other] = part if parts[other] is None else parts[other] + part
        d_key_ref[kv, own, :] += key_sum * scale
        d_value_ref[kv, own, :] += value_sum
    return parts


def back_kernel_all(
    length, plan,
    hidden_ref, d_own_ref, other_ref, own_ref,
    vectors_ref, weight_ref, mixed_ref, query_ref, log_ref, key_ref, value_ref, wide_before, down_before,
    wide_ref, down_ref, cot_in,
    d_hidden_ref, output_grad_out, second_ref, d_query_ref, d_key_ref, d_value_ref,
    wide_own, down_own, wide_part, down_part, result_ref,
    d_mixed_ref, cot_ref, output_grad_ref, half_ref, load_sem, *scratch,
):
    step = pl.program_id(0)
    ring = Ring(CHIPS)
    share = Share(ring, wide_before, wide_own, scratch[:5])
    share_rows = ShareRows(ring, down_before, down_own, scratch[5:8])
    reduce = feed_reduce(ring, wide_ref, down_ref, wide_part, down_part, scratch[8:])
    load = pltpu.make_async_copy(cot_in.at[ring.core], cot_ref, load_sem.at[0])
    blocks = length // BLOCK

    @pl.when(step == 0)
    def begin():
        load.start()
        ring.greet([ring.right, ring.left, ring.partner, ring.peer])
        reduce.begin()
        share.first()
        share_rows.first()
        d_key_ref[...] = jnp.zeros_like(d_key_ref)
        d_value_ref[...] = jnp.zeros_like(d_value_ref)
        load.wait()

    at_point(step, 0, plan, 2, 0, reduce)

    @pl.when(step < blocks)
    def norms():
        rows = pl.ds(pl.multiple_of(step * BLOCK, BLOCK), BLOCK)
        halves = length // 2 // BLOCK
        place = (lax.div(step, halves), pl.ds(pl.multiple_of(lax.rem(step, halves) * BLOCK, BLOCK), BLOCK))
        unsettle(
            rows, step == 0, hidden_ref, d_own_ref, other_ref, own_ref, cot_ref, vectors_ref, mixed_ref, weight_ref,
            d_hidden_ref, d_mixed_ref, output_grad_ref, second_ref, result_ref, place,
        )

    @pl.when(step == blocks - 1)
    def after():
        output_grad_out[...] = output_grad_ref[...].astype(BF16)
        share.second()
        share_rows.second()

    refs = (query_ref, d_mixed_ref, mixed_ref, log_ref, key_ref, value_ref, d_key_ref, d_value_ref)

    @pl.when(step >= blocks)
    def first_head():
        parts = back_head(step - blocks, 0, length, *refs)
        for index, part in enumerate(parts):
            half_ref[index * BLOCK : (index + 1) * BLOCK, :] = part

    at_point(step, 0, plan, 2, 1, reduce)

    @pl.when(step >= blocks)
    def second_head():
        scale = HEAD_DIM**-0.5
        columns = pl.ds(pl.multiple_of((step - blocks) * LANES, LANES), LANES)
        parts = back_head(step - blocks, 1, length, *refs)
        for index, part in enumerate(parts):
            rows = slice(index * BLOCK, (index + 1) * BLOCK)
            d_query_ref[rows, columns] = (join_heads(half_ref[rows, :], part) * scale).astype(BF16)

    @pl.when(step == blocks + PAIRS - 1)
    def last():
        at_end(plan, reduce)
        share.third()


def back_all(
    hidden, d_own, other, own, vectors, weight, mixed, query, logs, keys, values, wide_before, down_before,
    wide, down, cot,
):
    tokens, width = hidden.shape
    rows, before = wide_before.shape
    span = wide.shape[3]
    counts = [2 * split for split in SPLITS]
    blocks = tokens // BLOCK

    def block(step):
        return jnp.minimum(step, blocks - 1)

    line = pl.BlockSpec((BLOCK, width), lambda s: (block(s), 0))
    pair = pl.BlockSpec((2, BLOCK, width), lambda s: (0, block(s), 0))
    late = pl.BlockSpec((1, width, BOTH), lambda s: (1, 0, 0), pipeline_mode=pl.Buffered(1))
    ins = [mixed, query, logs, keys, values, wide_before, down_before, wide, down]
    outs = [
        ((tokens, width), F32), ((width, width), BF16), ((1, width), F32), (query.shape, BF16),
        (keys.shape, F32), (values.shape, F32),
        ((2, 2, rows // OWNERS, before), F32), ((counts[0] // 2, width), F32),
        ((rows, span), F32), ((counts[1], width), F32), ((2, tokens // 2, width), BF16),
    ]
    moves = [(hop, half) for hop in range(CHIPS) for half in HALVES]
    plan = [[] for _ in range(2 * (blocks + PAIRS) + 1)]
    for place, move in zip([2 * blocks - 4, 2 * blocks - 2] + list(range(2 * blocks, len(plan) - 1)), moves):
        plan[place].append(move)
    return pl.pallas_call(
        functools.partial(back_kernel_all, tokens, plan),
        grid=(blocks + PAIRS,),
        in_specs=[line, line, pair, line, inside(vectors.shape), late]
        + [inside(part.shape) for part in ins]
        + [ANY],
        out_specs=[inside(shape) for shape, _ in outs],
        out_shape=[jax.ShapeDtypeStruct(shape, kind) for shape, kind in outs],
        scratch_shapes=[
            pltpu.VMEM((tokens, width), BF16), pltpu.VMEM((tokens, width), BF16),
            pltpu.VMEM((width, width), F32), pltpu.VMEM((tokens, LANES), F32), dma(1),
        ]
        + share_scratch(rows // OWNERS, before, True)
        + share_rows_scratch(counts[0] // 2, width)
        + feed_reduce_scratch(rows, span, counts[1], width),
        compiler_params=pltpu.CompilerParams(
            collective_id=2, has_side_effects=True, vmem_limit_bytes=VMEM_LIMIT
        ),
    )(hidden, d_own, other, own, vectors, weight, *ins, cot)


def last_kernel(
    length,
    d_query_ref, d_key_ref, d_value_ref, table_ref, turned_ref, x_ref, vectors_ref, weight_ref, d_hidden_ref,
    output_grad_ref, second_ref, wide_first, down_first, wide_before, down_before, result_ref,
    qkv_grad_out, output_grad_out, bits_out, gate_grad_out, up_grad_out, down_grad_out, input_grad_out, result_out,
    d_pre_ref, both_ref, part_ref, both_own, wide_own, down_own, bits_ref, bits_land, bits_sum,
    input_grad_ref, input_grad_land, bits_send, bits_recv, swap_sems, bit_sems, *scratch,
):
    ring = Ring(CHIPS)
    core, mine = ring.core, ring.mine
    others = [{"fsdp": 2 * ring.chip_at(offset) + core} for offset in range(1, CHIPS)]
    ring.greet(others + [ring.partner, ring.peer])
    share = Share(ring, wide_before, wide_own, scratch[:5])
    share_rows = ShareRows(ring, down_before, down_own, scratch[5:8])
    share_both = Share(ring, part_ref, both_own, scratch[8:13])
    early = BOTH // 2
    pieces = []
    for start in (0, early):
        part = pl.ds(start, early)
        for direction, reach in WAYS:
            pieces.append((
                direction,
                lambda chip, part=part: both_ref.at[core, chip, :, part],
                lambda chip, part=part: both_ref.at[1 - core, chip, :, part],
                ring.partner, part_ref.at[:, part], reach, direction > 0,
            ))
    reduce = make_reduce(ring, pieces, scratch[13:])
    share.first()
    share_rows.first()
    result_keep = pltpu.make_async_copy(result_ref.at[mine], result_out.at[mine], swap_sems.at[4])
    result_swap = remote(result_ref.at[1 - mine], result_out.at[mine], swap_sems.at[2], swap_sems.at[3], ring.peer)

    qwidth = HEADS * HEAD_DIM
    width = d_hidden_ref.shape[1]
    half = length // 2
    bias = None
    for index in range(length // BLOCK):
        rows = slice(index * BLOCK, (index + 1) * BLOCK)
        cosine, sine = tables(table_ref[index * BLOCK // half, index * BLOCK % half : index * BLOCK % half + BLOCK, :])

        def back(part):
            return (part * cosine - swap_halves(part) * sine).astype(BF16)

        for tile in range(PAIRS):
            columns = slice(tile * LANES, (tile + 1) * LANES)
            d_pre_ref[rows, columns] = back(d_query_ref[rows, columns].astype(F32))
        keys = join_heads(d_key_ref[0, rows, :], d_key_ref[1, rows, :]).astype(BF16).astype(F32)
        d_pre_ref[rows, qwidth : qwidth + LANES] = back(keys)
        values = join_heads(d_value_ref[0, rows, :], d_value_ref[1, rows, :])
        d_pre_ref[rows, qwidth + LANES :] = values.astype(BF16)
        part = jnp.sum(d_pre_ref[rows, :].astype(F32), axis=0, keepdims=True)
        bias = part if bias is None else bias + part

    chip_rows = width // CHIPS
    grad = mm(turned_ref[...], d_pre_ref[...]).astype(BF16)
    rest = grad.shape[1] - BOTH
    for chip in range(CHIPS):
        rows = slice(chip * chip_rows, (chip + 1) * chip_rows)
        both_ref[0, chip] = grad[rows, :BOTH]
        both_ref[1, chip, :, :rest] = grad[rows, BOTH:]
        both_ref[1, chip, :, rest:] = output_grad_ref[rows, :]
    reduce.begin()
    reduce.advance(0, range(len(pieces)))
    result_keep.start()
    result_swap.start()
    share.second()
    share_rows.second()

    gain = vectors_ref[1:2, :width]
    weight_early, weight_late = weight_ref[0], weight_ref[1, :, : qwidth + 2 * LANES - BOTH]
    first = None
    for index in range(length // BLOCK):
        rows = slice(index * BLOCK, (index + 1) * BLOCK)
        which, start = index * BLOCK // half, index * BLOCK % half
        x = x_ref[which, start : start + BLOCK, :].astype(F32)
        upstream = mm(d_pre_ref[rows, :BOTH], weight_early, NT) + mm(d_pre_ref[rows, BOTH:], weight_late, NT)
        scale = lax.rsqrt(jnp.mean(x * x, axis=-1, keepdims=True) + EPS)
        weighted = upstream * gain
        inner = jnp.mean(weighted * x, axis=-1, keepdims=True)
        d_x = d_hidden_ref[rows, :] + scale * weighted - x * (scale * scale * scale * inner)
        part = jnp.sum(upstream * x * scale, axis=0, keepdims=True)
        first = part if first is None else first + part
        input_grad_ref[which, start : start + BLOCK, :] = d_x.astype(BF16)
        reduce.advance(index + 1, range(len(pieces)))
    swap = remote(input_grad_ref.at[1 - mine], input_grad_land, swap_sems.at[0], swap_sems.at[1], ring.peer)
    swap.start()

    bits_ref[...] = jnp.zeros_like(bits_ref)
    for chip in range(CHIPS):
        line = 0
        for values, each in ((bias, bias.shape[1] // CHIPS), (first, chip_rows), (second_ref[...], chip_rows)):
            for owner in range(OWNERS):
                count = each // OWNERS
                start = chip * each + owner * count
                bits_ref[chip, line : line + 1, :count] = values[:, start : start + count]
                line += 1
    copies = [
        remote(bits_ref.at[ring.chip_at(k + 1)], bits_land.at[k], bits_send.at[k], bits_recv.at[k], others[k])
        for k in range(CHIPS - 1)
    ]
    for copy in copies:
        copy.start()
    input_grad_out[mine] = input_grad_ref[mine].astype(F32)
    share.third()
    down_grad_out[: down_first.shape[0], :] = down_first[...]
    down_grad_out[down_first.shape[0] :, :] = down_own[...]
    own_rows = gate_grad_out.shape[0]
    sources = []
    for ref in (wide_first, wide_own):
        sources.append([stack_rows(ref[0, k], ref[1, k]).astype(BF16) for k in range(2)])

    def store(tile, part):
        columns = slice(tile * LANES, (tile + 1) * LANES)
        gate_grad_out[:, columns] = part[:own_rows]
        up_grad_out[:, columns] = part[own_rows:]

    spread_columns(sources, store, gate_grad_out.shape[1])
    share_both.first()
    total = bits_ref[ring.chip]
    for k, copy in enumerate(copies):
        copy.wait()
        total = total + bits_land[k]
    bits_sum[0] = total
    over_core = remote(bits_sum.at[0], bits_sum.at[1], bit_sems.at[0], bit_sems.at[1], ring.partner)
    over_core.start()
    over_core.wait()
    bits_sum[2] = bits_sum[0] + bits_sum[1]
    over_seq = remote(bits_sum.at[2], bits_sum.at[3], bit_sems.at[2], bit_sems.at[3], ring.peer)
    over_seq.start()
    swap.wait()
    input_grad_out[1 - mine] = input_grad_land[...].astype(F32)
    share_both.second()
    over_seq.wait()
    bits_out[...] = bits_sum[2] + bits_sum[3]
    share_both.third()
    rest = qkv_grad_out.shape[1] - BOTH
    qkv_grad_out[:, :BOTH] = both_own[0]
    qkv_grad_out[:, BOTH:] = both_own[1, :, :rest]
    output_grad_out[...] = both_own[1, :, rest:]
    reduce.finish()
    result_swap.wait()
    result_keep.wait()


def last_part(
    d_query, d_key, d_value, table, turned, x, vectors, weight, d_hidden, output_grad, second,
    wide_first, down_first, wide_before, down_before, result,
):
    tokens, width = d_hidden.shape
    ins = [
        d_query, d_key, d_value, table, turned, x, vectors, weight, d_hidden, output_grad, second,
        wide_first, down_first, wide_before, down_before,
    ]
    rows, span = wide_before.shape
    own_rows = rows // OWNERS
    own = sum(SPLITS)
    halves = (2, tokens // 2, width)
    qkv = vectors.shape[1]
    outs = [
        (own_rows, qkv), (own_rows, width), (BITS, LANES), (own_rows, 2 * CHIPS * 2 * own),
        (own_rows, 2 * CHIPS * 2 * own), (own, width), halves,
    ]
    return pl.pallas_call(
        functools.partial(last_kernel, tokens),
        in_specs=[pl.BlockSpec(memory_space=pltpu.VMEM)] * len(ins) + [ANY],
        out_specs=[pl.BlockSpec(memory_space=pltpu.VMEM)] * len(outs) + [ANY],
        out_shape=[jax.ShapeDtypeStruct(shape, F32) for shape in outs]
        + [jax.ShapeDtypeStruct(result.shape, BF16)],
        scratch_shapes=[
            pltpu.VMEM((tokens, qkv), BF16), pltpu.VMEM((2, CHIPS, rows, BOTH), BF16),
            pltpu.VMEM((rows, BOTH), F32), pltpu.VMEM((2, own_rows, BOTH), F32),
            pltpu.VMEM((2, 2, own_rows, span), F32), pltpu.VMEM((SPLITS[1], width), F32),
            pltpu.VMEM((CHIPS, BITS, LANES), F32), pltpu.VMEM((CHIPS - 1, BITS, LANES), F32),
            pltpu.VMEM((4, BITS, LANES), F32), pltpu.VMEM(halves, BF16), pltpu.VMEM(halves[1:], BF16),
            dma(CHIPS - 1), dma(CHIPS - 1), dma(5), dma(4),
        ]
        + share_scratch(own_rows, span, True)
        + share_rows_scratch(SPLITS[1], width)
        + share_scratch(own_rows, BOTH, False)
        + reduce_scratch([(rows, BOTH // 2, True)] * 4),
        compiler_params=pltpu.CompilerParams(
            collective_id=3, has_side_effects=True, vmem_limit_bytes=VMEM_LIMIT
        ),
    )(*ins, result)


def ring_shards(
    inputs, positions, qkv_weight, qkv_bias, output_weight, first_gain,
    gate_weight, up_weight, down_weight, second_gain, cotangent,
):
    _, half, width = inputs.shape
    tokens = 2 * half
    rows = gate_weight.shape[0]
    freqs = THETA ** (-jnp.arange(0, HEAD_DIM, 2).astype(F32) / HEAD_DIM)
    angles = positions.astype(F32)[..., None] * freqs
    cosine, sine = jnp.cos(angles), jnp.sin(angles)
    table = jnp.concatenate([cosine, cosine, -sine, sine], axis=-1)
    both = jnp.stack([
        qkv_weight[:, :BOTH], jnp.concatenate([qkv_weight[:, BOTH:], output_weight], axis=1),
    ])
    own_bias = qkv_bias.shape[0]
    pad = (0, own_bias - rows)
    small = jnp.stack([qkv_bias, jnp.pad(first_gain, pad), jnp.pad(second_gain, pad)], axis=1)
    small = jnp.pad(small, ((0, 0), (0, LANES - 3)))
    (
        x, table, weight, turned1, query, keys, values,
        vectors, mixed, logs, hidden, own_wide, own_down, cot, wide, down, normed2, turned2,
    ) = first_part(inputs, table, both, small, gate_weight, up_weight, down_weight, cotangent)
    weight = weight.reshape(2, width, BOTH)
    cot = cot.reshape(2, tokens, width)
    own, d_own, other, wide_second, down_second, wide_part_first, down_part_first = feed(
        normed2, turned2, cot, hidden, wide, down, own_wide, own_down
    )
    (
        d_hidden, output_grad, second, d_query, d_key, d_value,
        wide_first, down_first, wide_part_second, down_part_second, result,
    ) = back_all(
        hidden, d_own, other, own, vectors, weight, mixed, query, logs, keys, values,
        wide_part_first, down_part_first, wide_second, down_second, cot,
    )
    qkv_grad, output_grad, bits, gate_grad, up_grad, down_grad, input_grad, result = last_part(
        d_query, d_key, d_value, table, turned1, x, vectors, weight, d_hidden, output_grad, second,
        wide_first, down_first, wide_part_second, down_part_second, result,
    )
    owner = 2 * lax.rem(lax.axis_index("fsdp"), 2) + lax.axis_index("seq")

    def own_bits(which, count):
        return lax.dynamic_index_in_dim(bits, which * OWNERS + owner, 0, keepdims=False)[:count]

    return (
        result,
        input_grad,
        qkv_grad,
        own_bits(0, own_bias // 2),
        output_grad,
        own_bits(1, rows // 2),
        gate_grad,
        up_grad,
        down_grad,
        own_bits(2, rows // 2),
    )


def solution(mesh):
    tokens = P("fsdp", "seq", None)
    rows, row = P("fsdp", None), P("fsdp")
    grads, grad = P(("fsdp", "seq"), None), P(("fsdp", "seq"))
    ready = mesh.shape["fsdp"] == 2 * CHIPS and mesh.shape["seq"] == 2
    step = ring_shards if ready else plain_shards
    return jax.shard_map(
        step,
        mesh=mesh,
        in_specs=(tokens, P("fsdp", "seq"), rows, row, rows, row, rows, rows, rows, row, tokens),
        out_specs=(tokens, tokens, grads, grad, grads, grad, grads, grads, grads, grad),
        check_vma=False,
    )
```

```python
import functools

import jax
import jax.numpy as jnp
from jax import lax
from jax.experimental import pallas as pl
from jax.experimental.pallas import tpu as pltpu
from jax.sharding import PartitionSpec as P

HEADS = 14
KV_HEADS = 2
HEAD_DIM = 64
GROUP = HEADS // KV_HEADS
PAIRS = HEADS // 2
LANES = 128
BLOCK = 256
CHUNK = 256
EPS = 1e-06
THETA = 1000000.0
BF16 = jnp.bfloat16
F32 = jnp.float32
VMEM_LIMIT = 60 * 1024 * 1024

NN = (((1,), (0,)), ((), ()))
NT = (((1,), (1,)), ((), ()))
TN = (((0,), (0,)), ((), ()))


def mm(left, right, dims=NN):
    return lax.dot_general(left, right, dims, preferred_element_type=F32)


def params():
    return pltpu.CompilerParams(vmem_limit_bytes=VMEM_LIMIT)


def swap_halves(values):
    lane = lax.broadcasted_iota(jnp.int32, values.shape, 1)
    half = HEAD_DIM // 2
    ahead = pltpu.roll(values, LANES - half, 1)
    behind = pltpu.roll(values, half, 1)
    return jnp.where(lane % HEAD_DIM < half, ahead, behind)


def qkv_kernel(x_ref, gain_ref, weight_ref, bias_ref, cos_ref, sin_ref, normed_ref, query_ref, pair_ref):
    x = x_ref[...].astype(F32)
    scale = lax.rsqrt(jnp.mean(x * x, axis=-1, keepdims=True) + EPS)
    normed = (x * scale * gain_ref[...].astype(F32)).astype(BF16)
    normed_ref[...] = normed
    pre = mm(normed, weight_ref[...]) + bias_ref[...].astype(F32)
    cosine, sine = cos_ref[...], sin_ref[...]
    qwidth = HEADS * HEAD_DIM
    for tile in range(PAIRS):
        part = pre[:, tile * LANES : (tile + 1) * LANES]
        turned = part * cosine + swap_halves(part) * sine
        query_ref[:, tile * LANES : (tile + 1) * LANES] = turned.astype(BF16)
    part = pre[:, qwidth : qwidth + LANES]
    pair_ref[:, :LANES] = (part * cosine + swap_halves(part) * sine).astype(BF16)
    pair_ref[:, LANES:] = pre[:, qwidth + LANES :].astype(BF16)


def split_heads(block):
    wide = block.astype(F32)
    lane = lax.broadcasted_iota(jnp.int32, wide.shape, 1)
    first = jnp.where(lane < HEAD_DIM, wide, 0.0)
    second = jnp.where(lane < HEAD_DIM, pltpu.roll(wide, HEAD_DIM, 1), 0.0)
    return first, second


def join_heads(first, second):
    lane = lax.broadcasted_iota(jnp.int32, first.shape, 1)
    return jnp.where(lane < HEAD_DIM, first, pltpu.roll(second, HEAD_DIM, 1))


def attend_kernel(length, query_ref, key_ref, value_ref, mixed_ref, log_ref):
    pair = pl.program_id(1)
    scale = HEAD_DIM**-0.5
    heads = [part.astype(BF16) for part in split_heads(query_ref[0])]
    lane = lax.broadcasted_iota(jnp.int32, (BLOCK, LANES), 1)
    row = lax.broadcasted_iota(jnp.int32, (BLOCK, BLOCK), 0)
    col = lax.broadcasted_iota(jnp.int32, (BLOCK, BLOCK), 1)
    for index in range(length // BLOCK):
        rows = slice(index * BLOCK, (index + 1) * BLOCK)
        seen = index * BLOCK
        outs = []
        for which in range(2):
            head = 2 * pair + which
            kv = head // GROUP
            query = heads[which][rows]
            keys = key_ref[0, kv]
            diagonal = mm(query, keys[rows], NT) * scale
            diagonal = jnp.where(row >= col, diagonal, -1e30)
            top = jnp.max(diagonal, axis=-1, keepdims=True)
            if seen:
                before = mm(query, keys[:seen], NT) * scale
                top = jnp.maximum(top, jnp.max(before, axis=-1, keepdims=True))
            probs = jnp.exp(diagonal - top).astype(BF16)
            mixed = mm(probs, value_ref[0, kv, rows, :])
            if seen:
                probs = jnp.exp(before - top).astype(BF16)
                mixed = mixed + mm(probs, value_ref[0, kv, :seen, :])
            total = mixed[:, HEAD_DIM : HEAD_DIM + 1]
            outs.append(mixed / total)
            kept = jnp.where(lane == head, top + jnp.log(total), log_ref[0, rows, :])
            log_ref[0, rows, :] = kept
        mixed_ref[0, rows, :] = join_heads(outs[0], outs[1]).astype(BF16)


def widen(values, column):
    lane = lax.broadcasted_iota(jnp.int32, values.shape, 1)
    high = column.astype(BF16).astype(F32)
    middle = (column - high).astype(BF16).astype(F32)
    low = column - high - middle
    values = jnp.where(lane == HEAD_DIM, high, values)
    values = jnp.where(lane == HEAD_DIM + 1, middle, values)
    return jnp.where(lane == HEAD_DIM + 2, low, values).astype(BF16)


def back_kernel(length, query_ref, grad_ref, mixed_ref, log_ref, key_ref, value_ref, d_query_ref, d_key_ref, d_value_ref):
    pair = pl.program_id(1)
    scale = HEAD_DIM**-0.5

    @pl.when(pair == 0)
    def start():
        d_key_ref[...] = jnp.zeros_like(d_key_ref)
        d_value_ref[...] = jnp.zeros_like(d_value_ref)

    queries = split_heads(query_ref[0])
    grads = split_heads(grad_ref[0])
    mixes = split_heads(mixed_ref[0])
    lane = lax.broadcasted_iota(jnp.int32, (length, LANES), 1)
    row = lax.broadcasted_iota(jnp.int32, (BLOCK, BLOCK), 0)
    col = lax.broadcasted_iota(jnp.int32, (BLOCK, BLOCK), 1)
    outs = []
    for which in range(2):
        head = 2 * pair + which
        kv = head // GROUP
        log_total = jnp.sum(jnp.where(lane == head, log_ref[0], 0.0), axis=-1, keepdims=True)
        inner = jnp.sum(grads[which] * mixes[which], axis=-1, keepdims=True)
        query = widen(queries[which] * scale, -log_total)
        query_low = queries[which].astype(BF16)
        grad = widen(grads[which], -inner)
        grad_low = grads[which].astype(BF16)
        parts = [None] * (length // BLOCK)
        for index in range(length // BLOCK):
            own = slice(index * BLOCK, (index + 1) * BLOCK)
            keys, values = key_ref[0, kv, own, :], value_ref[0, kv, own, :]
            key_sum = value_sum = None
            for other in range(index, length // BLOCK):
                rows = slice(other * BLOCK, (other + 1) * BLOCK)
                scores = mm(keys, query[rows], NT)
                if other == index:
                    scores = jnp.where(row <= col, scores, -1e30)
                probs = jnp.exp(scores)
                d_scores = (probs * mm(values, grad[rows], NT)).astype(BF16)
                value_part = mm(probs.astype(BF16), grad_low[rows])
                key_part = mm(d_scores, query_low[rows])
                key_sum = key_part if key_sum is None else key_sum + key_part
                value_sum = value_part if value_sum is None else value_sum + value_part
                part = mm(d_scores, keys, TN)
                parts[other] = part if parts[other] is None else parts[other] + part
            d_key_ref[0, kv, own, :] += key_sum * scale
            d_value_ref[0, kv, own, :] += value_sum
        outs.append(parts)
    for index in range(length // BLOCK):
        rows = slice(index * BLOCK, (index + 1) * BLOCK)
        joined = join_heads(outs[0][index], outs[1][index]) * scale
        d_query_ref[0, rows, :] = joined.astype(BF16)


def plain_feed_kernel(
    normed_ref, turned_ref, cot_ref, gate_ref, up_ref, down_ref,
    result_ref, d_normed_ref, gate_grad_ref, up_grad_ref, down_grad_ref,
):
    @pl.when(pl.program_id(0) == 0)
    def start():
        result_ref[...] = jnp.zeros_like(result_ref)
        d_normed_ref[...] = jnp.zeros_like(d_normed_ref)

    normed, cot = normed_ref[...], cot_ref[...]
    gate_weight, up_weight, down_weight = gate_ref[...], up_ref[...], down_ref[...]
    gate = mm(normed, gate_weight)
    up = mm(normed, up_weight)
    d_act = mm(cot, down_weight, NT)
    sigma = jax.nn.sigmoid(gate)
    silu = gate * sigma
    act = (silu * up).astype(BF16)
    d_gate = (d_act * up * sigma * (1.0 + gate * (1.0 - sigma))).astype(BF16)
    d_up = (d_act * silu).astype(BF16)
    result_ref[...] += mm(act, down_weight)
    d_normed_ref[...] += mm(d_gate, gate_weight, NT) + mm(d_up, up_weight, NT)
    turned = turned_ref[...]
    gate_grad_ref[...] = mm(turned, d_gate).astype(gate_grad_ref.dtype)
    up_grad_ref[...] = mm(turned, d_up).astype(up_grad_ref.dtype)
    down_grad_ref[...] = mm(act, cot, TN).astype(down_grad_ref.dtype)


MESH = pl.DeviceIdType.MESH
ANY = pl.BlockSpec(memory_space=pl.ANY)


class Ring:
    def __init__(self, chips):
        self.n = chips
        self.core = lax.rem(lax.axis_index("fsdp"), 2)
        self.chip = lax.div(lax.axis_index("fsdp"), 2)
        self.mine = lax.axis_index("seq")
        side, line = lax.rem(self.chip, 2), lax.div(self.chip, 2)
        self.rank = line * (1 - side) + (chips - 1 - line) * side
        self.right = {"fsdp": 2 * self.chip_at(1) + self.core}
        self.left = {"fsdp": 2 * self.chip_at(-1) + self.core}
        self.partner = {"fsdp": 2 * self.chip + 1 - self.core}
        self.peer = {"seq": 1 - self.mine}

    def chip_at(self, offset):
        rank = lax.rem(self.rank + 2 * self.n + offset, self.n)
        side = lax.div(rank, self.n // 2)
        line = rank * (1 - side) + (self.n - 1 - rank) * side
        return 2 * line + side

    def greet(self, others):
        barrier = pltpu.get_barrier_semaphore()
        for other in others:
            pl.semaphore_signal(barrier, inc=1, device_id=other, device_id_type=MESH)
        pl.semaphore_wait(barrier, len(others))


def remote(src, dst, send, recv, device):
    return pltpu.make_async_remote_copy(
        src_ref=src, dst_ref=dst, send_sem=send, recv_sem=recv, device_id=device, device_id_type=MESH
    )


class Gather:
    def __init__(self, ring, pieces, sems):
        self.ring, self.pieces, self.sems = ring, pieces, sems

    def refs(self, piece, hop):
        direction, own, block = self.pieces[piece][:3]
        dst = block(self.ring.chip_at(-direction * hop))
        return (own if hop == 0 else dst), dst

    def along(self, piece, hop):
        src, dst = self.refs(piece, hop)
        target = self.ring.right if self.pieces[piece][0] > 0 else self.ring.left
        return remote(src, dst, self.sems[0].at[piece, hop], self.sems[1].at[piece, hop], target)

    def mirror(self, piece, hop):
        src, dst = self.refs(piece, hop)
        return remote(src, dst, self.sems[2].at[piece, hop], self.sems[3].at[piece, hop], self.pieces[piece][3])

    def mirrored(self, piece, hop):
        return self.pieces[piece][3] is not None and self.pieces[piece][4] <= hop <= self.pieces[piece][5]

    def advance(self, hop, pieces):
        for piece in pieces:
            reach = self.pieces[piece][5]
            if 0 < hop <= reach:
                self.along(piece, hop - 1).wait_recv()
            if hop < reach:
                self.along(piece, hop).start()
            if self.mirrored(piece, hop):
                self.mirror(piece, hop).start()

    def finish(self):
        for piece in range(len(self.pieces)):
            for hop in range(self.ring.n):
                if hop < self.pieces[piece][5]:
                    self.along(piece, hop).wait_send()
                if self.mirrored(piece, hop):
                    self.mirror(piece, hop).wait()


def gather_sems(pieces):
    return [pltpu.SemaphoreType.DMA((pieces, CHIPS)) for _ in range(4)]


class Reduce:
    def __init__(self, ring, pieces, buffers, sems):
        self.ring, self.pieces, self.buffers, self.sems = ring, pieces, buffers, sems

    def chip(self, piece, hop):
        return self.ring.chip_at(self.pieces[piece][0] * (self.pieces[piece][5] - hop))

    def give(self, piece, hop):
        src = self.pieces[piece][2](self.chip(piece, hop))
        dst = self.buffers[piece][2].at[hop]
        return remote(src, dst, self.sems[2].at[piece, hop], self.sems[3].at[piece, hop], self.pieces[piece][3])

    def along(self, piece, hop):
        send, recv = self.buffers[piece][:2]
        src = self.pieces[piece][1](self.chip(piece, 0)) if hop == 0 and self.alone(piece) else send.at[hop % 2]
        target = self.ring.right if self.pieces[piece][0] > 0 else self.ring.left
        return remote(src, recv.at[hop], self.sems[0].at[piece, hop], self.sems[1].at[piece, hop], target)

    def alone(self, piece):
        return self.pieces[piece][2] is None

    def begin(self):
        self.offer(0, range(len(self.pieces)))

    def given(self, piece, hop):
        reach, kept = self.pieces[piece][5:]
        return not self.alone(piece) and (hop < reach or hop == reach and kept)

    def offer(self, hop, pieces):
        for piece in pieces:
            if self.given(piece, hop):
                self.give(piece, hop).start()

    def advance(self, hop, pieces):
        for piece in pieces:
            reach, kept = self.pieces[piece][5:]
            send, recv, land = self.buffers[piece]
            if not kept and hop == reach + 1:
                self.along(piece, reach - 1).wait_recv()
                self.pieces[piece][4][...] += recv[reach - 1].astype(F32)
            if hop > reach or hop == reach and not kept:
                continue
            self.offer(hop + 1, [piece])
            if hop == 0 and self.alone(piece):
                self.along(piece, 0).start()
                continue
            if 2 <= hop < reach:
                self.along(piece, hop - 2).wait_send()
            addends = [self.pieces[piece][1](self.chip(piece, hop))[...].astype(F32)]
            if self.given(piece, hop):
                self.give(piece, hop).wait_recv()
                addends.append(land[hop].astype(F32))
            if hop > 0:
                self.along(piece, hop - 1).wait_recv()
                addends.append(recv[hop - 1].astype(F32))
            total = functools.reduce(lax.add, addends)
            if hop < reach:
                send[hop % 2] = total.astype(send.dtype)
                self.along(piece, hop).start()
            else:
                self.pieces[piece][4][...] = total

    def finish(self):
        for piece in range(len(self.pieces)):
            reach = self.pieces[piece][5]
            for hop in (reach - 2, reach - 1):
                self.along(piece, hop).wait_send()
            for hop in range(self.ring.n):
                if self.given(piece, hop):
                    self.give(piece, hop).wait_send()


def reduce_scratch(shapes):
    buffers = []
    for rows, columns, shared in shapes:
        buffers += [pltpu.VMEM((2, rows, columns), BF16), pltpu.VMEM((CHIPS - 1, rows, columns), BF16)]
        if shared:
            buffers.append(pltpu.VMEM((CHIPS, rows, columns), BF16))
    return buffers + [pltpu.SemaphoreType.DMA((len(shapes), CHIPS)) for _ in range(4)]


def make_reduce(ring, pieces, scratch):
    scratch = list(scratch)
    buffers = []
    for piece in pieces:
        send, recv = scratch.pop(0), scratch.pop(0)
        buffers.append((send, recv, None if piece[2] is None else scratch.pop(0)))
    return Reduce(ring, pieces, buffers, scratch)


class Share:
    def __init__(self, ring, part, out, scratch):
        self.ring, self.part, self.out = ring, part, out
        self.peer_send, self.peer_recv, self.core_send, self.core_recv, self.sems = scratch
        self.split = len(out.shape) == 4
        self.rows = out.shape[-2]

    def over_seq(self):
        return remote(self.peer_send, self.peer_recv, self.sems.at[0], self.sems.at[1], self.ring.peer)

    def over_core(self):
        return remote(self.core_send, self.core_recv, self.sems.at[2], self.sems.at[3], self.ring.partner)

    def owned(self, core, seq):
        start = (2 * core + seq) * self.rows
        return self.part[start : start + self.rows, :]

    def first(self):
        for mine in range(2):

            @pl.when(self.ring.mine == mine)
            def pick(mine=mine):
                for core in range(2):
                    self.peer_send[core] = self.owned(core, 1 - mine).astype(BF16)

        self.over_seq().start()

    def second(self):
        self.over_seq().wait()
        for mine in range(2):
            for core in range(2):

                @pl.when((self.ring.mine == mine) & (self.ring.core == core))
                def pick(mine=mine, core=core):
                    if self.split:
                        self.out[mine, core] = self.owned(core, mine)
                        self.out[1 - mine, core] = self.peer_recv[core].astype(F32)
                        self.core_send[mine] = self.owned(1 - core, mine).astype(BF16)
                        self.core_send[1 - mine] = self.peer_recv[1 - core]
                    else:
                        self.out[core] = self.owned(core, mine) + self.peer_recv[core].astype(F32)
                        give = self.owned(1 - core, mine) + self.peer_recv[1 - core].astype(F32)
                        self.core_send[0] = give.astype(BF16)

        self.over_core().start()

    def third(self):
        self.over_core().wait()
        if self.split:
            for seq in range(2):
                self.out[seq, 1 - self.ring.core] = self.core_recv[seq].astype(F32)
        else:
            self.out[1 - self.ring.core] = self.core_recv[0].astype(F32)


def share_scratch(rows, columns, split):
    both, last = (2, rows, columns), (2 if split else 1, rows, columns)
    return [
        pltpu.VMEM(both, BF16), pltpu.VMEM(both, BF16), pltpu.VMEM(last, BF16), pltpu.VMEM(last, BF16),
        pltpu.SemaphoreType.DMA((4,)),
    ]


class ShareRows:
    def __init__(self, ring, part, out, scratch):
        self.ring, self.part, self.out = ring, part, out
        self.send, self.recv, self.sems = scratch
        self.rows = out.shape[0]

    def over_seq(self):
        return remote(self.send, self.recv, self.sems.at[0], self.sems.at[1], self.ring.peer)

    def first(self):
        for mine in range(2):

            @pl.when(self.ring.mine == mine)
            def pick(mine=mine):
                start = (1 - mine) * self.rows
                self.send[...] = self.part[start : start + self.rows, :].astype(BF16)

        self.over_seq().start()

    def second(self):
        self.over_seq().wait()
        for mine in range(2):

            @pl.when(self.ring.mine == mine)
            def pick(mine=mine):
                start = mine * self.rows
                self.out[...] = self.part[start : start + self.rows, :] + self.recv[...].astype(F32)


def share_rows_scratch(rows, columns):
    one = (rows, columns)
    return [pltpu.VMEM(one, BF16), pltpu.VMEM(one, BF16), pltpu.SemaphoreType.DMA((2,))]


def spread(points, halves, now):
    plan = [[] for _ in range(points + 1)]
    steps = [(hop, half) for hop in range(CHIPS) for half in halves]
    plan[0] = steps[:now]
    rest = steps[now:]
    for index, step in enumerate(rest):
        plan[-(-(index + 1) * points // len(rest))].append(step)
    return plan


def at_point(step, first, plan, points, which, transfer):
    for place, moves in enumerate(plan[:-1]):
        if moves and place % points == which:

            @pl.when(step == first + place // points)
            def move(moves=moves):
                for hop, pieces in moves:
                    transfer.advance(hop, pieces)


def at_end(plan, transfer):
    for hop, pieces in plan[-1]:
        transfer.advance(hop, pieces)
    transfer.finish()


def rope_tables(positions):
    half = HEAD_DIM // 2
    freqs = THETA ** (-jnp.arange(0, HEAD_DIM, 2).astype(F32) / HEAD_DIM)
    angles = positions.astype(F32)[..., None] * freqs
    cosine, sine = jnp.cos(angles), jnp.sin(angles)
    return jnp.tile(cosine, (1, LANES // half)), jnp.tile(
        jnp.concatenate([-sine, sine], axis=-1), (1, LANES // HEAD_DIM)
    )


def rms_back(values, scale, gain, upstream):
    weighted = upstream * gain
    inner = jnp.mean(weighted * values, axis=-1, keepdims=True)
    grad_in = scale * weighted - values * (scale * scale * scale) * inner
    grad_gain = jnp.sum(upstream * values * scale, axis=0)
    return (grad_in, grad_gain)


def rotate_back(grads, cosine, sine):
    tokens, width = grads.shape
    tiles = grads.reshape(tokens, width // LANES, LANES)
    half = HEAD_DIM // 2
    lane = lax.iota(jnp.int32, LANES)
    ahead = jnp.concatenate([tiles[..., half:], tiles[..., :half]], axis=-1)
    behind = jnp.concatenate([tiles[..., -half:], tiles[..., :-half]], axis=-1)
    other = jnp.where(lane % HEAD_DIM < half, ahead, behind)
    return (tiles * cosine[:, None, :] - other * sine[:, None, :]).reshape(tokens, width)


def full(shape):
    return pl.BlockSpec(shape, lambda *_: (0,) * len(shape))


def plain_shards(
    inputs, positions, qkv_weight, qkv_bias, output_weight, first_gain,
    gate_weight, up_weight, down_weight, second_gain, cotangent,
):
    seqs, half_len, width = inputs.shape
    nseq = lax.axis_size("seq")
    length = half_len * nseq
    whole = seqs // nseq
    tokens = whole * length
    qwidth = HEADS * HEAD_DIM
    kvwidth = KV_HEADS * HEAD_DIM

    def gather(part):
        return lax.all_gather(part, "fsdp", axis=0, tiled=True)

    def to_sequences(part):
        return lax.all_to_all(part, "seq", split_axis=0, concat_axis=1, tiled=True)

    def to_tokens(part):
        return lax.all_to_all(part, "seq", split_axis=1, concat_axis=0, tiled=True)

    def scatter(grad):
        part = lax.psum_scatter(grad.astype(BF16), "fsdp", scatter_dimension=0, tiled=True)
        return lax.psum_scatter(part.astype(F32), "seq", scatter_dimension=0, tiled=True)

    x_low = to_sequences(inputs).reshape(tokens, width)
    places = to_sequences(positions).reshape(tokens)
    cot = to_sequences(cotangent).reshape(tokens, width)
    full_qkv, full_bias, full_output = gather(qkv_weight), gather(qkv_bias), gather(output_weight)
    gain1, gain2 = gather(first_gain), gather(second_gain)
    full_gate, full_up, full_down = gather(gate_weight), gather(up_weight), gather(down_weight)

    cosine, sine = rope_tables(places)
    normed1, query, pair = pl.pallas_call(
        qkv_kernel,
        grid=(tokens // BLOCK,),
        in_specs=[
            pl.BlockSpec((BLOCK, width), lambda i: (i, 0)),
            full((1, width)),
            full((width, qwidth + 2 * kvwidth)),
            full((1, qwidth + 2 * kvwidth)),
            pl.BlockSpec((BLOCK, LANES), lambda i: (i, 0)),
            pl.BlockSpec((BLOCK, LANES), lambda i: (i, 0)),
        ],
        out_specs=[
            pl.BlockSpec((BLOCK, width), lambda i: (i, 0)),
            pl.BlockSpec((BLOCK, qwidth), lambda i: (i, 0)),
            pl.BlockSpec((BLOCK, 2 * kvwidth), lambda i: (i, 0)),
        ],
        out_shape=[
            jax.ShapeDtypeStruct((tokens, width), BF16),
            jax.ShapeDtypeStruct((tokens, qwidth), BF16),
            jax.ShapeDtypeStruct((tokens, 2 * kvwidth), BF16),
        ],
        compiler_params=params(),
    )(x_low, gain1[None], full_qkv, full_bias[None], cosine, sine)

    query = query.reshape(whole, length, qwidth)
    pair = pair.reshape(whole, length, 2, KV_HEADS, HEAD_DIM).transpose(2, 0, 3, 1, 4)
    ones = jnp.ones((2, whole, KV_HEADS, length, 3), BF16)
    pair = jnp.pad(jnp.concatenate([pair, ones], axis=-1), ((0, 0),) * 4 + ((0, HEAD_DIM - 3),))
    keys, values = pair[0], pair[1]
    lanes_spec = pl.BlockSpec((1, length, LANES), lambda b, p: (b, 0, p))
    kv_spec = pl.BlockSpec((1, KV_HEADS, length, LANES), lambda b, p: (b, 0, 0, 0))
    log_spec = pl.BlockSpec((1, length, LANES), lambda b, p: (b, 0, 0))
    mixed, logs = pl.pallas_call(
        functools.partial(attend_kernel, length),
        grid=(whole, PAIRS),
        in_specs=[lanes_spec, kv_spec, kv_spec],
        out_specs=[lanes_spec, log_spec],
        out_shape=[
            jax.ShapeDtypeStruct((whole, length, qwidth), BF16),
            jax.ShapeDtypeStruct((whole, length, LANES), F32),
        ],
        compiler_params=params(),
    )(query, keys, values)

    mixed_tokens = mixed.reshape(tokens, qwidth)
    x = x_low.astype(F32)
    hidden = x + mm(mixed_tokens, full_output)
    gain2 = gain2.astype(F32)
    scale2 = lax.rsqrt(jnp.mean(hidden * hidden, axis=-1, keepdims=True) + EPS)
    normed2 = (hidden * scale2 * gain2).astype(BF16)

    ff = gate_weight.shape[1]
    column = pl.BlockSpec((width, CHUNK), lambda j: (0, j))
    line = pl.BlockSpec((CHUNK, width), lambda j: (j, 0))
    total, d_normed2, gate_grad, up_grad, down_grad = pl.pallas_call(
        plain_feed_kernel,
        grid=(ff // CHUNK,),
        in_specs=[full((tokens, width)), full((width, tokens)), full((tokens, width)), column, column, line],
        out_specs=[full((tokens, width)), full((tokens, width)), column, column, line],
        out_shape=[
            jax.ShapeDtypeStruct((tokens, width), F32),
            jax.ShapeDtypeStruct((tokens, width), F32),
            jax.ShapeDtypeStruct((width, ff), BF16),
            jax.ShapeDtypeStruct((width, ff), BF16),
            jax.ShapeDtypeStruct((ff, width), BF16),
        ],
        compiler_params=params(),
    )(normed2, normed2.T, cot, full_gate, full_up, full_down)

    result = to_tokens((hidden + total).astype(BF16).reshape(whole, length, width))
    back2, second_grad = rms_back(hidden, scale2, gain2, d_normed2)
    d_hidden = cot.astype(F32) + back2
    d_branch = d_hidden.astype(BF16)
    output_grad = mm(mixed_tokens, d_branch, TN)
    d_mixed = mm(d_branch, full_output, NT).astype(BF16).reshape(whole, length, qwidth)

    d_query, d_keys, d_values = pl.pallas_call(
        functools.partial(back_kernel, length),
        grid=(whole, PAIRS),
        in_specs=[lanes_spec, lanes_spec, lanes_spec, log_spec, kv_spec, kv_spec],
        out_specs=[lanes_spec, kv_spec, kv_spec],
        out_shape=[
            jax.ShapeDtypeStruct((whole, length, qwidth), BF16),
            jax.ShapeDtypeStruct((whole, KV_HEADS, length, LANES), F32),
            jax.ShapeDtypeStruct((whole, KV_HEADS, length, LANES), F32),
        ],
        compiler_params=params(),
    )(query, d_mixed, mixed, logs, keys, values)

    def merge(part):
        part = part[..., :HEAD_DIM].astype(BF16)
        return part.transpose(0, 2, 1, 3).reshape(tokens, kvwidth)

    turned = jnp.concatenate([d_query.reshape(tokens, qwidth), merge(d_keys)], axis=-1).astype(F32)
    turned = rotate_back(turned, cosine, sine).astype(BF16)
    d_pre = jnp.concatenate([turned, merge(d_values)], axis=-1)
    qkv_grad = mm(normed1, d_pre, TN)
    bias_grad = jnp.sum(d_pre.astype(F32), axis=0)
    d_normed1 = mm(d_pre, full_qkv, NT)
    scale1 = lax.rsqrt(jnp.mean(x * x, axis=-1, keepdims=True) + EPS)
    back1, first_grad = rms_back(x, scale1, gain1.astype(F32), d_normed1)
    input_grad = (d_hidden + back1).astype(BF16).reshape(whole, length, width)
    input_grad = to_tokens(input_grad).astype(F32)

    def scatter_small(grad):
        return lax.psum_scatter(grad, ("fsdp", "seq"), scatter_dimension=0, tiled=True)

    return (
        result,
        input_grad,
        scatter(qkv_grad),
        scatter_small(bias_grad),
        scatter(output_grad),
        scatter_small(first_grad),
        scatter(gate_grad),
        scatter(up_grad),
        scatter(down_grad),
        scatter_small(second_grad),
    )


CHIPS = 8
OWNERS = 4
SPLITS = (64, 88)
STARTS = (0, 64)
BITS = 16
QUARTER = 512
BOTH = 1024


def inside(shape):
    return pl.BlockSpec(shape, lambda *_: (0,) * len(shape), pipeline_mode=pl.Buffered(1))


def dma(*shape):
    return pltpu.SemaphoreType.DMA(shape)


def spans():
    return [2 * CHIPS * split for split in SPLITS]


def stack_rows(first, second):
    return jnp.concatenate([first.astype(F32), second.astype(F32)], axis=0)


def owner_columns(core, group):
    own = sum(SPLITS)
    starts = [OWNERS * own * chip + 2 * own * core + own * seq for chip in range(CHIPS) for seq in range(2)]
    return [(start + STARTS[group], SPLITS[group]) for start in starts]


def gather_columns(source, core, group):
    return jnp.concatenate([source[:, a : a + count] for a, count in owner_columns(core, group)], axis=1)


def spread_columns(sources):
    parts = []
    for chip in range(CHIPS):
        for core in range(2):
            for section in range(2 * chip, 2 * chip + 2):
                for group, split in enumerate(SPLITS):
                    parts.append(sources[group][core][:, section * split : (section + 1) * split])
    return jnp.concatenate(parts, axis=1)


def project(length, x_ref, table_ref, vectors_ref, weight_ref, turned_ref, query_ref, key_ref, value_ref):
    width = x_ref.shape[2]
    qwidth = HEADS * HEAD_DIM
    lane = lax.broadcasted_iota(jnp.int32, (BLOCK, LANES), 1)
    extra = (lane >= HEAD_DIM) & (lane < HEAD_DIM + 3)
    bias, gain = vectors_ref[0:1, :], vectors_ref[1:2, :width]
    early = weight_ref[0].reshape(width, BOTH)
    late = weight_ref[1, :, :, : qwidth + 2 * LANES - BOTH].reshape(width, qwidth + 2 * LANES - BOTH)
    for index in range(length // BLOCK):
        rows = slice(index * BLOCK, (index + 1) * BLOCK)
        half, start = index * BLOCK // (length // 2), index * BLOCK % (length // 2)
        x = x_ref[half, start : start + BLOCK, :].astype(F32)
        scale = lax.rsqrt(jnp.mean(x * x, axis=-1, keepdims=True) + EPS)
        normed = (x * scale * gain).astype(BF16)
        turned_ref[:, rows] = normed.T
        pre = mm(normed, early) + bias[:, :BOTH]
        values = mm(normed, late) + bias[:, BOTH:]
        cosine, sine = tables(table_ref[half, start : start + BLOCK, :])
        for tile in range(PAIRS):
            columns = slice(tile * LANES, (tile + 1) * LANES)
            part = pre[:, columns]
            query_ref[rows, columns] = (part * cosine + swap_halves(part) * sine).astype(BF16)
        part = pre[:, qwidth : qwidth + LANES]
        part = part * cosine + swap_halves(part) * sine
        for ref, both in ((key_ref, part), (value_ref, values)):
            for kv, head in enumerate(split_heads(both)):
                ref[kv, rows, :] = jnp.where(extra, 1.0, head).astype(BF16)


def tables(packed):
    lane = lax.broadcasted_iota(jnp.int32, packed.shape, 1)
    turned = pltpu.roll(packed, HEAD_DIM, 1)
    low = lane < HEAD_DIM
    return jnp.where(low, packed, turned), jnp.where(low, turned, packed)


def attend_pair(pair, length, query_ref, key_ref, value_ref, mixed_ref, log_ref):
    scale = HEAD_DIM**-0.5
    columns = pl.ds(pl.multiple_of(pair * LANES, LANES), LANES)
    heads = [part.astype(BF16) for part in split_heads(query_ref[:, columns])]
    lane = lax.broadcasted_iota(jnp.int32, (BLOCK, LANES), 1)
    row = lax.broadcasted_iota(jnp.int32, (BLOCK, BLOCK), 0)
    col = lax.broadcasted_iota(jnp.int32, (BLOCK, BLOCK), 1)
    for index in range(length // BLOCK):
        rows = slice(index * BLOCK, (index + 1) * BLOCK)
        seen = index * BLOCK
        outs = []
        for which in range(2):
            head = 2 * pair + which
            kv = head // GROUP
            query = heads[which][rows]
            diagonal = mm(query, key_ref[kv, rows, :], NT) * scale
            diagonal = jnp.where(row >= col, diagonal, -1e30)
            top = jnp.max(diagonal, axis=-1, keepdims=True)
            if seen:
                before = mm(query, key_ref[kv, :seen, :], NT) * scale
                top = jnp.maximum(top, jnp.max(before, axis=-1, keepdims=True))
            probs = jnp.exp(diagonal - top).astype(BF16)
            mixed = mm(probs, value_ref[kv, rows, :])
            if seen:
                probs = jnp.exp(before - top).astype(BF16)
                mixed = mixed + mm(probs, value_ref[kv, :seen, :])
            total = mixed[:, HEAD_DIM : HEAD_DIM + 1]
            outs.append(mixed / total)
            log_ref[rows, :] = jnp.where(lane == head, top + jnp.log(total), log_ref[rows, :])
        mixed_ref[rows, columns] = join_heads(outs[0], outs[1]).astype(BF16)


def settle(length, x_ref, mixed_ref, weight_ref, vectors_ref, hidden_ref, normed_ref, turned_ref):
    width = x_ref.shape[2]
    gain = vectors_ref[2:3, :width]
    weight = weight_ref[1, :, :, BOTH - width :].reshape(width, width)
    for index in range(length // BLOCK):
        rows = slice(index * BLOCK, (index + 1) * BLOCK)
        half, start = index * BLOCK // (length // 2), index * BLOCK % (length // 2)
        hidden = x_ref[half, start : start + BLOCK, :].astype(F32) + mm(mixed_ref[rows, :], weight)
        hidden_ref[rows, :] = hidden
        scale = lax.rsqrt(jnp.mean(hidden * hidden, axis=-1, keepdims=True) + EPS)
        normed = (hidden * scale * gain).astype(BF16)
        normed_ref[rows, :] = normed
        turned_ref[:, rows] = normed.T


HALVES = ((0, 1), (2, 3))
WAYS = ((1, CHIPS // 2), (-1, CHIPS - 1 - CHIPS // 2))


def row_cuts(rows):
    early = rows // 2 // 16 * 16 if rows == 112 else 80
    return (0, early), (early, rows - early)


def feed_gather(ring, own_wide, own_down, wide, down, sems):
    rows, count = own_wide.shape[1], own_down.shape[0]
    pieces = []
    for (start, some), (down_start, down_some) in zip(row_cuts(rows), row_cuts(count)):

        def down_block(chip, start=down_start, some=down_some):
            return down.at[pl.ds(pl.multiple_of(chip * count + start, 16), some), :]

        def wide_block(chip, start=start, some=some):
            return wide.at[ring.mine, chip, pl.ds(start, some), :]

        pieces.append((1, own_down.at[pl.ds(down_start, down_some), :], down_block, None, 0, CHIPS - 1))
        pieces.append((-1, own_wide.at[ring.mine, pl.ds(start, some), :], wide_block, ring.peer, 1, CHIPS - 1))
    return Gather(ring, pieces, sems)


def feed_keep(ring, own_wide, own_down, wide, down, sems):
    count = own_down.shape[0]
    rows = pl.ds(pl.multiple_of(ring.chip * count, 16), count)
    return [
        pltpu.make_async_copy(own_wide, wide.at[:, ring.chip], sems.at[0]),
        pltpu.make_async_copy(own_down, down.at[rows, :], sems.at[1]),
    ]


def feed_reduce(ring, wide, down, wide_part, down_part, scratch):
    rows, count = wide_part.shape[0], down_part.shape[0]
    pieces = []
    for (start, some), (down_start, down_some) in zip(row_cuts(rows), row_cuts(count)):

        def down_block(chip, start=down_start, some=down_some):
            return down.at[pl.ds(pl.multiple_of(chip * count + start, 16), some), :]

        def own_block(chip, start=start, some=some):
            return wide.at[ring.mine, chip, pl.ds(start, some), :]

        def other_block(chip, start=start, some=some):
            return wide.at[1 - ring.mine, chip, pl.ds(start, some), :]

        down_out = down_part.at[pl.ds(down_start, down_some), :]
        pieces.append((1, down_block, None, None, down_out, CHIPS - 1, True))
        pieces.append((
            -1, own_block, other_block, ring.peer, wide_part.at[pl.ds(start, some), :], CHIPS - 1, True
        ))
    return make_reduce(ring, pieces, scratch)


def feed_reduce_scratch(rows, span, count, width):
    shapes = []
    for (_, some), (_, down_some) in zip(row_cuts(rows), row_cuts(count)):
        shapes += [(down_some, width, False), (some, span, True)]
    return reduce_scratch(shapes)


def first_kernel(
    length, plan,
    x_in, table_in, both_in, small_in, gate_in, up_in, down_in, cot_in,
    x_out, table_out, weight_out, turned1_out, query_out, key_out, value_out,
    vectors_ref, mixed_ref, log_ref, hidden_ref, own_wide2, own_down2,
    cot_out, wide_out, down_out, normed_out, turned_out,
    x_ref, table_ref, weight_ref, turned1_ref, query_ref, key_ref, value_ref,
    normed_ref, turned_ref, both_land, small_land, both_own, small_own, small_all, perm_ref, wide_land, own_wide1, own_down1,
    swap_sems, core_sems, keep_sems, cot_sems, store_sems, *sems,
):
    step = pl.program_id(0)
    ring = Ring(CHIPS)
    core, mine = ring.core, ring.mine
    gather = feed_gather(ring, own_wide1, own_down1, wide_out, down_out, sems[:4])
    keeps = feed_keep(ring, own_wide1, own_down1, wide_out, down_out, keep_sems)
    early = BOTH // 2
    pieces = []
    for start in (0, early):
        part = pl.ds(start, early)
        for direction, reach in WAYS:
            pieces.append((
                direction, both_own.at[:, part], lambda chip, part=part: weight_ref.at[core, chip, :, part],
                ring.partner, 0 if direction > 0 else 1, reach,
            ))
    for direction, reach in WAYS:
        pieces.append((direction, small_own, lambda chip: small_all.at[chip], None, 0, reach))
    attention = Gather(ring, pieces, sems[4:])
    every = range(len(pieces))
    swaps = [
        remote(src.at[1 - mine], dst.at[mine], swap_sems.at[2 * k], swap_sems.at[2 * k + 1], ring.peer)
        for k, (src, dst) in enumerate([(x_in, x_ref), (table_in, table_ref), (cot_in, cot_out.at[core])])
    ]
    trades = [
        remote(src, dst, core_sems.at[2 * k], core_sems.at[2 * k + 1], ring.partner)
        for k, (src, dst) in enumerate([
            (both_in.at[1 - core], both_land), (small_in, small_land), (perm_ref.at[1 - core], wide_land),
            (cot_out.at[core], cot_out.at[core]), (normed_ref, normed_out.at[core]),
            (turned_ref, turned_out.at[core]),
        ])
    ]
    cot_keep = pltpu.make_async_copy(cot_in.at[mine], cot_out.at[core, mine], cot_sems.at[0])
    stores = [
        pltpu.make_async_copy(src, dst, store_sems.at[k])
        for k, (src, dst) in enumerate([
            (x_ref, x_out), (table_ref, table_out), (weight_ref, weight_out), (turned1_ref, turned1_out),
            (query_ref, query_out), (key_ref, key_out), (value_ref, value_out),
            (normed_ref, normed_out.at[core]), (turned_ref, turned_out.at[core]),
        ])
    ]

    @pl.when(step == 0)
    def enter():
        ring.greet([ring.right, ring.left, ring.partner, ring.peer])
        trades[0].start()
        trades[1].start()
        for swap in swaps:
            swap.start()
        cot_keep.start()
        x_ref[mine] = x_in[mine]
        table_ref[mine] = table_in[mine]
        trades[0].wait()
        trades[1].wait()
        half = small_in.shape[0]
        rows = both_in.shape[1]
        for which in range(2):

            @pl.when(core == which)
            def own(which=which):
                pair = (both_in[which], both_land[...])
                both_own[...] = stack_rows(*pair[:: 1 - 2 * which]).astype(BF16)
                pair = (small_in[...], small_land[...])[:: 1 - 2 * which]
                lane = lax.broadcasted_iota(jnp.int32, (2 * half, LANES), 1)
                gains = stack_rows(pair[0][:rows], pair[1][:rows])
                gains = jnp.concatenate([gains, jnp.zeros((2 * (half - rows), LANES), F32)], axis=0)
                small_own[...] = jnp.where(lane == 0, stack_rows(*pair), gains).astype(BF16)

        attention.advance(0, every)
        weight_ref[core, ring.chip] = both_own[...]
        small_all[ring.chip] = small_own[...]
        wide = stack_rows(gate_in[...], up_in[...])
        for side in range(2):
            for group, span in enumerate(spans()):
                first = group * spans()[0]
                part = gather_columns(wide, side, group).astype(BF16)
                perm_ref[side, 0, :, first : first + span] = part[:rows]
                perm_ref[side, 1, :, first : first + span] = part[rows:]
        trades[2].start()
        own = sum(SPLITS)
        for group, ref in enumerate((own_down1, own_down2)):
            start, count = STARTS[group], SPLITS[group]
            ref[...] = stack_rows(
                down_in[start : start + count, :], down_in[own + start : own + start + count, :]
            ).astype(BF16)
        attention.advance(1, every)
        trades[2].wait()
        for which in range(2):

            @pl.when(core == which)
            def chip_rows(which=which):
                for tensor in range(2):
                    pair = (perm_ref[which, tensor], wide_land[tensor])
                    block = stack_rows(*pair[:: 1 - 2 * which]).astype(BF16)
                    own_wide1[tensor] = block[:, : spans()[0]]
                    own_wide2[tensor] = block[:, spans()[0] :]

        gather.advance(0, (0, 1, 2, 3))
        for keep in keeps:
            keep.start()
        for hop in range(2, WAYS[0][1] + 1):
            attention.advance(hop, every)
            if hop == 3:
                gather.advance(1, HALVES[0])
        gather.advance(1, HALVES[1])
        attention.finish()
        rows = small_all.shape[1]
        turned = small_all[...].astype(F32).reshape(CHIPS * rows, LANES).T
        vectors_ref[0:1, :] = turned[0:1, :]
        width = x_in.shape[2]
        chip_rows = width // CHIPS
        turned = small_all[:, :chip_rows, :].astype(F32).reshape(width, LANES).T
        vectors_ref[1:3, :width] = turned[1:3, :]
        swaps[0].wait()
        swaps[1].wait()
        project(length, x_ref, table_ref, vectors_ref, weight_ref, turned1_ref, query_ref, key_ref, value_ref)
        for store in stores[:-2]:
            store.start()
        log_ref[...] = jnp.zeros_like(log_ref)

    at_point(step, 1, plan, 1, 0, gather)

    @pl.when((step >= 1) & (step <= PAIRS))
    def pairs():
        attend_pair(step - 1, length, query_ref, key_ref, value_ref, mixed_ref, log_ref)

    @pl.when(step == 4)
    def cotangent():
        swaps[2].wait()
        cot_keep.wait()
        trades[3].start()

    @pl.when(step == PAIRS + 1)
    def last():
        settle(length, x_ref, mixed_ref, weight_ref, vectors_ref, hidden_ref, normed_ref, turned_ref)
        for copy in trades[4:] + stores[-2:]:
            copy.start()
        at_end(plan, gather)
        for copy in keeps + trades[3:] + stores:
            copy.wait()


def first_part(x, table, both, small, gate, up, down, cot):
    _, half, width = x.shape
    tokens = 2 * half
    rows, ff = gate.shape
    one, two = spans()
    down_rows = [2 * split for split in SPLITS]
    stored = [
        (x.shape, BF16), (table.shape, F32), ((2, CHIPS, 2 * rows, BOTH), BF16), ((width, tokens), BF16),
        ((tokens, width), BF16), ((KV_HEADS, tokens, LANES), BF16), ((KV_HEADS, tokens, LANES), BF16),
    ]
    kept = [
        ((8, 2 * CHIPS * small.shape[0]), F32), ((tokens, width), BF16), ((tokens, LANES), F32),
        ((tokens, width), F32),
        ((2, 2 * rows, two), BF16), ((down_rows[1], width), BF16),
    ]
    far = [
        ((2,) + cot.shape, BF16), ((2, CHIPS, 2 * rows, one), BF16), ((CHIPS * down_rows[0], width), BF16),
        ((2, tokens, width), BF16), ((2, width, tokens), BF16),
    ]
    ins = [x, table, both, small, gate, up, down]
    steps = [(hop, half) for hop in range(2, CHIPS) for half in HALVES]
    points = PAIRS + 1
    plan = [[] for _ in range(points + 1)]
    for index, move in enumerate(steps):
        plan[-(-(index + 1) * points // len(steps))].append(move)
    return pl.pallas_call(
        functools.partial(first_kernel, tokens, plan),
        grid=(PAIRS + 2,),
        in_specs=[inside(part.shape) for part in ins] + [ANY],
        out_specs=[ANY] * len(stored) + [inside(shape) for shape, _ in kept] + [ANY] * len(far),
        out_shape=[jax.ShapeDtypeStruct(shape, kind) for shape, kind in stored + kept + far],
        scratch_shapes=[pltpu.VMEM(shape, kind) for shape, kind in stored]
        + [
            pltpu.VMEM((tokens, width), BF16), pltpu.VMEM((width, tokens), BF16),
            pltpu.VMEM(both.shape[1:], BF16), pltpu.VMEM(small.shape, BF16),
            pltpu.VMEM((2 * rows, BOTH), BF16), pltpu.VMEM((2 * small.shape[0], LANES), BF16),
            pltpu.VMEM((CHIPS, 2 * small.shape[0], LANES), BF16),
            pltpu.VMEM((2, 2, rows, one + two), BF16), pltpu.VMEM((2, rows, one + two), BF16),
            pltpu.VMEM((2, 2 * rows, one), BF16), pltpu.VMEM((down_rows[0], width), BF16),
            dma(6), dma(12), dma(2), dma(1), dma(len(stored) + 2),
        ]
        + gather_sems(4)
        + gather_sems(6),
        compiler_params=pltpu.CompilerParams(
            collective_id=0, has_side_effects=True, vmem_limit_bytes=VMEM_LIMIT
        ),
    )(*ins, cot)


def feed_chunk(count, offset, normed_ref, turned_ref, cot_ref, wide, down, result_ref, d_normed_ref, work, pause):
    width = normed_ref.shape[2]
    columns = pl.ds(offset, count)
    gate_weight = wide[0, :, :, columns].reshape(width, count)
    up_weight = wide[1, :, :, columns].reshape(width, count)
    down_weight = down[columns, :]
    act_at, gate_at, up_at = (slice(k * CHUNK, k * CHUNK + count) for k in range(3))
    parts = normed_ref.shape[1] // QUARTER
    for part in range(2 * parts):
        core, rows = part // parts, slice(part % parts * QUARTER, (part % parts + 1) * QUARTER)
        normed, cot = normed_ref[core, rows, :], cot_ref[core, rows, :]
        gate = mm(normed, gate_weight)
        up = mm(normed, up_weight)
        d_act = mm(cot, down_weight, NT)
        sigma = jax.nn.sigmoid(gate)
        silu = gate * sigma
        act = (silu * up).astype(BF16)
        d_gate = (d_act * up * sigma * (1.0 + gate * (1.0 - sigma))).astype(BF16)
        d_up = (d_act * silu).astype(BF16)
        work[core, rows, act_at], work[core, rows, gate_at], work[core, rows, up_at] = act, d_gate, d_up
        result_ref[core, rows, :] += mm(act, down_weight)
        d_normed_ref[core, rows, :] += mm(d_gate, gate_weight, NT) + mm(d_up, up_weight, NT)
        if part + 1 == parts:
            pause(1)
    pause(2)
    for tensor, at in ((0, gate_at), (1, up_at)):
        grad = mm(turned_ref[0], work[0, :, at]) + mm(turned_ref[1], work[1, :, at])
        wide[tensor, :, :, columns] = grad.astype(BF16).reshape(wide.shape[1], wide.shape[2], count)
    grad = mm(work[0, :, act_at], cot_ref[0], TN) + mm(work[1, :, act_at], cot_ref[1], TN)
    down[columns, :] = grad.astype(BF16)


def feed_kernel(
    gather_plan, reduce_plan,
    normed_ref, turned_ref, cot_ref, hidden_in, wide_in, down_in, own_wide, own_down,
    result_out, d_normed_out, other_out, wide_out, down_out, wide_part, down_part,
    result_ref, d_normed_ref, work, wide1, down1, wide2, down2,
    load_sems, keep_sems, trade_sems, store_sems, *scratch,
):
    step = pl.program_id(0)
    ring = Ring(CHIPS)
    core = ring.core
    gather = feed_gather(ring, own_wide, own_down, wide2, down2, scratch[:4])
    keeps = feed_keep(ring, own_wide, own_down, wide2, down2, keep_sems)
    reduce = feed_reduce(ring, wide1, down1, wide_part, down_part, scratch[4:])
    loads = [
        pltpu.make_async_copy(src, dst, load_sems.at[k])
        for k, (src, dst) in enumerate([(wide_in, wide1), (down_in, down1), (hidden_in, result_ref.at[core])])
    ]
    trades = [
        remote(work.at[k], other_out.at[k], trade_sems.at[2 * k], trade_sems.at[2 * k + 1], ring.partner)
        for k in range(2)
    ]
    stores = [
        pltpu.make_async_copy(src, dst, store_sems.at[k])
        for k, (src, dst) in enumerate([
            (wide2, wide_out), (down2, down_out), (result_ref.at[core], result_out),
            (d_normed_ref.at[core], d_normed_out),
        ])
    ]
    one, two = wide1.shape[3], wide2.shape[3]
    turns, last = one // CHUNK, one // CHUNK + -(-two // CHUNK) - 1

    @pl.when(step == 0)
    def begin():
        for load in loads:
            load.start()
        ring.greet([ring.right, ring.left, ring.partner, ring.peer])

    at_point(step, 0, gather_plan, 3, 0, gather)

    @pl.when(step == 0)
    def start():
        for keep in keeps:
            keep.start()
        result_ref[1 - core] = jnp.zeros(result_ref.shape[1:], F32)
        d_normed_ref[...] = jnp.zeros_like(d_normed_ref)
        for load in loads:
            load.wait()

    def chunk(count, offset, wide, down, first, plan, transfer):
        feed_chunk(
            count, offset, normed_ref, turned_ref, cot_ref, wide, down, result_ref, d_normed_ref, work,
            lambda which: at_point(step, first, plan, 3, which, transfer),
        )

    @pl.when(step < turns)
    def first_group():
        chunk(CHUNK, pl.multiple_of(step * CHUNK, CHUNK), wide1, down1, 0, gather_plan, gather)

    @pl.when(step == turns - 1)
    def between():
        at_end(gather_plan, gather)
        for keep in keeps:
            keep.wait()
        reduce.begin()

    at_point(step, turns, reduce_plan, 3, 0, reduce)

    @pl.when((step >= turns) & (step < last))
    def second_group():
        chunk(CHUNK, pl.multiple_of((step - turns) * CHUNK, CHUNK), wide2, down2, turns, reduce_plan, reduce)

    @pl.when(step == last)
    def end():
        done = (last - turns) * CHUNK
        chunk(two - done, done, wide2, down2, turns, reduce_plan, reduce)
        for store in stores:
            store.start()
        work[0] = result_ref[1 - core].astype(BF16)
        trades[0].start()
        work[1] = d_normed_ref[1 - core].astype(BF16)
        trades[1].start()
        at_end(reduce_plan, reduce)
        for copy in trades + stores:
            copy.wait()


def feed(normed, turned, cot, hidden, wide, down, own_wide, own_down):
    _, tokens, width = normed.shape
    one, two = wide.shape[3], own_wide.shape[2]
    rows = own_wide.shape[1]
    counts = [2 * split for split in SPLITS]
    turns, more = one // CHUNK, -(-two // CHUNK)
    wide_two, down_two = (2, CHIPS, rows, two), (CHIPS * counts[1], width)
    whole, halves = (tokens, width), (2, tokens, width)
    far = [(whole, F32), (whole, F32), (halves, BF16), (wide_two, BF16), (down_two, BF16)]
    near = [((rows, one), F32), ((counts[0], width), F32)]
    return pl.pallas_call(
        functools.partial(
            feed_kernel, spread(3 * turns, HALVES, len(HALVES)), spread(3 * more, HALVES, 0)
        ),
        grid=(turns + more,),
        in_specs=[inside(part.shape) for part in (normed, turned, cot)] + [ANY] * 5,
        out_specs=[ANY] * len(far) + [inside(shape) for shape, _ in near],
        out_shape=[jax.ShapeDtypeStruct(shape, kind) for shape, kind in far + near],
        scratch_shapes=[
            pltpu.VMEM(halves, F32), pltpu.VMEM(halves, F32), pltpu.VMEM(halves, BF16),
            pltpu.VMEM(wide.shape, BF16), pltpu.VMEM(down.shape, BF16),
            pltpu.VMEM(wide_two, BF16), pltpu.VMEM(down_two, BF16),
            dma(3), dma(2), dma(4), dma(4),
        ]
        + gather_sems(4)
        + feed_reduce_scratch(rows, one, counts[0], width),
        compiler_params=pltpu.CompilerParams(
            collective_id=1, has_side_effects=True, vmem_limit_bytes=VMEM_LIMIT
        ),
    )(normed, turned, cot, hidden, wide, down, own_wide, own_down)


def unsettle(
    rows, first, hidden_ref, d_own_ref, other_ref, own_ref, cot_ref, vectors_ref, mixed_ref, weight_ref,
    d_hidden_ref, d_mixed_ref, output_grad_ref, second_ref, result_ref, place,
):
    width = hidden_ref.shape[1]
    gain = vectors_ref[2:3, :width]
    weight = weight_ref[0, :, BOTH - width :]
    hidden = hidden_ref[...]
    upstream = d_own_ref[...] + other_ref[1].astype(F32)
    scale = lax.rsqrt(jnp.mean(hidden * hidden, axis=-1, keepdims=True) + EPS)
    weighted = upstream * gain
    inner = jnp.mean(weighted * hidden, axis=-1, keepdims=True)
    d_hidden = cot_ref[rows, :].astype(F32) + scale * weighted - hidden * (scale * scale * scale * inner)
    d_hidden_ref[rows, :] = d_hidden
    result_ref[place] = (own_ref[...] + other_ref[0].astype(F32)).astype(BF16)
    branch = d_hidden.astype(BF16)
    d_mixed_ref[rows, :] = mm(branch, weight, NT).astype(BF16)
    grad = mm(mixed_ref[rows, :], branch, TN)
    part = jnp.sum(upstream * hidden * scale, axis=0, keepdims=True)

    @pl.when(first)
    def begin():
        second_ref[...] = part
        output_grad_ref[...] = grad

    @pl.when(jnp.logical_not(first))
    def more():
        second_ref[...] += part
        output_grad_ref[...] += grad


def back_head(pair, which, length, query_ref, grad_ref, mixed_ref, log_ref, key_ref, value_ref, d_key_ref, d_value_ref):
    scale = HEAD_DIM**-0.5
    columns = pl.ds(pl.multiple_of(pair * LANES, LANES), LANES)
    query, grad, mixed = (split_heads(ref[:, columns])[which] for ref in (query_ref, grad_ref, mixed_ref))
    lane = lax.broadcasted_iota(jnp.int32, (length, LANES), 1)
    row = lax.broadcasted_iota(jnp.int32, (BLOCK, BLOCK), 0)
    col = lax.broadcasted_iota(jnp.int32, (BLOCK, BLOCK), 1)
    head = 2 * pair + which
    kv = head // GROUP
    log_total = jnp.sum(jnp.where(lane == head, log_ref[...], 0.0), axis=-1, keepdims=True)
    inner = jnp.sum(grad * mixed, axis=-1, keepdims=True)
    query_low, grad_low = query.astype(BF16), grad.astype(BF16)
    query, grad = widen(query * scale, -log_total), widen(grad, -inner)
    parts = [None] * (length // BLOCK)
    for index in range(length // BLOCK):
        own = slice(index * BLOCK, (index + 1) * BLOCK)
        keys, values = key_ref[kv, own, :], value_ref[kv, own, :]
        key_sum = value_sum = None
        for other in range(index, length // BLOCK):
            rows = slice(other * BLOCK, (other + 1) * BLOCK)
            scores = mm(keys, query[rows], NT)
            if other == index:
                scores = jnp.where(row <= col, scores, -1e30)
            probs = jnp.exp(scores)
            d_scores = (probs * mm(values, grad[rows], NT)).astype(BF16)
            value_part = mm(probs.astype(BF16), grad_low[rows])
            key_part = mm(d_scores, query_low[rows])
            key_sum = key_part if key_sum is None else key_sum + key_part
            value_sum = value_part if value_sum is None else value_sum + value_part
            part = mm(d_scores, keys, TN)
            parts[other] = part if parts[other] is None else parts[other] + part
        d_key_ref[kv, own, :] += key_sum * scale
        d_value_ref[kv, own, :] += value_sum
    return parts


def back_kernel_all(
    length, plan,
    hidden_ref, d_own_ref, other_ref, own_ref,
    vectors_ref, weight_ref, mixed_ref, query_ref, log_ref, key_ref, value_ref, wide_before, down_before,
    wide_ref, down_ref, cot_in,
    d_hidden_ref, output_grad_out, second_ref, d_query_ref, d_key_ref, d_value_ref,
    wide_own, down_own, wide_part, down_part, result_ref,
    d_mixed_ref, cot_ref, output_grad_ref, half_ref, load_sem, *scratch,
):
    step = pl.program_id(0)
    ring = Ring(CHIPS)
    share = Share(ring, wide_before, wide_own, scratch[:5])
    share_rows = ShareRows(ring, down_before, down_own, scratch[5:8])
    reduce = feed_reduce(ring, wide_ref, down_ref, wide_part, down_part, scratch[8:])
    load = pltpu.make_async_copy(cot_in.at[ring.core], cot_ref, load_sem.at[0])
    blocks = length // BLOCK

    @pl.when(step == 0)
    def begin():
        load.start()
        ring.greet([ring.right, ring.left, ring.partner, ring.peer])
        reduce.begin()
        share.first()
        share_rows.first()
        d_key_ref[...] = jnp.zeros_like(d_key_ref)
        d_value_ref[...] = jnp.zeros_like(d_value_ref)
        load.wait()

    at_point(step, 0, plan, 2, 0, reduce)

    @pl.when(step < blocks)
    def norms():
        rows = pl.ds(pl.multiple_of(step * BLOCK, BLOCK), BLOCK)
        halves = length // 2 // BLOCK
        place = (lax.div(step, halves), pl.ds(pl.multiple_of(lax.rem(step, halves) * BLOCK, BLOCK), BLOCK))
        unsettle(
            rows, step == 0, hidden_ref, d_own_ref, other_ref, own_ref, cot_ref, vectors_ref, mixed_ref, weight_ref,
            d_hidden_ref, d_mixed_ref, output_grad_ref, second_ref, result_ref, place,
        )

    @pl.when(step == blocks - 1)
    def after():
        output_grad_out[...] = output_grad_ref[...].astype(BF16)
        share.second()
        share_rows.second()

    refs = (query_ref, d_mixed_ref, mixed_ref, log_ref, key_ref, value_ref, d_key_ref, d_value_ref)

    @pl.when(step >= blocks)
    def first_head():
        parts = back_head(step - blocks, 0, length, *refs)
        for index, part in enumerate(parts):
            half_ref[index * BLOCK : (index + 1) * BLOCK, :] = part

    at_point(step, 0, plan, 2, 1, reduce)

    @pl.when(step >= blocks)
    def second_head():
        scale = HEAD_DIM**-0.5
        columns = pl.ds(pl.multiple_of((step - blocks) * LANES, LANES), LANES)
        parts = back_head(step - blocks, 1, length, *refs)
        for index, part in enumerate(parts):
            rows = slice(index * BLOCK, (index + 1) * BLOCK)
            d_query_ref[rows, columns] = (join_heads(half_ref[rows, :], part) * scale).astype(BF16)

    @pl.when(step == blocks + PAIRS - 1)
    def last():
        at_end(plan, reduce)
        share.third()


def back_all(
    hidden, d_own, other, own, vectors, weight, mixed, query, logs, keys, values, wide_before, down_before,
    wide, down, cot,
):
    tokens, width = hidden.shape
    rows, before = wide_before.shape
    span = wide.shape[3]
    counts = [2 * split for split in SPLITS]
    blocks = tokens // BLOCK

    def block(step):
        return jnp.minimum(step, blocks - 1)

    line = pl.BlockSpec((BLOCK, width), lambda s: (block(s), 0))
    pair = pl.BlockSpec((2, BLOCK, width), lambda s: (0, block(s), 0))
    late = pl.BlockSpec((1, width, BOTH), lambda s: (1, 0, 0), pipeline_mode=pl.Buffered(1))
    ins = [mixed, query, logs, keys, values, wide_before, down_before, wide, down]
    outs = [
        ((tokens, width), F32), ((width, width), BF16), ((1, width), F32), (query.shape, BF16),
        (keys.shape, F32), (values.shape, F32),
        ((2, 2, rows // OWNERS, before), F32), ((counts[0] // 2, width), F32),
        ((rows, span), F32), ((counts[1], width), F32), ((2, tokens // 2, width), BF16),
    ]
    moves = [(hop, half) for hop in range(CHIPS) for half in HALVES]
    plan = [[] for _ in range(2 * (blocks + PAIRS) + 1)]
    for place, move in zip([2 * blocks - 4, 2 * blocks - 2] + list(range(2 * blocks, len(plan) - 1)), moves):
        plan[place].append(move)
    return pl.pallas_call(
        functools.partial(back_kernel_all, tokens, plan),
        grid=(blocks + PAIRS,),
        in_specs=[line, line, pair, line, inside(vectors.shape), late]
        + [inside(part.shape) for part in ins]
        + [ANY],
        out_specs=[inside(shape) for shape, _ in outs],
        out_shape=[jax.ShapeDtypeStruct(shape, kind) for shape, kind in outs],
        scratch_shapes=[
            pltpu.VMEM((tokens, width), BF16), pltpu.VMEM((tokens, width), BF16),
            pltpu.VMEM((width, width), F32), pltpu.VMEM((tokens, LANES), F32), dma(1),
        ]
        + share_scratch(rows // OWNERS, before, True)
        + share_rows_scratch(counts[0] // 2, width)
        + feed_reduce_scratch(rows, span, counts[1], width),
        compiler_params=pltpu.CompilerParams(
            collective_id=2, has_side_effects=True, vmem_limit_bytes=VMEM_LIMIT
        ),
    )(hidden, d_own, other, own, vectors, weight, *ins, cot)


def last_kernel(
    length,
    d_query_ref, d_key_ref, d_value_ref, table_ref, vectors_ref, output_grad_ref, second_ref,
    wide_first, down_first, wide_before, down_before, result_ref, turned_in, x_in, weight_in, d_hidden_in,
    qkv_grad_out, output_grad_out, bits_out, gate_grad_out, up_grad_out, down_grad_out, input_grad_out, result_out,
    d_pre_ref, both_ref, part_ref, both_own, wide_own, down_own, bits_ref, bits_land, bits_sum,
    input_grad_ref, input_grad_land, turned_ref, x_ref, weight_ref, d_hidden_ref,
    bits_send, bits_recv, swap_sems, bit_sems, load_sems, *scratch,
):
    ring = Ring(CHIPS)
    core, mine = ring.core, ring.mine
    others = [{"fsdp": 2 * ring.chip_at(offset) + core} for offset in range(1, CHIPS)]
    loads = [
        pltpu.make_async_copy(src, dst, load_sems.at[k])
        for k, (src, dst) in enumerate([
            (turned_in, turned_ref), (weight_in, weight_ref), (x_in, x_ref), (d_hidden_in, d_hidden_ref),
        ])
    ]
    for load in loads:
        load.start()
    ring.greet(others + [ring.partner, ring.peer])
    share = Share(ring, wide_before, wide_own, scratch[:5])
    share_rows = ShareRows(ring, down_before, down_own, scratch[5:8])
    share_both = Share(ring, part_ref, both_own, scratch[8:13])
    early = BOTH // 2
    pieces = []
    for start in (0, early):
        part = pl.ds(start, early)
        for direction, reach in WAYS:
            pieces.append((
                direction,
                lambda chip, part=part: both_ref.at[core, chip, :, part],
                lambda chip, part=part: both_ref.at[1 - core, chip, :, part],
                ring.partner, part_ref.at[:, part], reach, direction > 0,
            ))
    reduce = make_reduce(ring, pieces, scratch[13:])
    share.first()
    share_rows.first()
    result_keep = pltpu.make_async_copy(result_ref.at[mine], result_out.at[mine], swap_sems.at[4])
    result_swap = remote(result_ref.at[1 - mine], result_out.at[mine], swap_sems.at[2], swap_sems.at[3], ring.peer)

    qwidth = HEADS * HEAD_DIM
    width = d_hidden_ref.shape[1]
    half = length // 2
    bias = None
    for index in range(length // BLOCK):
        rows = slice(index * BLOCK, (index + 1) * BLOCK)
        cosine, sine = tables(table_ref[index * BLOCK // half, index * BLOCK % half : index * BLOCK % half + BLOCK, :])

        def back(part):
            return (part * cosine - swap_halves(part) * sine).astype(BF16)

        for tile in range(PAIRS):
            columns = slice(tile * LANES, (tile + 1) * LANES)
            d_pre_ref[rows, columns] = back(d_query_ref[rows, columns].astype(F32))
        keys = join_heads(d_key_ref[0, rows, :], d_key_ref[1, rows, :]).astype(BF16).astype(F32)
        d_pre_ref[rows, qwidth : qwidth + LANES] = back(keys)
        values = join_heads(d_value_ref[0, rows, :], d_value_ref[1, rows, :])
        d_pre_ref[rows, qwidth + LANES :] = values.astype(BF16)
        part = jnp.sum(d_pre_ref[rows, :].astype(F32), axis=0, keepdims=True)
        bias = part if bias is None else bias + part

    chip_rows = width // CHIPS
    loads[0].wait()
    grad = mm(turned_ref[...], d_pre_ref[...]).astype(BF16)
    rest = grad.shape[1] - BOTH
    for chip in range(CHIPS):
        rows = slice(chip * chip_rows, (chip + 1) * chip_rows)
        both_ref[0, chip] = grad[rows, :BOTH]
        both_ref[1, chip, :, :rest] = grad[rows, BOTH:]
        both_ref[1, chip, :, rest:] = output_grad_ref[rows, :]
    reduce.begin()
    reduce.advance(0, range(len(pieces)))
    result_keep.start()
    result_swap.start()
    share.second()
    share_rows.second()

    gain = vectors_ref[1:2, :width]
    for load in loads[1:]:
        load.wait()
    weight_early, weight_late = weight_ref[0], weight_ref[1, :, : qwidth + 2 * LANES - BOTH]
    first = None
    for index in range(length // BLOCK):
        rows = slice(index * BLOCK, (index + 1) * BLOCK)
        which, start = index * BLOCK // half, index * BLOCK % half
        x = x_ref[which, start : start + BLOCK, :].astype(F32)
        upstream = mm(d_pre_ref[rows, :BOTH], weight_early, NT) + mm(d_pre_ref[rows, BOTH:], weight_late, NT)
        scale = lax.rsqrt(jnp.mean(x * x, axis=-1, keepdims=True) + EPS)
        weighted = upstream * gain
        inner = jnp.mean(weighted * x, axis=-1, keepdims=True)
        d_x = d_hidden_ref[rows, :] + scale * weighted - x * (scale * scale * scale * inner)
        part = jnp.sum(upstream * x * scale, axis=0, keepdims=True)
        first = part if first is None else first + part
        input_grad_ref[which, start : start + BLOCK, :] = d_x.astype(BF16)
        reduce.advance(index + 1, range(len(pieces)))
    swap = remote(input_grad_ref.at[1 - mine], input_grad_land, swap_sems.at[0], swap_sems.at[1], ring.peer)
    swap.start()

    bits_ref[...] = jnp.zeros_like(bits_ref)
    for chip in range(CHIPS):
        line = 0
        for values, each in ((bias, bias.shape[1] // CHIPS), (first, chip_rows), (second_ref[...], chip_rows)):
            for owner in range(OWNERS):
                count = each // OWNERS
                start = chip * each + owner * count
                bits_ref[chip, line : line + 1, :count] = values[:, start : start + count]
                line += 1
    copies = [
        remote(bits_ref.at[ring.chip_at(k + 1)], bits_land.at[k], bits_send.at[k], bits_recv.at[k], others[k])
        for k in range(CHIPS - 1)
    ]
    for copy in copies:
        copy.start()
    input_grad_out[mine] = input_grad_ref[mine].astype(F32)
    share.third()
    down_grad_out[: down_first.shape[0], :] = down_first[...]
    down_grad_out[down_first.shape[0] :, :] = down_own[...]
    own_rows = gate_grad_out.shape[0]
    sources = []
    for ref in (wide_first, wide_own):
        sources.append([stack_rows(ref[0, k], ref[1, k]) for k in range(2)])
    spread = spread_columns(sources)
    gate_grad_out[...] = spread[:own_rows]
    up_grad_out[...] = spread[own_rows:]
    share_both.first()
    total = bits_ref[ring.chip]
    for k, copy in enumerate(copies):
        copy.wait()
        total = total + bits_land[k]
    bits_sum[0] = total
    over_core = remote(bits_sum.at[0], bits_sum.at[1], bit_sems.at[0], bit_sems.at[1], ring.partner)
    over_core.start()
    over_core.wait()
    bits_sum[2] = bits_sum[0] + bits_sum[1]
    over_seq = remote(bits_sum.at[2], bits_sum.at[3], bit_sems.at[2], bit_sems.at[3], ring.peer)
    over_seq.start()
    swap.wait()
    input_grad_out[1 - mine] = input_grad_land[...].astype(F32)
    share_both.second()
    over_seq.wait()
    bits_out[...] = bits_sum[2] + bits_sum[3]
    share_both.third()
    rest = qkv_grad_out.shape[1] - BOTH
    qkv_grad_out[:, :BOTH] = both_own[0]
    qkv_grad_out[:, BOTH:] = both_own[1, :, :rest]
    output_grad_out[...] = both_own[1, :, rest:]
    reduce.finish()
    result_swap.wait()
    result_keep.wait()


def last_part(
    d_query, d_key, d_value, table, turned, x, vectors, weight, d_hidden, output_grad, second,
    wide_first, down_first, wide_before, down_before, result,
):
    tokens, width = d_hidden.shape
    ins = [
        d_query, d_key, d_value, table, vectors, output_grad, second, wide_first, down_first, wide_before, down_before,
    ]
    far = [turned, x, weight, d_hidden]
    rows, span = wide_before.shape
    own_rows = rows // OWNERS
    own = sum(SPLITS)
    halves = (2, tokens // 2, width)
    qkv = vectors.shape[1]
    outs = [
        (own_rows, qkv), (own_rows, width), (BITS, LANES), (own_rows, 2 * CHIPS * 2 * own),
        (own_rows, 2 * CHIPS * 2 * own), (own, width), halves,
    ]
    return pl.pallas_call(
        functools.partial(last_kernel, tokens),
        in_specs=[pl.BlockSpec(memory_space=pltpu.VMEM)] * len(ins) + [ANY] * 5,
        out_specs=[pl.BlockSpec(memory_space=pltpu.VMEM)] * len(outs) + [ANY],
        out_shape=[jax.ShapeDtypeStruct(shape, F32) for shape in outs]
        + [jax.ShapeDtypeStruct(result.shape, BF16)],
        scratch_shapes=[
            pltpu.VMEM((tokens, qkv), BF16), pltpu.VMEM((2, CHIPS, rows, BOTH), BF16),
            pltpu.VMEM((rows, BOTH), F32), pltpu.VMEM((2, own_rows, BOTH), F32),
            pltpu.VMEM((2, 2, own_rows, span), F32), pltpu.VMEM((SPLITS[1], width), F32),
            pltpu.VMEM((CHIPS, BITS, LANES), F32), pltpu.VMEM((CHIPS - 1, BITS, LANES), F32),
            pltpu.VMEM((4, BITS, LANES), F32), pltpu.VMEM(halves, BF16), pltpu.VMEM(halves[1:], BF16),
        ]
        + [pltpu.VMEM(part.shape, part.dtype) for part in far]
        + [dma(CHIPS - 1), dma(CHIPS - 1), dma(5), dma(4), dma(4)]
        + share_scratch(own_rows, span, True)
        + share_rows_scratch(SPLITS[1], width)
        + share_scratch(own_rows, BOTH, False)
        + reduce_scratch([(rows, BOTH // 2, True)] * 4),
        compiler_params=pltpu.CompilerParams(
            collective_id=3, has_side_effects=True, vmem_limit_bytes=VMEM_LIMIT
        ),
    )(*ins, result, *far)


def ring_shards(
    inputs, positions, qkv_weight, qkv_bias, output_weight, first_gain,
    gate_weight, up_weight, down_weight, second_gain, cotangent,
):
    _, half, width = inputs.shape
    tokens = 2 * half
    rows = gate_weight.shape[0]
    freqs = THETA ** (-jnp.arange(0, HEAD_DIM, 2).astype(F32) / HEAD_DIM)
    angles = positions.astype(F32)[..., None] * freqs
    cosine, sine = jnp.cos(angles), jnp.sin(angles)
    table = jnp.concatenate([cosine, cosine, -sine, sine], axis=-1)
    both = jnp.stack([
        qkv_weight[:, :BOTH], jnp.concatenate([qkv_weight[:, BOTH:], output_weight], axis=1),
    ])
    own_bias = qkv_bias.shape[0]
    pad = (0, own_bias - rows)
    small = jnp.stack([qkv_bias, jnp.pad(first_gain, pad), jnp.pad(second_gain, pad)], axis=1)
    small = jnp.pad(small, ((0, 0), (0, LANES - 3)))
    (
        x, table, weight, turned1, query, keys, values,
        vectors, mixed, logs, hidden, own_wide, own_down, cot, wide, down, normed2, turned2,
    ) = first_part(inputs, table, both, small, gate_weight, up_weight, down_weight, cotangent)
    weight = weight.reshape(2, width, BOTH)
    cot = cot.reshape(2, tokens, width)
    own, d_own, other, wide_second, down_second, wide_part_first, down_part_first = feed(
        normed2, turned2, cot, hidden, wide, down, own_wide, own_down
    )
    (
        d_hidden, output_grad, second, d_query, d_key, d_value,
        wide_first, down_first, wide_part_second, down_part_second, result,
    ) = back_all(
        hidden, d_own, other, own, vectors, weight, mixed, query, logs, keys, values,
        wide_part_first, down_part_first, wide_second, down_second, cot,
    )
    qkv_grad, output_grad, bits, gate_grad, up_grad, down_grad, input_grad, result = last_part(
        d_query, d_key, d_value, table, turned1, x, vectors, weight, d_hidden, output_grad, second,
        wide_first, down_first, wide_part_second, down_part_second, result,
    )
    owner = 2 * lax.rem(lax.axis_index("fsdp"), 2) + lax.axis_index("seq")

    def own_bits(which, count):
        return lax.dynamic_index_in_dim(bits, which * OWNERS + owner, 0, keepdims=False)[:count]

    return (
        result,
        input_grad,
        qkv_grad,
        own_bits(0, own_bias // 2),
        output_grad,
        own_bits(1, rows // 2),
        gate_grad,
        up_grad,
        down_grad,
        own_bits(2, rows // 2),
    )


def solution(mesh):
    tokens = P("fsdp", "seq", None)
    rows, row = P("fsdp", None), P("fsdp")
    grads, grad = P(("fsdp", "seq"), None), P(("fsdp", "seq"))
    ready = mesh.shape["fsdp"] == 2 * CHIPS and mesh.shape["seq"] == 2
    step = ring_shards if ready else plain_shards
    return jax.shard_map(
        step,
        mesh=mesh,
        in_specs=(tokens, P("fsdp", "seq"), rows, row, rows, row, rows, rows, rows, row, tokens),
        out_specs=(tokens, tokens, grads, grad, grads, grad, grads, grads, grads, grad),
        check_vma=False,
    )
```

```python
import functools

import jax
import jax.numpy as jnp
from jax import lax
from jax.experimental import pallas as pl
from jax.experimental.pallas import tpu as pltpu
from jax.sharding import PartitionSpec as P

HEADS = 14
KV_HEADS = 2
HEAD_DIM = 64
GROUP = HEADS // KV_HEADS
PAIRS = HEADS // 2
LANES = 128
BLOCK = 256
CHUNK = 256
EPS = 1e-06
THETA = 1000000.0
BF16 = jnp.bfloat16
F32 = jnp.float32
VMEM_LIMIT = 60 * 1024 * 1024

NN = (((1,), (0,)), ((), ()))
NT = (((1,), (1,)), ((), ()))
TN = (((0,), (0,)), ((), ()))


def mm(left, right, dims=NN):
    return lax.dot_general(left, right, dims, preferred_element_type=F32)


def params():
    return pltpu.CompilerParams(vmem_limit_bytes=VMEM_LIMIT)


def swap_halves(values):
    lane = lax.broadcasted_iota(jnp.int32, values.shape, 1)
    half = HEAD_DIM // 2
    ahead = pltpu.roll(values, LANES - half, 1)
    behind = pltpu.roll(values, half, 1)
    return jnp.where(lane % HEAD_DIM < half, ahead, behind)


def qkv_kernel(x_ref, gain_ref, weight_ref, bias_ref, cos_ref, sin_ref, normed_ref, query_ref, pair_ref):
    x = x_ref[...].astype(F32)
    scale = lax.rsqrt(jnp.mean(x * x, axis=-1, keepdims=True) + EPS)
    normed = (x * scale * gain_ref[...].astype(F32)).astype(BF16)
    normed_ref[...] = normed
    pre = mm(normed, weight_ref[...]) + bias_ref[...].astype(F32)
    cosine, sine = cos_ref[...], sin_ref[...]
    qwidth = HEADS * HEAD_DIM
    for tile in range(PAIRS):
        part = pre[:, tile * LANES : (tile + 1) * LANES]
        turned = part * cosine + swap_halves(part) * sine
        query_ref[:, tile * LANES : (tile + 1) * LANES] = turned.astype(BF16)
    part = pre[:, qwidth : qwidth + LANES]
    pair_ref[:, :LANES] = (part * cosine + swap_halves(part) * sine).astype(BF16)
    pair_ref[:, LANES:] = pre[:, qwidth + LANES :].astype(BF16)


def split_heads(block):
    wide = block.astype(F32)
    lane = lax.broadcasted_iota(jnp.int32, wide.shape, 1)
    first = jnp.where(lane < HEAD_DIM, wide, 0.0)
    second = jnp.where(lane < HEAD_DIM, pltpu.roll(wide, HEAD_DIM, 1), 0.0)
    return first, second


def join_heads(first, second):
    lane = lax.broadcasted_iota(jnp.int32, first.shape, 1)
    return jnp.where(lane < HEAD_DIM, first, pltpu.roll(second, HEAD_DIM, 1))


def attend_kernel(length, query_ref, key_ref, value_ref, mixed_ref, log_ref):
    pair = pl.program_id(1)
    scale = HEAD_DIM**-0.5
    heads = [part.astype(BF16) for part in split_heads(query_ref[0])]
    lane = lax.broadcasted_iota(jnp.int32, (BLOCK, LANES), 1)
    row = lax.broadcasted_iota(jnp.int32, (BLOCK, BLOCK), 0)
    col = lax.broadcasted_iota(jnp.int32, (BLOCK, BLOCK), 1)
    for index in range(length // BLOCK):
        rows = slice(index * BLOCK, (index + 1) * BLOCK)
        seen = index * BLOCK
        outs = []
        for which in range(2):
            head = 2 * pair + which
            kv = head // GROUP
            query = heads[which][rows]
            keys = key_ref[0, kv]
            diagonal = mm(query, keys[rows], NT) * scale
            diagonal = jnp.where(row >= col, diagonal, -1e30)
            top = jnp.max(diagonal, axis=-1, keepdims=True)
            if seen:
                before = mm(query, keys[:seen], NT) * scale
                top = jnp.maximum(top, jnp.max(before, axis=-1, keepdims=True))
            probs = jnp.exp(diagonal - top).astype(BF16)
            mixed = mm(probs, value_ref[0, kv, rows, :])
            if seen:
                probs = jnp.exp(before - top).astype(BF16)
                mixed = mixed + mm(probs, value_ref[0, kv, :seen, :])
            total = mixed[:, HEAD_DIM : HEAD_DIM + 1]
            outs.append(mixed / total)
            kept = jnp.where(lane == head, top + jnp.log(total), log_ref[0, rows, :])
            log_ref[0, rows, :] = kept
        mixed_ref[0, rows, :] = join_heads(outs[0], outs[1]).astype(BF16)


def widen(values, column):
    lane = lax.broadcasted_iota(jnp.int32, values.shape, 1)
    high = column.astype(BF16).astype(F32)
    middle = (column - high).astype(BF16).astype(F32)
    low = column - high - middle
    values = jnp.where(lane == HEAD_DIM, high, values)
    values = jnp.where(lane == HEAD_DIM + 1, middle, values)
    return jnp.where(lane == HEAD_DIM + 2, low, values).astype(BF16)


def back_kernel(length, query_ref, grad_ref, mixed_ref, log_ref, key_ref, value_ref, d_query_ref, d_key_ref, d_value_ref):
    pair = pl.program_id(1)
    scale = HEAD_DIM**-0.5

    @pl.when(pair == 0)
    def start():
        d_key_ref[...] = jnp.zeros_like(d_key_ref)
        d_value_ref[...] = jnp.zeros_like(d_value_ref)

    queries = split_heads(query_ref[0])
    grads = split_heads(grad_ref[0])
    mixes = split_heads(mixed_ref[0])
    lane = lax.broadcasted_iota(jnp.int32, (length, LANES), 1)
    row = lax.broadcasted_iota(jnp.int32, (BLOCK, BLOCK), 0)
    col = lax.broadcasted_iota(jnp.int32, (BLOCK, BLOCK), 1)
    outs = []
    for which in range(2):
        head = 2 * pair + which
        kv = head // GROUP
        log_total = jnp.sum(jnp.where(lane == head, log_ref[0], 0.0), axis=-1, keepdims=True)
        inner = jnp.sum(grads[which] * mixes[which], axis=-1, keepdims=True)
        query = widen(queries[which] * scale, -log_total)
        query_low = queries[which].astype(BF16)
        grad = widen(grads[which], -inner)
        grad_low = grads[which].astype(BF16)
        parts = [None] * (length // BLOCK)
        for index in range(length // BLOCK):
            own = slice(index * BLOCK, (index + 1) * BLOCK)
            keys, values = key_ref[0, kv, own, :], value_ref[0, kv, own, :]
            key_sum = value_sum = None
            for other in range(index, length // BLOCK):
                rows = slice(other * BLOCK, (other + 1) * BLOCK)
                scores = mm(keys, query[rows], NT)
                if other == index:
                    scores = jnp.where(row <= col, scores, -1e30)
                probs = jnp.exp(scores)
                d_scores = (probs * mm(values, grad[rows], NT)).astype(BF16)
                value_part = mm(probs.astype(BF16), grad_low[rows])
                key_part = mm(d_scores, query_low[rows])
                key_sum = key_part if key_sum is None else key_sum + key_part
                value_sum = value_part if value_sum is None else value_sum + value_part
                part = mm(d_scores, keys, TN)
                parts[other] = part if parts[other] is None else parts[other] + part
            d_key_ref[0, kv, own, :] += key_sum * scale
            d_value_ref[0, kv, own, :] += value_sum
        outs.append(parts)
    for index in range(length // BLOCK):
        rows = slice(index * BLOCK, (index + 1) * BLOCK)
        joined = join_heads(outs[0][index], outs[1][index]) * scale
        d_query_ref[0, rows, :] = joined.astype(BF16)


def plain_feed_kernel(
    normed_ref, turned_ref, cot_ref, gate_ref, up_ref, down_ref,
    result_ref, d_normed_ref, gate_grad_ref, up_grad_ref, down_grad_ref,
):
    @pl.when(pl.program_id(0) == 0)
    def start():
        result_ref[...] = jnp.zeros_like(result_ref)
        d_normed_ref[...] = jnp.zeros_like(d_normed_ref)

    normed, cot = normed_ref[...], cot_ref[...]
    gate_weight, up_weight, down_weight = gate_ref[...], up_ref[...], down_ref[...]
    gate = mm(normed, gate_weight)
    up = mm(normed, up_weight)
    d_act = mm(cot, down_weight, NT)
    sigma = jax.nn.sigmoid(gate)
    silu = gate * sigma
    act = (silu * up).astype(BF16)
    d_gate = (d_act * up * sigma * (1.0 + gate * (1.0 - sigma))).astype(BF16)
    d_up = (d_act * silu).astype(BF16)
    result_ref[...] += mm(act, down_weight)
    d_normed_ref[...] += mm(d_gate, gate_weight, NT) + mm(d_up, up_weight, NT)
    turned = turned_ref[...]
    gate_grad_ref[...] = mm(turned, d_gate).astype(gate_grad_ref.dtype)
    up_grad_ref[...] = mm(turned, d_up).astype(up_grad_ref.dtype)
    down_grad_ref[...] = mm(act, cot, TN).astype(down_grad_ref.dtype)


MESH = pl.DeviceIdType.MESH
ANY = pl.BlockSpec(memory_space=pl.ANY)


class Ring:
    def __init__(self, chips):
        self.n = chips
        self.core = lax.rem(lax.axis_index("fsdp"), 2)
        self.chip = lax.div(lax.axis_index("fsdp"), 2)
        self.mine = lax.axis_index("seq")
        side, line = lax.rem(self.chip, 2), lax.div(self.chip, 2)
        self.rank = line * (1 - side) + (chips - 1 - line) * side
        self.right = {"fsdp": 2 * self.chip_at(1) + self.core}
        self.left = {"fsdp": 2 * self.chip_at(-1) + self.core}
        self.partner = {"fsdp": 2 * self.chip + 1 - self.core}
        self.peer = {"seq": 1 - self.mine}

    def chip_at(self, offset):
        rank = lax.rem(self.rank + 2 * self.n + offset, self.n)
        side = lax.div(rank, self.n // 2)
        line = rank * (1 - side) + (self.n - 1 - rank) * side
        return 2 * line + side

    def greet(self, others):
        barrier = pltpu.get_barrier_semaphore()
        for other in others:
            pl.semaphore_signal(barrier, inc=1, device_id=other, device_id_type=MESH)
        pl.semaphore_wait(barrier, len(others))


def remote(src, dst, send, recv, device):
    return pltpu.make_async_remote_copy(
        src_ref=src, dst_ref=dst, send_sem=send, recv_sem=recv, device_id=device, device_id_type=MESH
    )


class Gather:
    def __init__(self, ring, pieces, sems):
        self.ring, self.pieces, self.sems = ring, pieces, sems

    def refs(self, piece, hop):
        direction, own, block = self.pieces[piece][:3]
        dst = block(self.ring.chip_at(-direction * hop))
        return (own if hop == 0 else dst), dst

    def along(self, piece, hop):
        src, dst = self.refs(piece, hop)
        target = self.ring.right if self.pieces[piece][0] > 0 else self.ring.left
        return remote(src, dst, self.sems[0].at[piece, hop], self.sems[1].at[piece, hop], target)

    def mirror(self, piece, hop):
        src, dst = self.refs(piece, hop)
        return remote(src, dst, self.sems[2].at[piece, hop], self.sems[3].at[piece, hop], self.pieces[piece][3])

    def mirrored(self, piece, hop):
        return self.pieces[piece][3] is not None and self.pieces[piece][4] <= hop <= self.pieces[piece][5]

    def advance(self, hop, pieces):
        for piece in pieces:
            reach = self.pieces[piece][5]
            if 0 < hop <= reach:
                self.along(piece, hop - 1).wait_recv()
            if hop < reach:
                self.along(piece, hop).start()
            if self.mirrored(piece, hop):
                self.mirror(piece, hop).start()

    def finish(self):
        for piece in range(len(self.pieces)):
            for hop in range(self.ring.n):
                if hop < self.pieces[piece][5]:
                    self.along(piece, hop).wait_send()
                if self.mirrored(piece, hop):
                    self.mirror(piece, hop).wait()


def gather_sems(pieces):
    return [pltpu.SemaphoreType.DMA((pieces, CHIPS)) for _ in range(4)]


class Reduce:
    def __init__(self, ring, pieces, buffers, sems):
        self.ring, self.pieces, self.buffers, self.sems = ring, pieces, buffers, sems

    def chip(self, piece, hop):
        return self.ring.chip_at(self.pieces[piece][0] * (self.pieces[piece][5] - hop))

    def give(self, piece, hop):
        src = self.pieces[piece][2](self.chip(piece, hop))
        dst = self.buffers[piece][2].at[hop]
        return remote(src, dst, self.sems[2].at[piece, hop], self.sems[3].at[piece, hop], self.pieces[piece][3])

    def along(self, piece, hop):
        send, recv = self.buffers[piece][:2]
        src = self.pieces[piece][1](self.chip(piece, 0)) if hop == 0 and self.alone(piece) else send.at[hop % 2]
        target = self.ring.right if self.pieces[piece][0] > 0 else self.ring.left
        return remote(src, recv.at[hop], self.sems[0].at[piece, hop], self.sems[1].at[piece, hop], target)

    def alone(self, piece):
        return self.pieces[piece][2] is None

    def begin(self):
        self.offer(0, range(len(self.pieces)))

    def given(self, piece, hop):
        reach, kept = self.pieces[piece][5:]
        return not self.alone(piece) and (hop < reach or hop == reach and kept)

    def offer(self, hop, pieces):
        for piece in pieces:
            if self.given(piece, hop):
                self.give(piece, hop).start()

    def advance(self, hop, pieces):
        for piece in pieces:
            reach, kept = self.pieces[piece][5:]
            send, recv, land = self.buffers[piece]
            if not kept and hop == reach + 1:
                self.along(piece, reach - 1).wait_recv()
                self.pieces[piece][4][...] += recv[reach - 1].astype(F32)
            if hop > reach or hop == reach and not kept:
                continue
            self.offer(hop + 1, [piece])
            if hop == 0 and self.alone(piece):
                self.along(piece, 0).start()
                continue
            if 2 <= hop < reach:
                self.along(piece, hop - 2).wait_send()
            addends = [self.pieces[piece][1](self.chip(piece, hop))[...].astype(F32)]
            if self.given(piece, hop):
                self.give(piece, hop).wait_recv()
                addends.append(land[hop].astype(F32))
            if hop > 0:
                self.along(piece, hop - 1).wait_recv()
                addends.append(recv[hop - 1].astype(F32))
            total = functools.reduce(lax.add, addends)
            if hop < reach:
                send[hop % 2] = total.astype(send.dtype)
                self.along(piece, hop).start()
            else:
                self.pieces[piece][4][...] = total

    def finish(self):
        for piece in range(len(self.pieces)):
            reach = self.pieces[piece][5]
            for hop in (reach - 2, reach - 1):
                self.along(piece, hop).wait_send()
            for hop in range(self.ring.n):
                if self.given(piece, hop):
                    self.give(piece, hop).wait_send()


def reduce_scratch(shapes):
    buffers = []
    for rows, columns, shared in shapes:
        buffers += [pltpu.VMEM((2, rows, columns), BF16), pltpu.VMEM((CHIPS - 1, rows, columns), BF16)]
        if shared:
            buffers.append(pltpu.VMEM((CHIPS, rows, columns), BF16))
    return buffers + [pltpu.SemaphoreType.DMA((len(shapes), CHIPS)) for _ in range(4)]


def make_reduce(ring, pieces, scratch):
    scratch = list(scratch)
    buffers = []
    for piece in pieces:
        send, recv = scratch.pop(0), scratch.pop(0)
        buffers.append((send, recv, None if piece[2] is None else scratch.pop(0)))
    return Reduce(ring, pieces, buffers, scratch)


class Share:
    def __init__(self, ring, part, out, scratch):
        self.ring, self.part, self.out = ring, part, out
        self.peer_send, self.peer_recv, self.core_send, self.core_recv, self.sems = scratch
        self.split = len(out.shape) == 4
        self.rows = out.shape[-2]

    def over_seq(self):
        return remote(self.peer_send, self.peer_recv, self.sems.at[0], self.sems.at[1], self.ring.peer)

    def over_core(self):
        return remote(self.core_send, self.core_recv, self.sems.at[2], self.sems.at[3], self.ring.partner)

    def owned(self, core, seq):
        start = (2 * core + seq) * self.rows
        return self.part[start : start + self.rows, :]

    def first(self):
        for mine in range(2):

            @pl.when(self.ring.mine == mine)
            def pick(mine=mine):
                for core in range(2):
                    self.peer_send[core] = self.owned(core, 1 - mine).astype(BF16)

        self.over_seq().start()

    def second(self):
        self.over_seq().wait()
        for mine in range(2):
            for core in range(2):

                @pl.when((self.ring.mine == mine) & (self.ring.core == core))
                def pick(mine=mine, core=core):
                    if self.split:
                        self.out[mine, core] = self.owned(core, mine)
                        self.out[1 - mine, core] = self.peer_recv[core].astype(F32)
                        self.core_send[mine] = self.owned(1 - core, mine).astype(BF16)
                        self.core_send[1 - mine] = self.peer_recv[1 - core]
                    else:
                        self.out[core] = self.owned(core, mine) + self.peer_recv[core].astype(F32)
                        give = self.owned(1 - core, mine) + self.peer_recv[1 - core].astype(F32)
                        self.core_send[0] = give.astype(BF16)

        self.over_core().start()

    def third(self):
        self.over_core().wait()
        if self.split:
            for seq in range(2):
                self.out[seq, 1 - self.ring.core] = self.core_recv[seq].astype(F32)
        else:
            self.out[1 - self.ring.core] = self.core_recv[0].astype(F32)


def share_scratch(rows, columns, split):
    both, last = (2, rows, columns), (2 if split else 1, rows, columns)
    return [
        pltpu.VMEM(both, BF16), pltpu.VMEM(both, BF16), pltpu.VMEM(last, BF16), pltpu.VMEM(last, BF16),
        pltpu.SemaphoreType.DMA((4,)),
    ]


class ShareRows:
    def __init__(self, ring, part, out, scratch):
        self.ring, self.part, self.out = ring, part, out
        self.send, self.recv, self.sems = scratch
        self.rows = out.shape[0]

    def over_seq(self):
        return remote(self.send, self.recv, self.sems.at[0], self.sems.at[1], self.ring.peer)

    def first(self):
        for mine in range(2):

            @pl.when(self.ring.mine == mine)
            def pick(mine=mine):
                start = (1 - mine) * self.rows
                self.send[...] = self.part[start : start + self.rows, :].astype(BF16)

        self.over_seq().start()

    def second(self):
        self.over_seq().wait()
        for mine in range(2):

            @pl.when(self.ring.mine == mine)
            def pick(mine=mine):
                start = mine * self.rows
                self.out[...] = self.part[start : start + self.rows, :] + self.recv[...].astype(F32)


def share_rows_scratch(rows, columns):
    one = (rows, columns)
    return [pltpu.VMEM(one, BF16), pltpu.VMEM(one, BF16), pltpu.SemaphoreType.DMA((2,))]


def spread(points, halves, now):
    plan = [[] for _ in range(points + 1)]
    steps = [(hop, half) for hop in range(CHIPS) for half in halves]
    plan[0] = steps[:now]
    rest = steps[now:]
    for index, step in enumerate(rest):
        plan[-(-(index + 1) * points // len(rest))].append(step)
    return plan


def at_point(step, first, plan, points, which, transfer):
    for place, moves in enumerate(plan[:-1]):
        if moves and place % points == which:

            @pl.when(step == first + place // points)
            def move(moves=moves):
                for hop, pieces in moves:
                    transfer.advance(hop, pieces)


def at_end(plan, transfer):
    for hop, pieces in plan[-1]:
        transfer.advance(hop, pieces)
    transfer.finish()


def rope_tables(positions):
    half = HEAD_DIM // 2
    freqs = THETA ** (-jnp.arange(0, HEAD_DIM, 2).astype(F32) / HEAD_DIM)
    angles = positions.astype(F32)[..., None] * freqs
    cosine, sine = jnp.cos(angles), jnp.sin(angles)
    return jnp.tile(cosine, (1, LANES // half)), jnp.tile(
        jnp.concatenate([-sine, sine], axis=-1), (1, LANES // HEAD_DIM)
    )


def rms_back(values, scale, gain, upstream):
    weighted = upstream * gain
    inner = jnp.mean(weighted * values, axis=-1, keepdims=True)
    grad_in = scale * weighted - values * (scale * scale * scale) * inner
    grad_gain = jnp.sum(upstream * values * scale, axis=0)
    return (grad_in, grad_gain)


def rotate_back(grads, cosine, sine):
    tokens, width = grads.shape
    tiles = grads.reshape(tokens, width // LANES, LANES)
    half = HEAD_DIM // 2
    lane = lax.iota(jnp.int32, LANES)
    ahead = jnp.concatenate([tiles[..., half:], tiles[..., :half]], axis=-1)
    behind = jnp.concatenate([tiles[..., -half:], tiles[..., :-half]], axis=-1)
    other = jnp.where(lane % HEAD_DIM < half, ahead, behind)
    return (tiles * cosine[:, None, :] - other * sine[:, None, :]).reshape(tokens, width)


def full(shape):
    return pl.BlockSpec(shape, lambda *_: (0,) * len(shape))


def plain_shards(
    inputs, positions, qkv_weight, qkv_bias, output_weight, first_gain,
    gate_weight, up_weight, down_weight, second_gain, cotangent,
):
    seqs, half_len, width = inputs.shape
    nseq = lax.axis_size("seq")
    length = half_len * nseq
    whole = seqs // nseq
    tokens = whole * length
    qwidth = HEADS * HEAD_DIM
    kvwidth = KV_HEADS * HEAD_DIM

    def gather(part):
        return lax.all_gather(part, "fsdp", axis=0, tiled=True)

    def to_sequences(part):
        return lax.all_to_all(part, "seq", split_axis=0, concat_axis=1, tiled=True)

    def to_tokens(part):
        return lax.all_to_all(part, "seq", split_axis=1, concat_axis=0, tiled=True)

    def scatter(grad):
        part = lax.psum_scatter(grad.astype(BF16), "fsdp", scatter_dimension=0, tiled=True)
        return lax.psum_scatter(part.astype(F32), "seq", scatter_dimension=0, tiled=True)

    x_low = to_sequences(inputs).reshape(tokens, width)
    places = to_sequences(positions).reshape(tokens)
    cot = to_sequences(cotangent).reshape(tokens, width)
    full_qkv, full_bias, full_output = gather(qkv_weight), gather(qkv_bias), gather(output_weight)
    gain1, gain2 = gather(first_gain), gather(second_gain)
    full_gate, full_up, full_down = gather(gate_weight), gather(up_weight), gather(down_weight)

    cosine, sine = rope_tables(places)
    normed1, query, pair = pl.pallas_call(
        qkv_kernel,
        grid=(tokens // BLOCK,),
        in_specs=[
            pl.BlockSpec((BLOCK, width), lambda i: (i, 0)),
            full((1, width)),
            full((width, qwidth + 2 * kvwidth)),
            full((1, qwidth + 2 * kvwidth)),
            pl.BlockSpec((BLOCK, LANES), lambda i: (i, 0)),
            pl.BlockSpec((BLOCK, LANES), lambda i: (i, 0)),
        ],
        out_specs=[
            pl.BlockSpec((BLOCK, width), lambda i: (i, 0)),
            pl.BlockSpec((BLOCK, qwidth), lambda i: (i, 0)),
            pl.BlockSpec((BLOCK, 2 * kvwidth), lambda i: (i, 0)),
        ],
        out_shape=[
            jax.ShapeDtypeStruct((tokens, width), BF16),
            jax.ShapeDtypeStruct((tokens, qwidth), BF16),
            jax.ShapeDtypeStruct((tokens, 2 * kvwidth), BF16),
        ],
        compiler_params=params(),
    )(x_low, gain1[None], full_qkv, full_bias[None], cosine, sine)

    query = query.reshape(whole, length, qwidth)
    pair = pair.reshape(whole, length, 2, KV_HEADS, HEAD_DIM).transpose(2, 0, 3, 1, 4)
    ones = jnp.ones((2, whole, KV_HEADS, length, 3), BF16)
    pair = jnp.pad(jnp.concatenate([pair, ones], axis=-1), ((0, 0),) * 4 + ((0, HEAD_DIM - 3),))
    keys, values = pair[0], pair[1]
    lanes_spec = pl.BlockSpec((1, length, LANES), lambda b, p: (b, 0, p))
    kv_spec = pl.BlockSpec((1, KV_HEADS, length, LANES), lambda b, p: (b, 0, 0, 0))
    log_spec = pl.BlockSpec((1, length, LANES), lambda b, p: (b, 0, 0))
    mixed, logs = pl.pallas_call(
        functools.partial(attend_kernel, length),
        grid=(whole, PAIRS),
        in_specs=[lanes_spec, kv_spec, kv_spec],
        out_specs=[lanes_spec, log_spec],
        out_shape=[
            jax.ShapeDtypeStruct((whole, length, qwidth), BF16),
            jax.ShapeDtypeStruct((whole, length, LANES), F32),
        ],
        compiler_params=params(),
    )(query, keys, values)

    mixed_tokens = mixed.reshape(tokens, qwidth)
    x = x_low.astype(F32)
    hidden = x + mm(mixed_tokens, full_output)
    gain2 = gain2.astype(F32)
    scale2 = lax.rsqrt(jnp.mean(hidden * hidden, axis=-1, keepdims=True) + EPS)
    normed2 = (hidden * scale2 * gain2).astype(BF16)

    ff = gate_weight.shape[1]
    column = pl.BlockSpec((width, CHUNK), lambda j: (0, j))
    line = pl.BlockSpec((CHUNK, width), lambda j: (j, 0))
    total, d_normed2, gate_grad, up_grad, down_grad = pl.pallas_call(
        plain_feed_kernel,
        grid=(ff // CHUNK,),
        in_specs=[full((tokens, width)), full((width, tokens)), full((tokens, width)), column, column, line],
        out_specs=[full((tokens, width)), full((tokens, width)), column, column, line],
        out_shape=[
            jax.ShapeDtypeStruct((tokens, width), F32),
            jax.ShapeDtypeStruct((tokens, width), F32),
            jax.ShapeDtypeStruct((width, ff), BF16),
            jax.ShapeDtypeStruct((width, ff), BF16),
            jax.ShapeDtypeStruct((ff, width), BF16),
        ],
        compiler_params=params(),
    )(normed2, normed2.T, cot, full_gate, full_up, full_down)

    result = to_tokens((hidden + total).astype(BF16).reshape(whole, length, width))
    back2, second_grad = rms_back(hidden, scale2, gain2, d_normed2)
    d_hidden = cot.astype(F32) + back2
    d_branch = d_hidden.astype(BF16)
    output_grad = mm(mixed_tokens, d_branch, TN)
    d_mixed = mm(d_branch, full_output, NT).astype(BF16).reshape(whole, length, qwidth)

    d_query, d_keys, d_values = pl.pallas_call(
        functools.partial(back_kernel, length),
        grid=(whole, PAIRS),
        in_specs=[lanes_spec, lanes_spec, lanes_spec, log_spec, kv_spec, kv_spec],
        out_specs=[lanes_spec, kv_spec, kv_spec],
        out_shape=[
            jax.ShapeDtypeStruct((whole, length, qwidth), BF16),
            jax.ShapeDtypeStruct((whole, KV_HEADS, length, LANES), F32),
            jax.ShapeDtypeStruct((whole, KV_HEADS, length, LANES), F32),
        ],
        compiler_params=params(),
    )(query, d_mixed, mixed, logs, keys, values)

    def merge(part):
        part = part[..., :HEAD_DIM].astype(BF16)
        return part.transpose(0, 2, 1, 3).reshape(tokens, kvwidth)

    turned = jnp.concatenate([d_query.reshape(tokens, qwidth), merge(d_keys)], axis=-1).astype(F32)
    turned = rotate_back(turned, cosine, sine).astype(BF16)
    d_pre = jnp.concatenate([turned, merge(d_values)], axis=-1)
    qkv_grad = mm(normed1, d_pre, TN)
    bias_grad = jnp.sum(d_pre.astype(F32), axis=0)
    d_normed1 = mm(d_pre, full_qkv, NT)
    scale1 = lax.rsqrt(jnp.mean(x * x, axis=-1, keepdims=True) + EPS)
    back1, first_grad = rms_back(x, scale1, gain1.astype(F32), d_normed1)
    input_grad = (d_hidden + back1).astype(BF16).reshape(whole, length, width)
    input_grad = to_tokens(input_grad).astype(F32)

    def scatter_small(grad):
        return lax.psum_scatter(grad, ("fsdp", "seq"), scatter_dimension=0, tiled=True)

    return (
        result,
        input_grad,
        scatter(qkv_grad),
        scatter_small(bias_grad),
        scatter(output_grad),
        scatter_small(first_grad),
        scatter(gate_grad),
        scatter(up_grad),
        scatter(down_grad),
        scatter_small(second_grad),
    )


CHIPS = 8
OWNERS = 4
SPLITS = (64, 88)
STARTS = (0, 64)
BITS = 16
QUARTER = 512
BOTH = 1024


def inside(shape):
    return pl.BlockSpec(shape, lambda *_: (0,) * len(shape), pipeline_mode=pl.Buffered(1))


def dma(*shape):
    return pltpu.SemaphoreType.DMA(shape)


def spans():
    return [2 * CHIPS * split for split in SPLITS]


def stack_rows(first, second):
    return jnp.concatenate([first.astype(F32), second.astype(F32)], axis=0)


def owner_columns(core, group):
    own = sum(SPLITS)
    starts = [OWNERS * own * chip + 2 * own * core + own * seq for chip in range(CHIPS) for seq in range(2)]
    return [(start + STARTS[group], SPLITS[group]) for start in starts]


def gather_columns(source, core, group):
    return jnp.concatenate([source[:, a : a + count] for a, count in owner_columns(core, group)], axis=1)


def spread_columns(sources):
    parts = []
    for chip in range(CHIPS):
        for core in range(2):
            for section in range(2 * chip, 2 * chip + 2):
                for group, split in enumerate(SPLITS):
                    parts.append(sources[group][core][:, section * split : (section + 1) * split])
    return jnp.concatenate(parts, axis=1)


def project(length, x_ref, table_ref, vectors_ref, weight_ref, turned_ref, query_ref, key_ref, value_ref):
    width = x_ref.shape[2]
    qwidth = HEADS * HEAD_DIM
    lane = lax.broadcasted_iota(jnp.int32, (BLOCK, LANES), 1)
    extra = (lane >= HEAD_DIM) & (lane < HEAD_DIM + 3)
    bias, gain = vectors_ref[0:1, :], vectors_ref[1:2, :width]
    early = weight_ref[0].reshape(width, BOTH)
    late = weight_ref[1, :, :, : qwidth + 2 * LANES - BOTH].reshape(width, qwidth + 2 * LANES - BOTH)
    for index in range(length // BLOCK):
        rows = slice(index * BLOCK, (index + 1) * BLOCK)
        half, start = index * BLOCK // (length // 2), index * BLOCK % (length // 2)
        x = x_ref[half, start : start + BLOCK, :].astype(F32)
        scale = lax.rsqrt(jnp.mean(x * x, axis=-1, keepdims=True) + EPS)
        normed = (x * scale * gain).astype(BF16)
        turned_ref[:, rows] = normed.T
        pre = mm(normed, early) + bias[:, :BOTH]
        values = mm(normed, late) + bias[:, BOTH:]
        cosine, sine = tables(table_ref[half, start : start + BLOCK, :])
        for tile in range(PAIRS):
            columns = slice(tile * LANES, (tile + 1) * LANES)
            part = pre[:, columns]
            query_ref[rows, columns] = (part * cosine + swap_halves(part) * sine).astype(BF16)
        part = pre[:, qwidth : qwidth + LANES]
        part = part * cosine + swap_halves(part) * sine
        for ref, both in ((key_ref, part), (value_ref, values)):
            for kv, head in enumerate(split_heads(both)):
                ref[kv, rows, :] = jnp.where(extra, 1.0, head).astype(BF16)


def tables(packed):
    lane = lax.broadcasted_iota(jnp.int32, packed.shape, 1)
    turned = pltpu.roll(packed, HEAD_DIM, 1)
    low = lane < HEAD_DIM
    return jnp.where(low, packed, turned), jnp.where(low, turned, packed)


def attend_pair(pair, length, query_ref, key_ref, value_ref, mixed_ref, log_ref):
    scale = HEAD_DIM**-0.5
    columns = pl.ds(pl.multiple_of(pair * LANES, LANES), LANES)
    heads = [part.astype(BF16) for part in split_heads(query_ref[:, columns])]
    lane = lax.broadcasted_iota(jnp.int32, (BLOCK, LANES), 1)
    row = lax.broadcasted_iota(jnp.int32, (BLOCK, BLOCK), 0)
    col = lax.broadcasted_iota(jnp.int32, (BLOCK, BLOCK), 1)
    for index in range(length // BLOCK):
        rows = slice(index * BLOCK, (index + 1) * BLOCK)
        seen = index * BLOCK
        outs = []
        for which in range(2):
            head = 2 * pair + which
            kv = head // GROUP
            query = heads[which][rows]
            diagonal = mm(query, key_ref[kv, rows, :], NT) * scale
            diagonal = jnp.where(row >= col, diagonal, -1e30)
            top = jnp.max(diagonal, axis=-1, keepdims=True)
            if seen:
                before = mm(query, key_ref[kv, :seen, :], NT) * scale
                top = jnp.maximum(top, jnp.max(before, axis=-1, keepdims=True))
            probs = jnp.exp(diagonal - top).astype(BF16)
            mixed = mm(probs, value_ref[kv, rows, :])
            if seen:
                probs = jnp.exp(before - top).astype(BF16)
                mixed = mixed + mm(probs, value_ref[kv, :seen, :])
            total = mixed[:, HEAD_DIM : HEAD_DIM + 1]
            outs.append(mixed / total)
            log_ref[rows, :] = jnp.where(lane == head, top + jnp.log(total), log_ref[rows, :])
        mixed_ref[rows, columns] = join_heads(outs[0], outs[1]).astype(BF16)


def settle(length, x_ref, mixed_ref, weight_ref, vectors_ref, hidden_ref, normed_ref, turned_ref):
    width = x_ref.shape[2]
    gain = vectors_ref[2:3, :width]
    weight = weight_ref[1, :, :, BOTH - width :].reshape(width, width)
    for index in range(length // BLOCK):
        rows = slice(index * BLOCK, (index + 1) * BLOCK)
        half, start = index * BLOCK // (length // 2), index * BLOCK % (length // 2)
        hidden = x_ref[half, start : start + BLOCK, :].astype(F32) + mm(mixed_ref[rows, :], weight)
        hidden_ref[rows, :] = hidden
        scale = lax.rsqrt(jnp.mean(hidden * hidden, axis=-1, keepdims=True) + EPS)
        normed = (hidden * scale * gain).astype(BF16)
        normed_ref[rows, :] = normed
        turned_ref[:, rows] = normed.T


HALVES = ((0, 1), (2, 3))
WAYS = ((1, CHIPS // 2), (-1, CHIPS - 1 - CHIPS // 2))


def row_cuts(rows):
    early = rows // 2 // 16 * 16 if rows == 112 else 80
    return (0, early), (early, rows - early)


def feed_gather(ring, own_wide, own_down, wide, down, sems):
    rows, count = own_wide.shape[1], own_down.shape[0]
    pieces = []
    for (start, some), (down_start, down_some) in zip(row_cuts(rows), row_cuts(count)):

        def down_block(chip, start=down_start, some=down_some):
            return down.at[pl.ds(pl.multiple_of(chip * count + start, 16), some), :]

        def wide_block(chip, start=start, some=some):
            return wide.at[ring.mine, chip, pl.ds(start, some), :]

        pieces.append((1, own_down.at[pl.ds(down_start, down_some), :], down_block, None, 0, CHIPS - 1))
        pieces.append((-1, own_wide.at[ring.mine, pl.ds(start, some), :], wide_block, ring.peer, 1, CHIPS - 1))
    return Gather(ring, pieces, sems)


def feed_keep(ring, own_wide, own_down, wide, down, sems):
    count = own_down.shape[0]
    rows = pl.ds(pl.multiple_of(ring.chip * count, 16), count)
    return [
        pltpu.make_async_copy(own_wide, wide.at[:, ring.chip], sems.at[0]),
        pltpu.make_async_copy(own_down, down.at[rows, :], sems.at[1]),
    ]


def feed_reduce(ring, wide, down, wide_part, down_part, scratch):
    rows, count = wide_part.shape[0], down_part.shape[0]
    pieces = []
    for (start, some), (down_start, down_some) in zip(row_cuts(rows), row_cuts(count)):

        def down_block(chip, start=down_start, some=down_some):
            return down.at[pl.ds(pl.multiple_of(chip * count + start, 16), some), :]

        def own_block(chip, start=start, some=some):
            return wide.at[ring.mine, chip, pl.ds(start, some), :]

        def other_block(chip, start=start, some=some):
            return wide.at[1 - ring.mine, chip, pl.ds(start, some), :]

        down_out = down_part.at[pl.ds(down_start, down_some), :]
        pieces.append((1, down_block, None, None, down_out, CHIPS - 1, True))
        pieces.append((
            -1, own_block, other_block, ring.peer, wide_part.at[pl.ds(start, some), :], CHIPS - 1, True
        ))
    return make_reduce(ring, pieces, scratch)


def feed_reduce_scratch(rows, span, count, width):
    shapes = []
    for (_, some), (_, down_some) in zip(row_cuts(rows), row_cuts(count)):
        shapes += [(down_some, width, False), (some, span, True)]
    return reduce_scratch(shapes)


def first_kernel(
    length, plan,
    x_in, table_in, both_in, small_in, gate_in, up_in, down_in, cot_in,
    x_out, table_out, weight_out, turned1_out, query_out, key_out, value_out,
    vectors_ref, mixed_ref, log_ref, hidden_ref, own_wide2, own_down2,
    cot_out, wide_out, down_out, normed_out, turned_out,
    x_ref, table_ref, weight_ref, turned1_ref, query_ref, key_ref, value_ref,
    normed_ref, turned_ref, both_land, small_land, both_own, small_own, small_all, perm_ref, wide_land, own_wide1, own_down1,
    swap_sems, core_sems, keep_sems, cot_sems, store_sems, *sems,
):
    step = pl.program_id(0)
    ring = Ring(CHIPS)
    core, mine = ring.core, ring.mine
    gather = feed_gather(ring, own_wide1, own_down1, wide_out, down_out, sems[:4])
    keeps = feed_keep(ring, own_wide1, own_down1, wide_out, down_out, keep_sems)
    early = BOTH // 2
    pieces = []
    for start in (0, early):
        part = pl.ds(start, early)
        for direction, reach in WAYS:
            pieces.append((
                direction, both_own.at[:, part], lambda chip, part=part: weight_ref.at[core, chip, :, part],
                ring.partner, 0 if direction > 0 else 1, reach,
            ))
    for direction, reach in WAYS:
        pieces.append((direction, small_own, lambda chip: small_all.at[chip], None, 0, reach))
    attention = Gather(ring, pieces, sems[4:])
    every = range(len(pieces))
    swaps = [
        remote(src.at[1 - mine], dst.at[mine], swap_sems.at[2 * k], swap_sems.at[2 * k + 1], ring.peer)
        for k, (src, dst) in enumerate([(x_in, x_ref), (table_in, table_ref), (cot_in, cot_out.at[core])])
    ]
    trades = [
        remote(src, dst, core_sems.at[2 * k], core_sems.at[2 * k + 1], ring.partner)
        for k, (src, dst) in enumerate([
            (both_in.at[1 - core], both_land), (small_in, small_land), (perm_ref.at[1 - core], wide_land),
            (cot_out.at[core], cot_out.at[core]), (normed_ref, normed_out.at[core]),
            (turned_ref, turned_out.at[core]),
        ])
    ]
    cot_keep = pltpu.make_async_copy(cot_in.at[mine], cot_out.at[core, mine], cot_sems.at[0])
    stores = [
        pltpu.make_async_copy(src, dst, store_sems.at[k])
        for k, (src, dst) in enumerate([
            (x_ref, x_out), (table_ref, table_out), (weight_ref, weight_out), (turned1_ref, turned1_out),
            (query_ref, query_out), (key_ref, key_out), (value_ref, value_out),
            (normed_ref, normed_out.at[core]), (turned_ref, turned_out.at[core]),
        ])
    ]

    @pl.when(step == 0)
    def enter():
        ring.greet([ring.right, ring.left, ring.partner, ring.peer])
        trades[0].start()
        trades[1].start()
        for swap in swaps:
            swap.start()
        cot_keep.start()
        x_ref[mine] = x_in[mine]
        table_ref[mine] = table_in[mine]
        trades[0].wait()
        trades[1].wait()
        half = small_in.shape[0]
        rows = both_in.shape[1]
        for which in range(2):

            @pl.when(core == which)
            def own(which=which):
                pair = (both_in[which], both_land[...])
                both_own[...] = stack_rows(*pair[:: 1 - 2 * which]).astype(BF16)
                pair = (small_in[...], small_land[...])[:: 1 - 2 * which]
                lane = lax.broadcasted_iota(jnp.int32, (2 * half, LANES), 1)
                gains = stack_rows(pair[0][:rows], pair[1][:rows])
                gains = jnp.concatenate([gains, jnp.zeros((2 * (half - rows), LANES), F32)], axis=0)
                small_own[...] = jnp.where(lane == 0, stack_rows(*pair), gains).astype(BF16)

        attention.advance(0, every)
        weight_ref[core, ring.chip] = both_own[...]
        small_all[ring.chip] = small_own[...]
        wide = stack_rows(gate_in[...], up_in[...])
        for side in range(2):
            for group, span in enumerate(spans()):
                first = group * spans()[0]
                part = gather_columns(wide, side, group).astype(BF16)
                perm_ref[side, 0, :, first : first + span] = part[:rows]
                perm_ref[side, 1, :, first : first + span] = part[rows:]
        trades[2].start()
        own = sum(SPLITS)
        for group, ref in enumerate((own_down1, own_down2)):
            start, count = STARTS[group], SPLITS[group]
            ref[...] = stack_rows(
                down_in[start : start + count, :], down_in[own + start : own + start + count, :]
            ).astype(BF16)
        attention.advance(1, every)
        trades[2].wait()
        for which in range(2):

            @pl.when(core == which)
            def chip_rows(which=which):
                for tensor in range(2):
                    pair = (perm_ref[which, tensor], wide_land[tensor])
                    block = stack_rows(*pair[:: 1 - 2 * which]).astype(BF16)
                    own_wide1[tensor] = block[:, : spans()[0]]
                    own_wide2[tensor] = block[:, spans()[0] :]

        gather.advance(0, (0, 1, 2, 3))
        for keep in keeps:
            keep.start()
        for hop in range(2, WAYS[0][1] + 1):
            attention.advance(hop, every)
            if hop == 3:
                gather.advance(1, HALVES[0])
        gather.advance(1, HALVES[1])
        attention.finish()
        rows = small_all.shape[1]
        turned = small_all[...].astype(F32).reshape(CHIPS * rows, LANES).T
        vectors_ref[0:1, :] = turned[0:1, :]
        width = x_in.shape[2]
        chip_rows = width // CHIPS
        turned = small_all[:, :chip_rows, :].astype(F32).reshape(width, LANES).T
        vectors_ref[1:3, :width] = turned[1:3, :]
        swaps[0].wait()
        swaps[1].wait()
        project(length, x_ref, table_ref, vectors_ref, weight_ref, turned1_ref, query_ref, key_ref, value_ref)
        for store in stores[:-2]:
            store.start()
        log_ref[...] = jnp.zeros_like(log_ref)

    at_point(step, 1, plan, 1, 0, gather)

    @pl.when((step >= 1) & (step <= PAIRS))
    def pairs():
        attend_pair(step - 1, length, query_ref, key_ref, value_ref, mixed_ref, log_ref)

    @pl.when(step == 4)
    def cotangent():
        swaps[2].wait()
        cot_keep.wait()
        trades[3].start()

    @pl.when(step == PAIRS + 1)
    def last():
        settle(length, x_ref, mixed_ref, weight_ref, vectors_ref, hidden_ref, normed_ref, turned_ref)
        for copy in trades[4:] + stores[-2:]:
            copy.start()
        at_end(plan, gather)
        for copy in keeps + trades[3:] + stores:
            copy.wait()


def first_part(x, table, both, small, gate, up, down, cot):
    _, half, width = x.shape
    tokens = 2 * half
    rows, ff = gate.shape
    one, two = spans()
    down_rows = [2 * split for split in SPLITS]
    stored = [
        (x.shape, BF16), (table.shape, F32), ((2, CHIPS, 2 * rows, BOTH), BF16), ((width, tokens), BF16),
        ((tokens, width), BF16), ((KV_HEADS, tokens, LANES), BF16), ((KV_HEADS, tokens, LANES), BF16),
    ]
    kept = [
        ((8, 2 * CHIPS * small.shape[0]), F32), ((tokens, width), BF16), ((tokens, LANES), F32),
        ((tokens, width), F32),
        ((2, 2 * rows, two), BF16), ((down_rows[1], width), BF16),
    ]
    far = [
        ((2,) + cot.shape, BF16), ((2, CHIPS, 2 * rows, one), BF16), ((CHIPS * down_rows[0], width), BF16),
        ((2, tokens, width), BF16), ((2, width, tokens), BF16),
    ]
    ins = [x, table, both, small, gate, up, down]
    steps = [(hop, half) for hop in range(2, CHIPS) for half in HALVES]
    points = PAIRS + 1
    plan = [[] for _ in range(points + 1)]
    for index, move in enumerate(steps):
        plan[-(-(index + 1) * points // len(steps))].append(move)
    return pl.pallas_call(
        functools.partial(first_kernel, tokens, plan),
        grid=(PAIRS + 2,),
        in_specs=[inside(part.shape) for part in ins] + [ANY],
        out_specs=[ANY] * len(stored) + [inside(shape) for shape, _ in kept] + [ANY] * len(far),
        out_shape=[jax.ShapeDtypeStruct(shape, kind) for shape, kind in stored + kept + far],
        scratch_shapes=[pltpu.VMEM(shape, kind) for shape, kind in stored]
        + [
            pltpu.VMEM((tokens, width), BF16), pltpu.VMEM((width, tokens), BF16),
            pltpu.VMEM(both.shape[1:], BF16), pltpu.VMEM(small.shape, BF16),
            pltpu.VMEM((2 * rows, BOTH), BF16), pltpu.VMEM((2 * small.shape[0], LANES), BF16),
            pltpu.VMEM((CHIPS, 2 * small.shape[0], LANES), BF16),
            pltpu.VMEM((2, 2, rows, one + two), BF16), pltpu.VMEM((2, rows, one + two), BF16),
            pltpu.VMEM((2, 2 * rows, one), BF16), pltpu.VMEM((down_rows[0], width), BF16),
            dma(6), dma(12), dma(2), dma(1), dma(len(stored) + 2),
        ]
        + gather_sems(4)
        + gather_sems(6),
        compiler_params=pltpu.CompilerParams(
            collective_id=0, has_side_effects=True, vmem_limit_bytes=VMEM_LIMIT
        ),
    )(*ins, cot)


def feed_chunk(count, offset, normed_ref, turned_ref, cot_ref, wide, down, result_ref, d_normed_ref, work, pause):
    width = normed_ref.shape[2]
    columns = pl.ds(offset, count)
    gate_weight = wide[0, :, :, columns].reshape(width, count)
    up_weight = wide[1, :, :, columns].reshape(width, count)
    down_weight = down[columns, :]
    act_at, gate_at, up_at = (slice(k * CHUNK, k * CHUNK + count) for k in range(3))
    parts = normed_ref.shape[1] // QUARTER
    for part in range(2 * parts):
        core, rows = part // parts, slice(part % parts * QUARTER, (part % parts + 1) * QUARTER)
        normed, cot = normed_ref[core, rows, :], cot_ref[core, rows, :]
        gate = mm(normed, gate_weight)
        up = mm(normed, up_weight)
        d_act = mm(cot, down_weight, NT)
        sigma = jax.nn.sigmoid(gate)
        silu = gate * sigma
        act = (silu * up).astype(BF16)
        d_gate = (d_act * up * sigma * (1.0 + gate * (1.0 - sigma))).astype(BF16)
        d_up = (d_act * silu).astype(BF16)
        work[core, rows, act_at], work[core, rows, gate_at], work[core, rows, up_at] = act, d_gate, d_up
        result_ref[core, rows, :] += mm(act, down_weight)
        d_normed_ref[core, rows, :] += mm(d_gate, gate_weight, NT) + mm(d_up, up_weight, NT)
        if part + 1 == parts:
            pause(1)
    pause(2)
    for tensor, at in ((0, gate_at), (1, up_at)):
        grad = mm(turned_ref[0], work[0, :, at]) + mm(turned_ref[1], work[1, :, at])
        wide[tensor, :, :, columns] = grad.astype(BF16).reshape(wide.shape[1], wide.shape[2], count)
    grad = mm(work[0, :, act_at], cot_ref[0], TN) + mm(work[1, :, act_at], cot_ref[1], TN)
    down[columns, :] = grad.astype(BF16)


def feed_kernel(
    gather_plan, reduce_plan,
    normed_ref, turned_ref, cot_ref, hidden_in, wide_in, down_in, own_wide, own_down,
    result_out, d_normed_out, other_out, wide_out, down_out, wide_part, down_part,
    result_ref, d_normed_ref, work, wide1, down1, wide2, down2,
    load_sems, keep_sems, trade_sems, store_sems, *scratch,
):
    step = pl.program_id(0)
    ring = Ring(CHIPS)
    core = ring.core
    gather = feed_gather(ring, own_wide, own_down, wide2, down2, scratch[:4])
    keeps = feed_keep(ring, own_wide, own_down, wide2, down2, keep_sems)
    reduce = feed_reduce(ring, wide1, down1, wide_part, down_part, scratch[4:])
    loads = [
        pltpu.make_async_copy(src, dst, load_sems.at[k])
        for k, (src, dst) in enumerate([(wide_in, wide1), (down_in, down1), (hidden_in, result_ref.at[core])])
    ]
    trades = [
        remote(work.at[k], other_out.at[k], trade_sems.at[2 * k], trade_sems.at[2 * k + 1], ring.partner)
        for k in range(2)
    ]
    stores = [
        pltpu.make_async_copy(src, dst, store_sems.at[k])
        for k, (src, dst) in enumerate([
            (wide2, wide_out), (down2, down_out), (result_ref.at[core], result_out),
            (d_normed_ref.at[core], d_normed_out),
        ])
    ]
    one, two = wide1.shape[3], wide2.shape[3]
    turns, last = one // CHUNK, one // CHUNK + -(-two // CHUNK) - 1

    @pl.when(step == 0)
    def begin():
        for load in loads:
            load.start()
        ring.greet([ring.right, ring.left, ring.partner, ring.peer])

    at_point(step, 0, gather_plan, 3, 0, gather)

    @pl.when(step == 0)
    def start():
        for keep in keeps:
            keep.start()
        result_ref[1 - core] = jnp.zeros(result_ref.shape[1:], F32)
        d_normed_ref[...] = jnp.zeros_like(d_normed_ref)
        for load in loads:
            load.wait()

    def chunk(count, offset, wide, down, first, plan, transfer):
        feed_chunk(
            count, offset, normed_ref, turned_ref, cot_ref, wide, down, result_ref, d_normed_ref, work,
            lambda which: at_point(step, first, plan, 3, which, transfer),
        )

    @pl.when(step < turns)
    def first_group():
        chunk(CHUNK, pl.multiple_of(step * CHUNK, CHUNK), wide1, down1, 0, gather_plan, gather)

    @pl.when(step == turns - 1)
    def between():
        at_end(gather_plan, gather)
        for keep in keeps:
            keep.wait()
        reduce.begin()

    at_point(step, turns, reduce_plan, 3, 0, reduce)

    @pl.when((step >= turns) & (step < last))
    def second_group():
        chunk(CHUNK, pl.multiple_of((step - turns) * CHUNK, CHUNK), wide2, down2, turns, reduce_plan, reduce)

    @pl.when(step == last)
    def end():
        done = (last - turns) * CHUNK
        chunk(two - done, done, wide2, down2, turns, reduce_plan, reduce)
        for store in stores:
            store.start()
        work[0] = result_ref[1 - core].astype(BF16)
        trades[0].start()
        work[1] = d_normed_ref[1 - core].astype(BF16)
        trades[1].start()
        at_end(reduce_plan, reduce)
        for copy in trades + stores:
            copy.wait()


def feed(normed, turned, cot, hidden, wide, down, own_wide, own_down):
    _, tokens, width = normed.shape
    one, two = wide.shape[3], own_wide.shape[2]
    rows = own_wide.shape[1]
    counts = [2 * split for split in SPLITS]
    turns, more = one // CHUNK, -(-two // CHUNK)
    wide_two, down_two = (2, CHIPS, rows, two), (CHIPS * counts[1], width)
    whole, halves = (tokens, width), (2, tokens, width)
    far = [(whole, F32), (whole, F32), (halves, BF16), (wide_two, BF16), (down_two, BF16)]
    near = [((rows, one), F32), ((counts[0], width), F32)]
    return pl.pallas_call(
        functools.partial(
            feed_kernel, spread(3 * turns, HALVES, len(HALVES)), spread(3 * more, HALVES, 0)
        ),
        grid=(turns + more,),
        in_specs=[inside(part.shape) for part in (normed, turned, cot)] + [ANY] * 5,
        out_specs=[ANY] * len(far) + [inside(shape) for shape, _ in near],
        out_shape=[jax.ShapeDtypeStruct(shape, kind) for shape, kind in far + near],
        scratch_shapes=[
            pltpu.VMEM(halves, F32), pltpu.VMEM(halves, F32), pltpu.VMEM(halves, BF16),
            pltpu.VMEM(wide.shape, BF16), pltpu.VMEM(down.shape, BF16),
            pltpu.VMEM(wide_two, BF16), pltpu.VMEM(down_two, BF16),
            dma(3), dma(2), dma(4), dma(4),
        ]
        + gather_sems(4)
        + feed_reduce_scratch(rows, one, counts[0], width),
        compiler_params=pltpu.CompilerParams(
            collective_id=1, has_side_effects=True, vmem_limit_bytes=VMEM_LIMIT
        ),
    )(normed, turned, cot, hidden, wide, down, own_wide, own_down)


def unsettle(
    rows, first, hidden_ref, d_own_ref, other_ref, own_ref, cot_ref, vectors_ref, mixed_ref, weight_ref,
    d_hidden_ref, d_mixed_ref, output_grad_ref, second_ref, result_ref, place,
):
    width = hidden_ref.shape[1]
    gain = vectors_ref[2:3, :width]
    weight = weight_ref[0, :, BOTH - width :]
    hidden = hidden_ref[...]
    upstream = d_own_ref[...] + other_ref[1].astype(F32)
    scale = lax.rsqrt(jnp.mean(hidden * hidden, axis=-1, keepdims=True) + EPS)
    weighted = upstream * gain
    inner = jnp.mean(weighted * hidden, axis=-1, keepdims=True)
    d_hidden = cot_ref[rows, :].astype(F32) + scale * weighted - hidden * (scale * scale * scale * inner)
    d_hidden_ref[rows, :] = d_hidden
    result_ref[place] = (own_ref[...] + other_ref[0].astype(F32)).astype(BF16)
    branch = d_hidden.astype(BF16)
    d_mixed_ref[rows, :] = mm(branch, weight, NT).astype(BF16)
    grad = mm(mixed_ref[rows, :], branch, TN)
    part = jnp.sum(upstream * hidden * scale, axis=0, keepdims=True)

    @pl.when(first)
    def begin():
        second_ref[...] = part
        output_grad_ref[...] = grad

    @pl.when(jnp.logical_not(first))
    def more():
        second_ref[...] += part
        output_grad_ref[...] += grad


def back_head(pair, which, length, query_ref, grad_ref, mixed_ref, log_ref, key_ref, value_ref, d_key_ref, d_value_ref):
    scale = HEAD_DIM**-0.5
    columns = pl.ds(pl.multiple_of(pair * LANES, LANES), LANES)
    query, grad, mixed = (split_heads(ref[:, columns])[which] for ref in (query_ref, grad_ref, mixed_ref))
    lane = lax.broadcasted_iota(jnp.int32, (length, LANES), 1)
    row = lax.broadcasted_iota(jnp.int32, (BLOCK, BLOCK), 0)
    col = lax.broadcasted_iota(jnp.int32, (BLOCK, BLOCK), 1)
    head = 2 * pair + which
    kv = head // GROUP
    log_total = jnp.sum(jnp.where(lane == head, log_ref[...], 0.0), axis=-1, keepdims=True)
    inner = jnp.sum(grad * mixed, axis=-1, keepdims=True)
    query_low, grad_low = query.astype(BF16), grad.astype(BF16)
    query, grad = widen(query * scale, -log_total), widen(grad, -inner)
    parts = [None] * (length // BLOCK)
    for index in range(length // BLOCK):
        own = slice(index * BLOCK, (index + 1) * BLOCK)
        keys, values = key_ref[kv, own, :], value_ref[kv, own, :]
        key_sum = value_sum = None
        for other in range(index, length // BLOCK):
            rows = slice(other * BLOCK, (other + 1) * BLOCK)
            scores = mm(keys, query[rows], NT)
            if other == index:
                scores = jnp.where(row <= col, scores, -1e30)
            probs = jnp.exp(scores)
            d_scores = (probs * mm(values, grad[rows], NT)).astype(BF16)
            value_part = mm(probs.astype(BF16), grad_low[rows])
            key_part = mm(d_scores, query_low[rows])
            key_sum = key_part if key_sum is None else key_sum + key_part
            value_sum = value_part if value_sum is None else value_sum + value_part
            part = mm(d_scores, keys, TN)
            parts[other] = part if parts[other] is None else parts[other] + part
        d_key_ref[kv, own, :] += key_sum * scale
        d_value_ref[kv, own, :] += value_sum
    return parts


def back_kernel_all(
    length, plan,
    hidden_ref, d_own_ref, other_ref, own_ref,
    vectors_ref, weight_ref, mixed_ref, query_ref, log_ref, key_ref, value_ref, wide_before, down_before,
    wide_ref, down_ref, cot_in,
    d_hidden_ref, output_grad_out, second_ref, d_query_ref, d_key_ref, d_value_ref,
    wide_own, down_own, wide_part, down_part, result_ref,
    d_mixed_ref, cot_ref, output_grad_ref, half_ref, load_sem, *scratch,
):
    step = pl.program_id(0)
    ring = Ring(CHIPS)
    share = Share(ring, wide_before, wide_own, scratch[:5])
    share_rows = ShareRows(ring, down_before, down_own, scratch[5:8])
    reduce = feed_reduce(ring, wide_ref, down_ref, wide_part, down_part, scratch[8:])
    load = pltpu.make_async_copy(cot_in.at[ring.core], cot_ref, load_sem.at[0])
    blocks = length // BLOCK

    @pl.when(step == 0)
    def begin():
        load.start()
        ring.greet([ring.right, ring.left, ring.partner, ring.peer])
        reduce.begin()
        share.first()
        share_rows.first()
        d_key_ref[...] = jnp.zeros_like(d_key_ref)
        d_value_ref[...] = jnp.zeros_like(d_value_ref)
        load.wait()

    at_point(step, 0, plan, 2, 0, reduce)

    @pl.when(step < blocks)
    def norms():
        rows = pl.ds(pl.multiple_of(step * BLOCK, BLOCK), BLOCK)
        halves = length // 2 // BLOCK
        place = (lax.div(step, halves), pl.ds(pl.multiple_of(lax.rem(step, halves) * BLOCK, BLOCK), BLOCK))
        unsettle(
            rows, step == 0, hidden_ref, d_own_ref, other_ref, own_ref, cot_ref, vectors_ref, mixed_ref, weight_ref,
            d_hidden_ref, d_mixed_ref, output_grad_ref, second_ref, result_ref, place,
        )

    @pl.when(step == blocks - 1)
    def after():
        output_grad_out[...] = output_grad_ref[...].astype(BF16)
        share.second()
        share_rows.second()

    refs = (query_ref, d_mixed_ref, mixed_ref, log_ref, key_ref, value_ref, d_key_ref, d_value_ref)

    @pl.when(step >= blocks)
    def first_head():
        parts = back_head(step - blocks, 0, length, *refs)
        for index, part in enumerate(parts):
            half_ref[index * BLOCK : (index + 1) * BLOCK, :] = part

    at_point(step, 0, plan, 2, 1, reduce)

    @pl.when(step >= blocks)
    def second_head():
        scale = HEAD_DIM**-0.5
        columns = pl.ds(pl.multiple_of((step - blocks) * LANES, LANES), LANES)
        parts = back_head(step - blocks, 1, length, *refs)
        for index, part in enumerate(parts):
            rows = slice(index * BLOCK, (index + 1) * BLOCK)
            d_query_ref[rows, columns] = (join_heads(half_ref[rows, :], part) * scale).astype(BF16)

    @pl.when(step == blocks + PAIRS - 1)
    def last():
        at_end(plan, reduce)
        share.third()


def back_all(
    hidden, d_own, other, own, vectors, weight, mixed, query, logs, keys, values, wide_before, down_before,
    wide, down, cot,
):
    tokens, width = hidden.shape
    rows, before = wide_before.shape
    span = wide.shape[3]
    counts = [2 * split for split in SPLITS]
    blocks = tokens // BLOCK

    def block(step):
        return jnp.minimum(step, blocks - 1)

    line = pl.BlockSpec((BLOCK, width), lambda s: (block(s), 0))
    pair = pl.BlockSpec((2, BLOCK, width), lambda s: (0, block(s), 0))
    late = pl.BlockSpec((1, width, BOTH), lambda s: (1, 0, 0), pipeline_mode=pl.Buffered(1))
    ins = [mixed, query, logs, keys, values, wide_before, down_before, wide, down]
    outs = [
        ((tokens, width), F32), ((width, width), BF16), ((1, width), F32), (query.shape, BF16),
        (keys.shape, F32), (values.shape, F32),
        ((2, 2, rows // OWNERS, before), F32), ((counts[0] // 2, width), F32),
        ((rows, span), F32), ((counts[1], width), F32), ((2, tokens // 2, width), BF16),
    ]
    moves = [(hop, half) for hop in range(CHIPS) for half in HALVES]
    plan = [[] for _ in range(2 * (blocks + PAIRS) + 1)]
    for place, move in zip([2, 4, 6] + list(range(2 * blocks, len(plan) - 2)), moves):
        plan[place].append(move)
    return pl.pallas_call(
        functools.partial(back_kernel_all, tokens, plan),
        grid=(blocks + PAIRS,),
        in_specs=[line, line, pair, line, inside(vectors.shape), late]
        + [inside(part.shape) for part in ins]
        + [ANY],
        out_specs=[inside(shape) for shape, _ in outs],
        out_shape=[jax.ShapeDtypeStruct(shape, kind) for shape, kind in outs],
        scratch_shapes=[
            pltpu.VMEM((tokens, width), BF16), pltpu.VMEM((tokens, width), BF16),
            pltpu.VMEM((width, width), F32), pltpu.VMEM((tokens, LANES), F32), dma(1),
        ]
        + share_scratch(rows // OWNERS, before, True)
        + share_rows_scratch(counts[0] // 2, width)
        + feed_reduce_scratch(rows, span, counts[1], width),
        compiler_params=pltpu.CompilerParams(
            collective_id=2, has_side_effects=True, vmem_limit_bytes=VMEM_LIMIT
        ),
    )(hidden, d_own, other, own, vectors, weight, *ins, cot)


def last_kernel(
    length,
    d_query_ref, d_key_ref, d_value_ref, table_ref, vectors_ref, output_grad_ref, second_ref,
    wide_first, down_first, wide_before, down_before, result_ref, turned_in, x_in, weight_in, d_hidden_in,
    qkv_grad_out, output_grad_out, bits_out, gate_grad_out, up_grad_out, down_grad_out, input_grad_out, result_out,
    d_pre_ref, both_ref, part_ref, both_own, wide_own, down_own, bits_ref, bits_land, bits_sum,
    input_grad_ref, input_grad_land, turned_ref, x_ref, weight_ref, d_hidden_ref,
    bits_send, bits_recv, swap_sems, bit_sems, load_sems, *scratch,
):
    ring = Ring(CHIPS)
    core, mine = ring.core, ring.mine
    others = [{"fsdp": 2 * ring.chip_at(offset) + core} for offset in range(1, CHIPS)]
    loads = [
        pltpu.make_async_copy(src, dst, load_sems.at[k])
        for k, (src, dst) in enumerate([
            (turned_in, turned_ref), (weight_in, weight_ref), (x_in, x_ref), (d_hidden_in, d_hidden_ref),
        ])
    ]
    for load in loads:
        load.start()
    ring.greet(others + [ring.partner, ring.peer])
    share = Share(ring, wide_before, wide_own, scratch[:5])
    share_rows = ShareRows(ring, down_before, down_own, scratch[5:8])
    share_both = Share(ring, part_ref, both_own, scratch[8:13])
    early = BOTH // 2
    pieces = []
    for start in (0, early):
        part = pl.ds(start, early)
        for direction, reach in WAYS:
            pieces.append((
                direction,
                lambda chip, part=part: both_ref.at[core, chip, :, part],
                lambda chip, part=part: both_ref.at[1 - core, chip, :, part],
                ring.partner, part_ref.at[:, part], reach, direction > 0,
            ))
    reduce = make_reduce(ring, pieces, scratch[13:])
    share.first()
    share_rows.first()
    result_keep = pltpu.make_async_copy(result_ref.at[mine], result_out.at[mine], swap_sems.at[4])
    result_swap = remote(result_ref.at[1 - mine], result_out.at[mine], swap_sems.at[2], swap_sems.at[3], ring.peer)
    result_keep.start()
    result_swap.start()

    qwidth = HEADS * HEAD_DIM
    width = d_hidden_ref.shape[1]
    half = length // 2
    bias = None
    for index in range(length // BLOCK):
        rows = slice(index * BLOCK, (index + 1) * BLOCK)
        cosine, sine = tables(table_ref[index * BLOCK // half, index * BLOCK % half : index * BLOCK % half + BLOCK, :])

        def back(part):
            return (part * cosine - swap_halves(part) * sine).astype(BF16)

        for tile in range(PAIRS):
            columns = slice(tile * LANES, (tile + 1) * LANES)
            d_pre_ref[rows, columns] = back(d_query_ref[rows, columns].astype(F32))
        keys = join_heads(d_key_ref[0, rows, :], d_key_ref[1, rows, :]).astype(BF16).astype(F32)
        d_pre_ref[rows, qwidth : qwidth + LANES] = back(keys)
        values = join_heads(d_value_ref[0, rows, :], d_value_ref[1, rows, :])
        d_pre_ref[rows, qwidth + LANES :] = values.astype(BF16)
        part = jnp.sum(d_pre_ref[rows, :].astype(F32), axis=0, keepdims=True)
        bias = part if bias is None else bias + part

    chip_rows = width // CHIPS
    loads[0].wait()
    grad = mm(turned_ref[...], d_pre_ref[...]).astype(BF16)
    rest = grad.shape[1] - BOTH
    for chip in range(CHIPS):
        rows = slice(chip * chip_rows, (chip + 1) * chip_rows)
        both_ref[0, chip] = grad[rows, :BOTH]
        both_ref[1, chip, :, :rest] = grad[rows, BOTH:]
        both_ref[1, chip, :, rest:] = output_grad_ref[rows, :]
    reduce.begin()
    reduce.advance(0, range(len(pieces)))
    share.second()
    share_rows.second()

    gain = vectors_ref[1:2, :width]
    for load in loads[1:]:
        load.wait()
    weight_early, weight_late = weight_ref[0], weight_ref[1, :, : qwidth + 2 * LANES - BOTH]
    first = None
    for index in range(length // BLOCK):
        rows = slice(index * BLOCK, (index + 1) * BLOCK)
        which, start = index * BLOCK // half, index * BLOCK % half
        x = x_ref[which, start : start + BLOCK, :].astype(F32)
        upstream = mm(d_pre_ref[rows, :BOTH], weight_early, NT) + mm(d_pre_ref[rows, BOTH:], weight_late, NT)
        scale = lax.rsqrt(jnp.mean(x * x, axis=-1, keepdims=True) + EPS)
        weighted = upstream * gain
        inner = jnp.mean(weighted * x, axis=-1, keepdims=True)
        d_x = d_hidden_ref[rows, :] + scale * weighted - x * (scale * scale * scale * inner)
        part = jnp.sum(upstream * x * scale, axis=0, keepdims=True)
        first = part if first is None else first + part
        input_grad_ref[which, start : start + BLOCK, :] = d_x.astype(BF16)
        reduce.advance(index + 1, range(len(pieces)))
    swap = remote(input_grad_ref.at[1 - mine], input_grad_land, swap_sems.at[0], swap_sems.at[1], ring.peer)
    swap.start()

    bits_ref[...] = jnp.zeros_like(bits_ref)
    for chip in range(CHIPS):
        line = 0
        for values, each in ((bias, bias.shape[1] // CHIPS), (first, chip_rows), (second_ref[...], chip_rows)):
            for owner in range(OWNERS):
                count = each // OWNERS
                start = chip * each + owner * count
                bits_ref[chip, line : line + 1, :count] = values[:, start : start + count]
                line += 1
    copies = [
        remote(bits_ref.at[ring.chip_at(k + 1)], bits_land.at[k], bits_send.at[k], bits_recv.at[k], others[k])
        for k in range(CHIPS - 1)
    ]
    for copy in copies:
        copy.start()
    input_grad_out[mine] = input_grad_ref[mine].astype(F32)
    share.third()
    down_grad_out[: down_first.shape[0], :] = down_first[...]
    down_grad_out[down_first.shape[0] :, :] = down_own[...]
    own_rows = gate_grad_out.shape[0]
    sources = []
    for ref in (wide_first, wide_own):
        sources.append([stack_rows(ref[0, k], ref[1, k]) for k in range(2)])
    spread = spread_columns(sources)
    gate_grad_out[...] = spread[:own_rows]
    up_grad_out[...] = spread[own_rows:]
    share_both.first()
    total = bits_ref[ring.chip]
    for k, copy in enumerate(copies):
        copy.wait()
        total = total + bits_land[k]
    bits_sum[0] = total
    over_core = remote(bits_sum.at[0], bits_sum.at[1], bit_sems.at[0], bit_sems.at[1], ring.partner)
    over_core.start()
    over_core.wait()
    bits_sum[2] = bits_sum[0] + bits_sum[1]
    over_seq = remote(bits_sum.at[2], bits_sum.at[3], bit_sems.at[2], bit_sems.at[3], ring.peer)
    over_seq.start()
    swap.wait()
    input_grad_out[1 - mine] = input_grad_land[...].astype(F32)
    share_both.second()
    over_seq.wait()
    bits_out[...] = bits_sum[2] + bits_sum[3]
    share_both.third()
    rest = qkv_grad_out.shape[1] - BOTH
    qkv_grad_out[:, :BOTH] = both_own[0]
    qkv_grad_out[:, BOTH:] = both_own[1, :, :rest]
    output_grad_out[...] = both_own[1, :, rest:]
    reduce.finish()
    result_swap.wait()
    result_keep.wait()


def last_part(
    d_query, d_key, d_value, table, turned, x, vectors, weight, d_hidden, output_grad, second,
    wide_first, down_first, wide_before, down_before, result,
):
    tokens, width = d_hidden.shape
    ins = [
        d_query, d_key, d_value, table, vectors, output_grad, second, wide_first, down_first, wide_before, down_before,
    ]
    far = [turned, x, weight, d_hidden]
    rows, span = wide_before.shape
    own_rows = rows // OWNERS
    own = sum(SPLITS)
    halves = (2, tokens // 2, width)
    qkv = vectors.shape[1]
    outs = [
        (own_rows, qkv), (own_rows, width), (BITS, LANES), (own_rows, 2 * CHIPS * 2 * own),
        (own_rows, 2 * CHIPS * 2 * own), (own, width), halves,
    ]
    return pl.pallas_call(
        functools.partial(last_kernel, tokens),
        in_specs=[pl.BlockSpec(memory_space=pltpu.VMEM)] * len(ins) + [ANY] * 5,
        out_specs=[pl.BlockSpec(memory_space=pltpu.VMEM)] * len(outs) + [ANY],
        out_shape=[jax.ShapeDtypeStruct(shape, F32) for shape in outs]
        + [jax.ShapeDtypeStruct(result.shape, BF16)],
        scratch_shapes=[
            pltpu.VMEM((tokens, qkv), BF16), pltpu.VMEM((2, CHIPS, rows, BOTH), BF16),
            pltpu.VMEM((rows, BOTH), F32), pltpu.VMEM((2, own_rows, BOTH), F32),
            pltpu.VMEM((2, 2, own_rows, span), F32), pltpu.VMEM((SPLITS[1], width), F32),
            pltpu.VMEM((CHIPS, BITS, LANES), F32), pltpu.VMEM((CHIPS - 1, BITS, LANES), F32),
            pltpu.VMEM((4, BITS, LANES), F32), pltpu.VMEM(halves, BF16), pltpu.VMEM(halves[1:], BF16),
        ]
        + [pltpu.VMEM(part.shape, part.dtype) for part in far]
        + [dma(CHIPS - 1), dma(CHIPS - 1), dma(5), dma(4), dma(4)]
        + share_scratch(own_rows, span, True)
        + share_rows_scratch(SPLITS[1], width)
        + share_scratch(own_rows, BOTH, False)
        + reduce_scratch([(rows, BOTH // 2, True)] * 4),
        compiler_params=pltpu.CompilerParams(
            collective_id=3, has_side_effects=True, vmem_limit_bytes=VMEM_LIMIT
        ),
    )(*ins, result, *far)


def ring_shards(
    inputs, positions, qkv_weight, qkv_bias, output_weight, first_gain,
    gate_weight, up_weight, down_weight, second_gain, cotangent,
):
    _, half, width = inputs.shape
    tokens = 2 * half
    rows = gate_weight.shape[0]
    freqs = THETA ** (-jnp.arange(0, HEAD_DIM, 2).astype(F32) / HEAD_DIM)
    angles = positions.astype(F32)[..., None] * freqs
    cosine, sine = jnp.cos(angles), jnp.sin(angles)
    table = jnp.concatenate([cosine, cosine, -sine, sine], axis=-1)
    both = jnp.stack([
        qkv_weight[:, :BOTH], jnp.concatenate([qkv_weight[:, BOTH:], output_weight], axis=1),
    ])
    own_bias = qkv_bias.shape[0]
    pad = (0, own_bias - rows)
    small = jnp.stack([qkv_bias, jnp.pad(first_gain, pad), jnp.pad(second_gain, pad)], axis=1)
    small = jnp.pad(small, ((0, 0), (0, LANES - 3)))
    (
        x, table, weight, turned1, query, keys, values,
        vectors, mixed, logs, hidden, own_wide, own_down, cot, wide, down, normed2, turned2,
    ) = first_part(inputs, table, both, small, gate_weight, up_weight, down_weight, cotangent)
    weight = weight.reshape(2, width, BOTH)
    cot = cot.reshape(2, tokens, width)
    own, d_own, other, wide_second, down_second, wide_part_first, down_part_first = feed(
        normed2, turned2, cot, hidden, wide, down, own_wide, own_down
    )
    (
        d_hidden, output_grad, second, d_query, d_key, d_value,
        wide_first, down_first, wide_part_second, down_part_second, result,
    ) = back_all(
        hidden, d_own, other, own, vectors, weight, mixed, query, logs, keys, values,
        wide_part_first, down_part_first, wide_second, down_second, cot,
    )
    qkv_grad, output_grad, bits, gate_grad, up_grad, down_grad, input_grad, result = last_part(
        d_query, d_key, d_value, table, turned1, x, vectors, weight, d_hidden, output_grad, second,
        wide_first, down_first, wide_part_second, down_part_second, result,
    )
    owner = 2 * lax.rem(lax.axis_index("fsdp"), 2) + lax.axis_index("seq")

    def own_bits(which, count):
        return lax.dynamic_index_in_dim(bits, which * OWNERS + owner, 0, keepdims=False)[:count]

    return (
        result,
        input_grad,
        qkv_grad,
        own_bits(0, own_bias // 2),
        output_grad,
        own_bits(1, rows // 2),
        gate_grad,
        up_grad,
        down_grad,
        own_bits(2, rows // 2),
    )


def solution(mesh):
    tokens = P("fsdp", "seq", None)
    rows, row = P("fsdp", None), P("fsdp")
    grads, grad = P(("fsdp", "seq"), None), P(("fsdp", "seq"))
    ready = mesh.shape["fsdp"] == 2 * CHIPS and mesh.shape["seq"] == 2
    step = ring_shards if ready else plain_shards
    return jax.shard_map(
        step,
        mesh=mesh,
        in_specs=(tokens, P("fsdp", "seq"), rows, row, rows, row, rows, rows, rows, row, tokens),
        out_specs=(tokens, tokens, grads, grad, grads, grad, grads, grads, grads, grad),
        check_vma=False,
    )
```
